256 devices in a mesh: ctx: 32 (over x, z), tp: 8 (over y, core).
Axes of the slice: x: 4, y: 4, z: 8, core: 2. Of those that a mesh axis runs over, the one named last changes fastest.
Arguments:
- features: bfloat16 [16384, 3, 4096], P('ctx', None, 'tp'), may hold values from -6 to 6
- short_filter: float32 [7, 3, 4096], P(None, None, 'tp'), may hold values from -2 to 2
- medium_filter: float32 [128, 256], replicated, may hold values from -4 to 4
- skip_bias: float32 [4096], P('tp'), may hold values from -4 to 4
- cotangent: bfloat16 [16384, 4096], P('ctx', 'tp'), may hold values from -6 to 6
- doc_lengths: int32 [64], replicated, may hold values from 1 to 1024, 16384 in all
Outputs:
- grad_features: bfloat16 [16384, 3, 4096], P('ctx', None, 'tp')
- grad_short_filter: float32 [7, 3, 4096], P(None, None, 'tp')
- grad_medium_filter: float32 [128, 256], replicated
- grad_skip: float32 [4096], P('tp')
The draws below stay inside these ranges and needn't reach their ends.
Inputs may be any that keep to these rules, and one draw needn't show every extreme that they name: `doc_lengths`: the lengths sum to 16384; the longest is exactly 1024.
All inputs are finite; a program needn't handle non-finite values.
Results may differ from the reference program's by a relative error of at most 0.0073.
Values may be sent and summed in bfloat16 or wider, within the bound.
No kernel may reach another device: no remote copies, remote signals or barrier semaphores. Data moves between devices by JAX's collectives and lax.ppermute only.
A program may use at most 192 MiB of HBM per device.

```python
import math
import jax
import jax.numpy as jnp
import numpy as np
from jax import lax

D = 4096
GROUP = 16
GROUPS = 256
SE_LEN = 7
MR_LEN = 128
STRETCH = 256
SEQ = 16384
DOCS = 64
MOST = 1024
N_CTX = 32


def draw_medium_filter(key, part):
    key = jax.random.fold_in(key, 11)
    noise_key, span_key = jax.random.split(key)
    lowest, highest = (10.0, 1000.0)
    span = jnp.exp(jax.random.uniform(span_key, (1, GROUPS), jnp.float32, jnp.log(lowest), jnp.log(highest)))
    lags = jnp.arange(MR_LEN, dtype=jnp.float32)[:, None]
    ratio = jnp.exp(-1.0 / span)
    weight_norm = jnp.sqrt((1.0 - ratio * ratio) / (1.0 - ratio ** (2 * MR_LEN)))
    noise = jax.random.truncated_normal(noise_key, -3.0, 3.0, (MR_LEN, GROUPS), jnp.float32)
    return noise * jnp.exp(-lags / span) * weight_norm


def levels(own_key, dims, cuts, low, largest):
    level = 1.0
    for dim, blocks in cuts:
        steps = jax.random.uniform(jax.random.fold_in(jax.random.fold_in(own_key, 6), dim), (blocks,), jnp.float32, low / len(cuts), largest / len(cuts))
        level = level * jnp.repeat(jnp.exp(steps), dims[dim] // blocks).reshape((-1,) + (1,) * (len(dims) - 1 - dim))
    return level


def length_profile(amount, total, reach, slope):
    weights = [(1 << 20) // math.isqrt(standing ** slope) + 1 for standing in range(2, amount + 1)]
    rest, holding = total - reach - (amount - 1), [1] * (amount - 1)
    while rest > 0:
        free = [i for i in range(amount - 1) if holding[i] < reach]
        mass, left = sum([weights[i] for i in free]), rest
        for i in free:
            addition = min(reach - holding[i], max(1, left * weights[i] // mass), rest)
            holding[i] = holding[i] + addition
            rest = rest - addition
    return np.array([reach] + holding)


def uneven_parts(stream_key, number_of, total, bound, lean):
    if number_of == 2:
        one = jax.random.randint(stream_key, (), max(1, total - bound), min(bound, total - 1) + 1)
        return jnp.stack([one, total - one])
    tallies = jnp.asarray(length_profile(number_of, total, bound, lean), jnp.int32)
    pairs = (number_of - 1) // 2
    source_of, sink = tallies[1:1 + 2 * pairs:2], tallies[2:2 + 2 * pairs:2]
    room = jnp.minimum(source_of - 1, bound - sink)
    shifted = jax.random.randint(jax.random.fold_in(stream_key, 1), (pairs,), 0, 1 << 20) % (room + 1)
    tallies = tallies.at[1:1 + 2 * pairs:2].set(source_of - shifted).at[2:2 + 2 * pairs:2].set(sink + shifted)
    return tallies[jax.random.permutation(jax.random.fold_in(stream_key, 2), number_of)]


def gaussian(rng, extent, scale, bound, shards=(), held_as=jnp.bfloat16):
    gain = levels(rng, extent, shards, -0.22, 0.18) if shards else 1.0
    result = jax.random.normal(rng, extent, jnp.float32) * scale * gain
    return jnp.minimum(jnp.maximum(result, -bound), bound).astype(held_as)


def setup_inputs(seed: int = 0) -> dict:
    arg_keys = jax.random.split(jax.random.key(seed), 7)
    return {
        "features": gaussian(arg_keys[0], (SEQ, 3, D), 1.0, 6.0, ((0, 32), (2, 8))),
        "short_filter": gaussian(arg_keys[1], (SE_LEN, 3, D), SE_LEN ** -0.5, 2.0, ((2, 8),), jnp.float32),
        "medium_filter": draw_medium_filter(jax.random.fold_in(arg_keys[6], 71), 0),
        "skip_bias": gaussian(arg_keys[3], (D,), 1.0, 4.0, ((0, 8),), jnp.float32),
        "cotangent": gaussian(arg_keys[4], (SEQ, D), 1.0, 6.0, ((0, 32), (1, 8))),
        "doc_lengths": uneven_parts(arg_keys[5], DOCS, SEQ, MOST, 2).astype(jnp.int32),
    }


def rounded(quantity):
    return lax.optimization_barrier(quantity.astype(jnp.bfloat16))

def reference(features, short_filter, medium_filter, skip_bias, cotangent, doc_lengths):
    slot_ids = jnp.arange(N_CTX, dtype=jnp.int32)
    slot_stretch = jnp.stack([slot_ids, 2 * N_CTX - 1 - slot_ids], axis=1).reshape(-1)

    def to_sequence(source):
        pieces = source.reshape((2 * N_CTX, STRETCH) + source.shape[1:])
        return jnp.zeros_like(pieces).at[slot_stretch].set(pieces).reshape(source.shape)

    def to_slots(source):
        pieces = source.reshape((2 * N_CTX, STRETCH) + source.shape[1:])
        return pieces[slot_stretch].reshape(source.shape)
    inputs = to_sequence(features)
    upstream = to_sequence(cotangent).astype(jnp.float32)
    starts = (jnp.cumsum(doc_lengths) - doc_lengths).astype(jnp.int32)
    position = jnp.arange(SEQ, dtype=jnp.int32)
    start_at = lax.optimization_barrier(jnp.max(jnp.where(starts[None, :] <= position[:, None], starts[None, :], 0), axis=1)).astype(jnp.int32)
    offset = position - start_at
    running = jnp.zeros(inputs.shape, jnp.float32)
    for tap_lag in range(SE_LEN):
        moved = jnp.pad(inputs, ((tap_lag, 0), (0, 0), (0, 0)))[:SEQ].astype(jnp.float32)
        running = running + jnp.where((offset >= tap_lag)[:, None, None], short_filter[tap_lag] * moved, 0.0)
    featurized = rounded(running)
    query_rows = featurized[:, 0].astype(jnp.float32)
    key_rows = featurized[:, 1].astype(jnp.float32)
    value_rows = featurized[:, 2].astype(jnp.float32)
    mixed = rounded(key_rows * value_rows).astype(jnp.float32)
    grad_mixed = rounded(upstream * query_rows).astype(jnp.float32)
    filter_taps = rounded(medium_filter).astype(jnp.float32).T
    row_index = jnp.arange(128)[:, None]
    col_index = jnp.arange(256)[None, :]
    lag_forward = row_index + 128 - col_index
    forward_taps = jnp.where(((lag_forward >= 0) & (lag_forward < MR_LEN))[None], filter_taps[:, jnp.clip(lag_forward, 0, MR_LEN - 1)], 0.0)
    lag_backward = col_index - row_index
    backward_taps = jnp.where(((lag_backward >= 0) & (lag_backward < MR_LEN))[None], filter_taps[:, jnp.clip(lag_backward, 0, MR_LEN - 1)], 0.0)
    diag_cols = jnp.arange(128)[:, None] + 128 - jnp.arange(128)[None, :]
    padded_mixed = jnp.concatenate([jnp.zeros((128, D), mixed.dtype), mixed])
    padded_grad = jnp.concatenate([grad_mixed, jnp.zeros((128, D), grad_mixed.dtype)])
    padded_start = jnp.concatenate([start_at, jnp.zeros((128,), jnp.int32)])

    def one_block(block_index):
        first_row = block_index * 128
        window = lax.dynamic_slice_in_dim(padded_mixed, first_row, 256, 0).reshape(256, GROUPS, GROUP)
        grad_window = lax.dynamic_slice_in_dim(padded_grad, first_row, 256, 0).reshape(256, GROUPS, GROUP)
        own_grad = lax.dynamic_slice_in_dim(grad_mixed, first_row, 128, 0).reshape(128, GROUPS, GROUP)
        row_start = lax.dynamic_slice_in_dim(start_at, first_row, 128, 0)
        source_pos = first_row - 128 + jnp.arange(256, dtype=jnp.int32)
        keep_forward = source_pos[None, :] >= row_start[:, None]
        toeplitz = jnp.where(keep_forward[None], forward_taps, 0.0)
        convolved = jnp.einsum('gts,sgc->tgc', toeplitz, window).reshape(128, D)
        pairwise = jnp.where(keep_forward[None], jnp.einsum('tgc,sgc->gts', own_grad, window), 0.0)
        tap_grads = lax.optimization_barrier(jnp.sum(pairwise[:, row_index, diag_cols], axis=1))
        target_start = lax.dynamic_slice_in_dim(padded_start, first_row, 256, 0)
        own_pos = first_row + jnp.arange(128, dtype=jnp.int32)
        keep_backward = own_pos[:, None] >= target_start[None, :]
        backward = jnp.einsum('gst,tgc->sgc', jnp.where(keep_backward[None], backward_taps, 0.0), grad_window).reshape(128, D)
        return (convolved, backward, tap_grads)
    conv_all, back_all, taps_all = lax.map(one_block, jnp.arange(SEQ // 128, dtype=jnp.int32))
    medium = conv_all.reshape(SEQ, D) + skip_bias * mixed
    grad_query = upstream * medium
    grad_conv = back_all.reshape(SEQ, D) + skip_bias * grad_mixed
    grad_stack = rounded(jnp.stack([grad_query, grad_conv * value_rows, grad_conv * key_rows], axis=1))
    grad_inputs = jnp.zeros(inputs.shape, jnp.float32)
    short_grads = []
    for tap_lag in range(SE_LEN):
        later = jnp.pad(grad_stack, ((0, tap_lag), (0, 0), (0, 0)))[tap_lag:].astype(jnp.float32)
        later_offset = jnp.pad(offset, (0, tap_lag), constant_values=-1)[tap_lag:]
        grad_inputs = grad_inputs + jnp.where((later_offset >= tap_lag)[:, None, None], short_filter[tap_lag] * later, 0.0)
        moved = jnp.pad(inputs, ((tap_lag, 0), (0, 0), (0, 0)))[:SEQ].astype(jnp.float32)
        short_grads.append(lax.optimization_barrier(jnp.sum(jnp.where((offset >= tap_lag)[:, None, None], grad_stack.astype(jnp.float32) * moved, 0.0), axis=0)))
    scale = 1.0 / math.sqrt(SEQ)
    return (to_slots(grad_inputs.astype(jnp.bfloat16)), jnp.stack(short_grads) * scale, lax.optimization_barrier(jnp.sum(taps_all, axis=0)).T * scale, lax.optimization_barrier(jnp.sum(grad_mixed * mixed, axis=0)) * scale)
```

```python
import functools
import math

import jax
import jax.numpy as jnp
from jax import lax
from jax.experimental import pallas as pl
from jax.experimental.pallas import tpu as pltpu
from jax.sharding import PartitionSpec as P

STRETCH = 256
TILE = 128
GROUP = 16
PER_TILE = TILE // GROUP
LAGS = 128
TAPS = 7
EDGE = 16
TAIL = 128 + 3 * EDGE
HEAD = 144 + 4 * EDGE
DOCS = 64
F32 = jnp.float32
BF16 = jnp.bfloat16


def base_of(device, members, member):
    first = device * STRETCH
    second = (2 * members - 1 - device) * STRETCH
    if isinstance(member, int):
        return first if member == 0 else second
    return jnp.where(member == 0, first, second)


def lane_starts(lengths_ref, base, count):
    position = (base + lax.broadcasted_iota(jnp.int32, (8, count), 1)).astype(F32)
    found = jnp.zeros((8, count), F32)
    running = jnp.int32(0)
    for doc in range(DOCS):
        here = running.astype(F32)
        found = jnp.where(position >= here, here, found)
        running = running + lengths_ref[doc]
    return found


def row_starts(starts, block):
    row = starts[0:1, block * 128 : (block + 1) * 128]
    return jnp.broadcast_to(row, (128, 128)).T


def row_positions(base, block):
    return (base + block * 128 + lax.broadcasted_iota(jnp.int32, (128, 128), 0)).astype(F32)


def own_kernel(
    members, device_ref, lengths_ref, feat_ref, cot_ref, taps_ref,
    kvg_ref, up_ref, down_ref, masks, rows,
):
    device = device_ref[0]

    @pl.when(pl.program_id(0) == 0)
    def _():
        for member in range(2):
            base = base_of(device, members, member)
            starts = lane_starts(lengths_ref, base, STRETCH)
            for block in range(2):
                offset = row_positions(base, block) - row_starts(starts, block)
                for lag in range(1, TAPS):
                    masks[member, lag - 1, pl.ds(block * 128, 128), :] = jnp.where(
                        offset >= lag, 1.0, 0.0
                    )

    for member in range(2):
        first = member * STRETCH
        for stream in range(3):
            rows[pl.ds(0, 8), :] = jnp.zeros((8, TILE), F32)
            rows[pl.ds(8, STRETCH), :] = feat_ref[stream, pl.ds(first, STRETCH), :].astype(F32)
            weights = taps_ref[stream]
            for chunk in range(0, STRETCH, 64):
                total = rows[pl.ds(8 + chunk, 64), :] * weights[0:1, :]
                for lag in range(1, TAPS):
                    moved = rows[pl.ds(8 + chunk - lag, 64), :] * weights[lag : lag + 1, :]
                    total = total + moved * masks[member, lag - 1, pl.ds(chunk, 64), :]
                rounded = total.astype(BF16)
                if stream == 0:
                    cot = cot_ref[pl.ds(first + chunk, 64), :].astype(F32)
                    rounded = (cot * rounded.astype(F32)).astype(BF16)
                    kvg_ref[2, pl.ds(first + chunk, 64), :] = rounded
                else:
                    kvg_ref[stream - 1, pl.ds(first + chunk, 64), :] = rounded
    for member in range(2):
        first = member * STRETCH
        tail_ref = up_ref if member == 0 else down_ref
        head_ref = down_ref if member == 0 else up_ref
        last = first + 128
        mixed = kvg_ref[0, pl.ds(last, 128), :].astype(F32) * kvg_ref[1, pl.ds(last, 128), :].astype(F32)
        tail_ref[pl.ds(0, 128), :] = mixed.astype(BF16)
        for stream in range(3):
            tail_ref[pl.ds(128 + stream * EDGE, EDGE), :] = feat_ref[
                stream, pl.ds(first + STRETCH - EDGE, EDGE), :
            ]
            head_ref[pl.ds(TAIL + 144 + stream * EDGE, EDGE), :] = feat_ref[
                stream, pl.ds(first, EDGE), :
            ]
        head_ref[pl.ds(TAIL, 144), :] = kvg_ref[2, pl.ds(first, 144), :]
        head_ref[pl.ds(TAIL + 144 + 3 * EDGE, EDGE), :] = cot_ref[pl.ds(first, EDGE), :]


def tables_kernel(
    members, device_ref, lengths_ref, medium_ref,
    forward_ref, backward_ref, keep_f_ref, keep_b_ref, keep_r_ref, shifted_ref, edge_ref,
    forward_rows, backward_rows, offsets,
):
    device = device_ref[0]

    @pl.when(pl.program_id(0) == 0)
    def _():
        lag = lax.broadcasted_iota(jnp.int32, (LAGS, 256), 0)
        lane = lax.broadcasted_iota(jnp.int32, (LAGS, 256), 1)
        taps = medium_ref[...].astype(BF16)
        dims = (((0,), (0,)), ((), ()))
        place_f = jnp.where(lane == LAGS - lag, 1.0, 0.0).astype(BF16)
        place_b = jnp.where(lane == lag, 1.0, 0.0).astype(BF16)
        forward_rows[...] = lax.dot_general(taps, place_f, dims, preferred_element_type=F32)
        backward_rows[...] = lax.dot_general(taps, place_b, dims, preferred_element_type=F32)
        wide = lax.broadcasted_iota(jnp.int32, (128, 256), 1)
        tall = lax.broadcasted_iota(jnp.int32, (128, 256), 0)
        for member in range(2):
            base = base_of(device, members, member)
            starts = lane_starts(lengths_ref, base, 512)
            for block in range(3):
                begin = row_starts(starts, block)
                begin = jnp.concatenate([begin, begin], axis=1)
                source = (base + (block - 1) * 128 + wide).astype(F32)
                keep_f_ref[member, block] = jnp.where(source >= begin, 1.0, 0.0).astype(BF16)
                if block < 2:
                    turned = (base + (block - 1) * 128 + 255 - wide).astype(F32)
                    keep_r_ref[member, block] = jnp.where(turned >= begin, 1.0, 0.0)
                own = (base + block * 128 + tall).astype(F32)
                target = jnp.broadcast_to(starts[0:1, block * 128 : block * 128 + 256], (128, 256))
                keep_b_ref[member, block] = jnp.where(own >= target, 1.0, 0.0).astype(BF16)
                offsets[pl.ds(block * 128, 128), :] = row_positions(base, block) - begin[:, :128]
            for lag in range(1, TAPS):
                shifted_ref[member, lag - 1] = jnp.where(
                    offsets[pl.ds(lag, STRETCH), :] >= lag, 1.0, 0.0
                )
                for side in range(2):
                    edge_ref[member, side, lag - 1] = jnp.where(
                        offsets[pl.ds(side * STRETCH, EDGE), :] >= lag, 1.0, 0.0
                    )

    first = pl.multiple_of(device_ref[1] * 32 + pl.program_id(0) * PER_TILE, PER_TILE)
    rows_f = forward_rows[pl.ds(first, PER_TILE), :]
    rows_b = backward_rows[pl.ds(first, PER_TILE), :]
    for group in range(PER_TILE):
        for rows, out_ref in ((rows_f, forward_ref), (rows_b, backward_ref)):
            spread = jnp.broadcast_to(rows[group : group + 1, :], (128, 256))
            out_ref[group] = pltpu.roll(spread, 0, 1, stride=1, stride_axis=0).astype(BF16)


def edge_conv(rows, weights, edge_ref, side):
    total = rows[pl.ds(EDGE, EDGE), :] * weights[0:1, :]
    for lag in range(1, TAPS):
        moved = rows[pl.ds(EDGE - lag, EDGE), :] * weights[lag : lag + 1, :]
        total = total + moved * edge_ref[side, lag - 1]
    return total.astype(BF16).astype(F32)


def main_kernel(
    members, device_ref, feat_ref, kvg_ref, cot_ref, own_up_ref, up_ref, down_ref, taps_ref, skip_ref,
    forward_ref, backward_ref, keep_f_ref, keep_b_ref, keep_r_ref, shifted_ref, edge_ref,
    out_ref, sums_ref,
    left, right, rows, keys, values, mixed, grads, cots, stack, pairs,
):
    member = pl.program_id(1)
    is_last = device_ref[0] == members - 1

    @pl.when(member == 0)
    def _():
        left[...] = up_ref[pl.ds(0, TAIL), :]

    @pl.when((member == 1) & is_last)
    def _():
        left[...] = own_up_ref[pl.ds(0, TAIL), :]

    @pl.when((member == 1) & jnp.logical_not(is_last))
    def _():
        left[...] = down_ref[pl.ds(0, TAIL), :]

    @pl.when(member == 1)
    def _():
        right[...] = up_ref[pl.ds(TAIL, HEAD), :]

    @pl.when((member == 0) & is_last)
    def _():
        right[...] = own_up_ref[pl.ds(TAIL, HEAD), :]

    @pl.when((member == 0) & jnp.logical_not(is_last))
    def _():
        right[...] = down_ref[pl.ds(TAIL, HEAD), :]

    keys[pl.ds(EDGE, STRETCH - EDGE), :] = kvg_ref[0, pl.ds(EDGE, STRETCH - EDGE), :].astype(F32)
    values[pl.ds(EDGE, STRETCH - EDGE), :] = kvg_ref[1, pl.ds(EDGE, STRETCH - EDGE), :].astype(F32)
    cots[pl.ds(0, STRETCH), :] = cot_ref[...].astype(F32)
    cots[pl.ds(STRETCH, EDGE), :] = right[pl.ds(144 + 3 * EDGE, EDGE), :].astype(F32)
    for stream in range(3):
        weights = taps_ref[stream]
        for side in range(2):
            if side == 0:
                before = left[pl.ds(128 + stream * EDGE, EDGE), :]
                after = feat_ref[stream, pl.ds(0, EDGE), :]
            else:
                before = feat_ref[stream, pl.ds(STRETCH - EDGE, EDGE), :]
                after = right[pl.ds(144 + stream * EDGE, EDGE), :]
            rows[pl.ds(0, EDGE), :] = before.astype(F32)
            rows[pl.ds(EDGE, EDGE), :] = after.astype(F32)
            fixed = edge_conv(rows, weights, edge_ref.at[0], side)
            place = pl.ds(side * STRETCH, EDGE)
            if stream == 0:
                grads[place, :] = (cots[place, :] * fixed).astype(BF16)
            elif stream == 1:
                keys[place, :] = fixed
            else:
                values[place, :] = fixed
    mixed[pl.ds(0, 128), :] = left[pl.ds(0, 128), :]
    mixed[pl.ds(128, STRETCH + EDGE), :] = (keys[...] * values[...]).astype(BF16)
    mixed[pl.ds(400, 112), :] = jnp.zeros((112, TILE), BF16)
    grads[pl.ds(EDGE, STRETCH - EDGE), :] = kvg_ref[2, pl.ds(EDGE, STRETCH - EDGE), :]
    grads[pl.ds(STRETCH + EDGE, 128), :] = right[pl.ds(EDGE, 128), :]
    grads[pl.ds(400, 112), :] = jnp.zeros((112, TILE), BF16)

    lane_group = lax.broadcasted_iota(jnp.int32, (128, TILE), 1) // GROUP
    skip = skip_ref[...]
    turn = jnp.where(
        lax.broadcasted_iota(jnp.int32, (256, 256), 0) + lax.broadcasted_iota(jnp.int32, (256, 256), 1) == 255,
        1.0, 0.0,
    ).astype(BF16)

    def convolved(table_ref, keep_ref, window, block):
        height = 128 if block < 2 else EDGE
        keep = keep_ref[0, block, pl.ds(0, height), :]
        result = jnp.zeros((height, TILE), F32)
        for group in range(PER_TILE):
            matrix = table_ref[group, pl.ds(0, height), :] * keep
            product = jnp.dot(matrix, window, preferred_element_type=F32)
            result = jnp.where(lane_group[:height] == group, product, result)
        return result

    for block in range(3):
        height = 128 if block < 2 else EDGE
        place = pl.ds(block * 128, height)
        window = mixed[pl.ds(block * 128, 256), :]
        medium = convolved(forward_ref, keep_f_ref, window, block)
        medium = medium + skip * mixed[pl.ds(block * 128 + 128, height), :].astype(F32)
        grad_conv = convolved(backward_ref, keep_b_ref, grads[pl.ds(block * 128, 256), :], block)
        grad_conv = grad_conv + skip * grads[place, :].astype(F32)
        stack[0, place, :] = (cots[place, :] * medium).astype(BF16).astype(F32)
        stack[1, place, :] = (grad_conv * values[place, :]).astype(BF16).astype(F32)
        stack[2, place, :] = (grad_conv * keys[place, :]).astype(BF16).astype(F32)
        if block < 2:
            turned = jnp.dot(turn, window, preferred_element_type=F32).astype(BF16)
            own = grads[place, :]
            for group in range(PER_TILE):
                chosen = jnp.where(lane_group == group, own.astype(F32), 0.0).astype(BF16)
                pair = lax.dot_general(
                    chosen, turned, (((1,), (1,)), ((), ())), preferred_element_type=F32
                )
                pair = pair * keep_r_ref[0, block]
                if block == 0:
                    @pl.when(member == 0)
                    def _():
                        pairs[group] = pair

                    @pl.when(member == 1)
                    def _():
                        pairs[group] = pairs[group] + pair
                else:
                    pairs[group] = pairs[group] + pair

    @pl.when(member == 0)
    def _():
        sums_ref[...] = jnp.zeros(sums_ref.shape, F32)

    for stream in range(3):
        weights = taps_ref[stream]
        partial = [jnp.zeros((8, TILE), F32) for _ in range(TAPS)]
        for chunk in range(0, STRETCH, 64):
            source = feat_ref[stream, pl.ds(chunk, 64), :].astype(F32)
            total = jnp.zeros((64, TILE), F32)
            for lag in range(TAPS):
                later = stack[stream, pl.ds(chunk + lag, 64), :]
                if lag > 0:
                    later = later * shifted_ref[0, lag - 1, pl.ds(chunk, 64), :]
                total = total + later * weights[lag : lag + 1, :]
                partial[lag] = partial[lag] + jnp.sum((later * source).reshape(8, 8, TILE), axis=0)
            out_ref[stream, pl.ds(chunk, 64), :] = total.astype(BF16)
        for lag in range(TAPS):
            row = pl.ds(stream * 8 + lag, 1)
            sums_ref[row, :] += jnp.sum(partial[lag], axis=0, keepdims=True)
    bias = jnp.sum(
        grads[pl.ds(0, STRETCH), :].astype(F32) * mixed[pl.ds(128, STRETCH), :].astype(F32),
        axis=0, keepdims=True,
    )
    sums_ref[pl.ds(7, 1), :] += bias

    @pl.when(member == 1)
    def _():
        for group in range(PER_TILE):
            turned_back = pltpu.roll(pairs[group], 129, 1, stride=1, stride_axis=0)
            sums_ref[pl.ds(24 + group, 1), :] = jnp.sum(turned_back, axis=0, keepdims=True)[:, :LAGS]


def turn_kernel(scale, gathered_ref, out_ref):
    out_ref[...] = gathered_ref[...].T * scale


def exchange(block, axis, flip):
    size = lax.axis_size(axis)
    return lax.ppermute(block, axis, [(i, i ^ flip) for i in range(size)])


def shards(features, short_filter, medium_filter, skip_bias, cotangent, doc_lengths):
    members = lax.axis_size("ctx")
    device = lax.axis_index("ctx")
    tp = lax.axis_index("tp")
    channels = features.shape[2]
    tiles = channels // TILE
    scale = 1.0 / math.sqrt(2 * STRETCH * members)
    streams = jnp.transpose(features, (1, 0, 2))
    weights = jnp.transpose(short_filter, (1, 0, 2))
    where_am_i = jnp.stack([device, tp]).astype(jnp.int32)
    smem = pl.BlockSpec(memory_space=pltpu.SMEM)
    shape = jax.ShapeDtypeStruct
    params = pltpu.CompilerParams(vmem_limit_bytes=40 * 1024 * 1024)

    kvg, pay_up, pay_down = pl.pallas_call(
        functools.partial(own_kernel, members),
        grid=(tiles,),
        in_specs=[
            smem, smem,
            pl.BlockSpec((3, 2 * STRETCH, TILE), lambda l: (0, 0, l)),
            pl.BlockSpec((2 * STRETCH, TILE), lambda l: (0, l)),
            pl.BlockSpec((3, TAPS, TILE), lambda l: (0, 0, l)),
        ],
        out_specs=[
            pl.BlockSpec((3, 2 * STRETCH, TILE), lambda l: (0, 0, l)),
            pl.BlockSpec((TAIL + HEAD, TILE), lambda l: (0, l)),
            pl.BlockSpec((TAIL + HEAD, TILE), lambda l: (0, l)),
        ],
        out_shape=[
            shape((3, 2 * STRETCH, channels), BF16),
            shape((TAIL + HEAD, channels), BF16),
            shape((TAIL + HEAD, channels), BF16),
        ],
        scratch_shapes=[
            pltpu.VMEM((2, TAPS - 1, STRETCH, TILE), F32),
            pltpu.VMEM((STRETCH + 8, TILE), F32),
        ],
        compiler_params=params,
        cost_estimate=pl.CostEstimate(flops=40_000_000, bytes_accessed=4_500_000, transcendentals=0),
        name="own_rows",
    )(where_am_i, doc_lengths, streams, cotangent, weights)

    got_up = lax.ppermute(pay_up, "ctx", [(i, i + 1) for i in range(members - 1)])
    got_down = lax.ppermute(pay_down, "ctx", [(i + 1, i) for i in range(members - 1)])

    groups = channels // GROUP
    tables = pl.pallas_call(
        functools.partial(tables_kernel, members),
        grid=(tiles,),
        in_specs=[smem, smem, pl.BlockSpec(medium_filter.shape, lambda l: (0, 0))],
        out_specs=[
            pl.BlockSpec((PER_TILE, 128, 256), lambda l: (l, 0, 0)),
            pl.BlockSpec((PER_TILE, 128, 256), lambda l: (l, 0, 0)),
            pl.BlockSpec((2, 3, 128, 256), lambda l: (0, 0, 0, 0)),
            pl.BlockSpec((2, 3, 128, 256), lambda l: (0, 0, 0, 0)),
            pl.BlockSpec((2, 2, 128, 256), lambda l: (0, 0, 0, 0)),
            pl.BlockSpec((2, TAPS - 1, STRETCH, TILE), lambda l: (0, 0, 0, 0)),
            pl.BlockSpec((2, 2, TAPS - 1, EDGE, TILE), lambda l: (0, 0, 0, 0, 0)),
        ],
        out_shape=[
            shape((groups, 128, 256), BF16),
            shape((groups, 128, 256), BF16),
            shape((2, 3, 128, 256), BF16),
            shape((2, 3, 128, 256), BF16),
            shape((2, 2, 128, 256), F32),
            shape((2, TAPS - 1, STRETCH, TILE), F32),
            shape((2, 2, TAPS - 1, EDGE, TILE), F32),
        ],
        scratch_shapes=[
            pltpu.VMEM((256, 256), F32),
            pltpu.VMEM((256, 256), F32),
            pltpu.VMEM((384, TILE), F32),
        ],
        compiler_params=params,
        cost_estimate=pl.CostEstimate(flops=20_000_000, bytes_accessed=7_000_000, transcendentals=0),
        name="tables",
    )(where_am_i, doc_lengths, medium_filter)

    ends = pl.BlockSpec((TAIL + HEAD, TILE), lambda l, m: (0, l))
    matrix = pl.BlockSpec((PER_TILE, 128, 256), lambda l, m: (l, 0, 0))
    grad_streams, sums = pl.pallas_call(
        functools.partial(main_kernel, members),
        grid=(tiles, 2),
        in_specs=[
            smem,
            pl.BlockSpec((3, STRETCH, TILE), lambda l, m: (0, m, l)),
            pl.BlockSpec((3, STRETCH, TILE), lambda l, m: (0, m, l)),
            pl.BlockSpec((STRETCH, TILE), lambda l, m: (m, l)),
            ends, ends, ends,
            pl.BlockSpec((3, TAPS, TILE), lambda l, m: (0, 0, l)),
            pl.BlockSpec((1, TILE), lambda l, m: (0, l)),
            matrix, matrix,
            pl.BlockSpec((1, 3, 128, 256), lambda l, m: (m, 0, 0, 0)),
            pl.BlockSpec((1, 3, 128, 256), lambda l, m: (m, 0, 0, 0)),
            pl.BlockSpec((1, 2, 128, 256), lambda l, m: (m, 0, 0, 0)),
            pl.BlockSpec((1, TAPS - 1, STRETCH, TILE), lambda l, m: (m, 0, 0, 0)),
            pl.BlockSpec((1, 2, TAPS - 1, EDGE, TILE), lambda l, m: (m, 0, 0, 0, 0)),
        ],
        out_specs=[
            pl.BlockSpec((3, STRETCH, TILE), lambda l, m: (0, m, l)),
            pl.BlockSpec((32, TILE), lambda l, m: (0, l)),
        ],
        out_shape=[shape((3, 2 * STRETCH, channels), BF16), shape((32, channels), F32)],
        scratch_shapes=[
            pltpu.VMEM((TAIL, TILE), BF16),
            pltpu.VMEM((HEAD, TILE), BF16),
            pltpu.VMEM((2 * EDGE, TILE), F32),
            pltpu.VMEM((STRETCH + EDGE, TILE), F32),
            pltpu.VMEM((STRETCH + EDGE, TILE), F32),
            pltpu.VMEM((512, TILE), BF16),
            pltpu.VMEM((512, TILE), BF16),
            pltpu.VMEM((STRETCH + EDGE, TILE), F32),
            pltpu.VMEM((3, STRETCH + EDGE, TILE), F32),
            pltpu.VMEM((PER_TILE, 128, 256), F32),
        ],
        compiler_params=params,
        cost_estimate=pl.CostEstimate(flops=900_000_000, bytes_accessed=12_000_000, transcendentals=0),
        name="main_rows",
    )(
        where_am_i, streams, kvg, cotangent, pay_up, got_up, got_down, weights,
        skip_bias.reshape(1, channels), *tables,
    )

    flip = 1
    while flip < members:
        sums = sums + exchange(sums, "ctx", flip)
        flip *= 2
    mine = sums[24:].reshape(PER_TILE, tiles, LAGS).transpose(1, 0, 2).reshape(groups, LAGS)
    gathered = mine
    flip = 1
    while flip < lax.axis_size("tp"):
        other = exchange(gathered, "tp", flip)
        upper = (tp // flip) % 2 == 1
        gathered = jnp.concatenate(
            [jnp.where(upper, other, gathered), jnp.where(upper, gathered, other)], axis=0
        )
        flip *= 2
    grad_medium = pl.pallas_call(
        functools.partial(turn_kernel, scale),
        out_shape=shape(medium_filter.shape, F32),
        name="turn",
    )(gathered)
    short = jnp.transpose(sums[:24].reshape(3, 8, channels)[:, :TAPS], (1, 0, 2)) * scale
    return (jnp.transpose(grad_streams, (1, 0, 2)), short, grad_medium, sums[7] * scale)


def solution(mesh):
    in_specs = (P("ctx", None, "tp"), P(None, None, "tp"), P(), P("tp"), P("ctx", "tp"), P())
    out_specs = (P("ctx", None, "tp"), P(None, None, "tp"), P(), P("tp"))
    return jax.shard_map(shards, mesh=mesh, in_specs=in_specs, out_specs=out_specs, check_vma=False)
```

```python
import functools
import math

import jax
import jax.numpy as jnp
from jax import lax
from jax.experimental import pallas as pl
from jax.experimental.pallas import tpu as pltpu
from jax.sharding import PartitionSpec as P

STRETCH = 256
TILE = 128
GROUP = 16
PER_TILE = TILE // GROUP
LAGS = 128
TAPS = 7
EDGE = 16
TAIL = 128 + 3 * EDGE
HEAD = 144 + 4 * EDGE
DOCS = 64
F32 = jnp.float32
BF16 = jnp.bfloat16


def base_of(device, members, member):
    first = device * STRETCH
    second = (2 * members - 1 - device) * STRETCH
    if isinstance(member, int):
        return first if member == 0 else second
    return jnp.where(member == 0, first, second)


def lane_starts(lengths_ref, base, count):
    position = (base + lax.broadcasted_iota(jnp.int32, (8, count), 1)).astype(F32)
    found = jnp.zeros((8, count), F32)
    running = jnp.int32(0)
    for doc in range(DOCS):
        here = running.astype(F32)
        found = jnp.where(position >= here, here, found)
        running = running + lengths_ref[doc]
    return found


def row_starts(starts, block):
    row = starts[0:1, block * 128 : (block + 1) * 128]
    return jnp.broadcast_to(row, (128, 128)).T


def row_positions(base, block):
    return (base + block * 128 + lax.broadcasted_iota(jnp.int32, (128, 128), 0)).astype(F32)


def conv_rows(rows, weights, masks, member, first, count):
    total = rows[pl.ds(8 + first, count), :] * weights[0:1, :]
    for lag in range(1, TAPS):
        moved = rows[pl.ds(8 + first - lag, count), :] * weights[lag : lag + 1, :]
        total = total + moved * masks[member, lag - 1, pl.ds(first, count), :]
    return total.astype(BF16)


def own_masks(members, lengths_ref, masks):
    for member in range(2):
        base = base_of(lax.axis_index("ctx"), members, member)
        starts = lane_starts(lengths_ref, base, STRETCH)
        for block in range(2):
            offset = row_positions(base, block) - row_starts(starts, block)
            for lag in range(1, TAPS):
                masks[member, lag - 1, pl.ds(block * 128, 128), :] = jnp.where(offset >= lag, 1.0, 0.0)


def payload_kernel(
    members, lengths_ref, feat_hbm, cot_hbm, taps_ref, up_ref, down_ref, feat, cots, masks, rows, feat_sem, cot_sem,
):
    tiles = feat.shape[0]
    copies = []
    for tile in range(tiles):
        lanes = pl.ds(tile * TILE, TILE)
        copies.append((
            pltpu.make_async_copy(feat_hbm.at[:, :, lanes], feat.at[tile], feat_sem.at[tile]),
            pltpu.make_async_copy(cot_hbm.at[:, lanes], cots.at[tile], cot_sem.at[tile]),
        ))
        copies[-1][0].start()
        copies[-1][1].start()
    own_masks(members, lengths_ref, masks)
    rows[pl.ds(0, 8), :] = jnp.zeros((8, TILE), F32)
    for tile in range(tiles):
        lanes = pl.ds(tile * TILE, TILE)
        copies[tile][0].wait()
        copies[tile][1].wait()
        for member in range(2):
            first = member * STRETCH
            tail_ref = up_ref if member == 0 else down_ref
            head_ref = down_ref if member == 0 else up_ref
            rows[pl.ds(8, 144), :] = feat[tile, 0, pl.ds(first, 144), :].astype(F32)
            weights = taps_ref[0, :, lanes]
            for chunk in range(0, 144, 48):
                query = conv_rows(rows, weights, masks, member, chunk, 48).astype(F32)
                cot = cots[tile, pl.ds(first + chunk, 48), :].astype(F32)
                head_ref[pl.ds(TAIL + chunk, 48), lanes] = (cot * query).astype(BF16)
            for stream in (1, 2):
                rows[pl.ds(8 + 112, 144), :] = feat[tile, stream, pl.ds(first + 112, 144), :].astype(F32)
                weights = taps_ref[stream, :, lanes]
                for chunk in range(0, 128, 64):
                    part = conv_rows(rows, weights, masks, member, 128 + chunk, 64)
                    place = pl.ds(chunk, 64)
                    if stream == 2:
                        part = (tail_ref[place, lanes].astype(F32) * part.astype(F32)).astype(BF16)
                    tail_ref[place, lanes] = part
            for stream in range(3):
                tail_ref[pl.ds(128 + stream * EDGE, EDGE), lanes] = feat[
                    tile, stream, pl.ds(first + STRETCH - EDGE, EDGE), :
                ]
                head_ref[pl.ds(TAIL + 144 + stream * EDGE, EDGE), lanes] = feat[
                    tile, stream, pl.ds(first, EDGE), :
                ]
            head_ref[pl.ds(TAIL + 144 + 3 * EDGE, EDGE), lanes] = cots[tile, pl.ds(first, EDGE), :]


def own_kernel(members, lengths_ref, feat_ref, cot_ref, taps_ref, kvg_ref, masks, rows):
    @pl.when(pl.program_id(0) == 0)
    def _():
        own_masks(members, lengths_ref, masks)

    rows[pl.ds(0, 8), :] = jnp.zeros((8, TILE), F32)
    for member in range(2):
        first = member * STRETCH
        for stream in range(3):
            rows[pl.ds(8, STRETCH), :] = feat_ref[stream, pl.ds(first, STRETCH), :].astype(F32)
            weights = taps_ref[stream]
            for chunk in range(0, STRETCH, 64):
                rounded = conv_rows(rows, weights, masks, member, chunk, 64)
                if stream == 0:
                    cot = cot_ref[pl.ds(first + chunk, 64), :].astype(F32)
                    rounded = (cot * rounded.astype(F32)).astype(BF16)
                    kvg_ref[2, pl.ds(first + chunk, 64), :] = rounded
                else:
                    kvg_ref[stream - 1, pl.ds(first + chunk, 64), :] = rounded


def tables_kernel(
    members, lengths_ref, medium_ref,
    forward_ref, backward_ref, keep_f_ref, keep_b_ref, keep_r_ref, shifted_ref, edge_ref,
    forward_rows, backward_rows, offsets,
):
    device = lax.axis_index("ctx")

    @pl.when(pl.program_id(0) == 0)
    def _():
        lag = lax.broadcasted_iota(jnp.int32, (LAGS, 256), 0)
        lane = lax.broadcasted_iota(jnp.int32, (LAGS, 256), 1)
        taps = medium_ref[...].astype(BF16)
        dims = (((0,), (0,)), ((), ()))
        place_f = jnp.where(lane == LAGS - lag, 1.0, 0.0).astype(BF16)
        place_b = jnp.where(lane == lag, 1.0, 0.0).astype(BF16)
        forward_rows[...] = lax.dot_general(taps, place_f, dims, preferred_element_type=F32)
        backward_rows[...] = lax.dot_general(taps, place_b, dims, preferred_element_type=F32)
        wide = lax.broadcasted_iota(jnp.int32, (128, 256), 1)
        tall = lax.broadcasted_iota(jnp.int32, (128, 256), 0)
        narrow = lax.broadcasted_iota(jnp.int32, (128, 128), 1)
        for member in range(2):
            base = base_of(device, members, member)
            starts = lane_starts(lengths_ref, base, 512)
            for block in range(3):
                begin = row_starts(starts, block)
                begin = jnp.concatenate([begin, begin], axis=1)
                source = (base + (block - 1) * 128 + wide).astype(F32)
                keep_f_ref[member, block] = jnp.where(source >= begin, 1.0, 0.0).astype(BF16)
                if block < 2:
                    turned = jnp.where(
                        narrow + tall[:, :128] >= 127,
                        base + block * 128 + 127 - narrow, base + (block - 1) * 128 + 127 - narrow,
                    ).astype(F32)
                    keep_r_ref[member, block] = jnp.where(turned >= begin[:, :128], 1.0, 0.0)
                own = (base + block * 128 + tall).astype(F32)
                target = jnp.broadcast_to(starts[0:1, block * 128 : block * 128 + 256], (128, 256))
                keep_b_ref[member, block] = jnp.where(own >= target, 1.0, 0.0).astype(BF16)
                offsets[pl.ds(block * 128, 128), :] = row_positions(base, block) - begin[:, :128]
            for lag in range(1, TAPS):
                shifted_ref[member, lag - 1] = jnp.where(
                    offsets[pl.ds(lag, STRETCH), :] >= lag, 1.0, 0.0
                )
                for side in range(2):
                    edge_ref[member, side, lag - 1] = jnp.where(
                        offsets[pl.ds(side * STRETCH, EDGE), :] >= lag, 1.0, 0.0
                    )

    first = pl.multiple_of(lax.axis_index("tp") * 32 + pl.program_id(0) * PER_TILE, PER_TILE)
    rows_f = forward_rows[pl.ds(first, PER_TILE), :]
    rows_b = backward_rows[pl.ds(first, PER_TILE), :]
    for group in range(PER_TILE):
        for rows, out_ref in ((rows_f, forward_ref), (rows_b, backward_ref)):
            spread = jnp.broadcast_to(rows[group : group + 1, :], (128, 256))
            out_ref[group] = pltpu.roll(spread, 0, 1, stride=1, stride_axis=0).astype(BF16)


def edge_conv(rows, weights, edge_ref, side):
    total = rows[pl.ds(EDGE, EDGE), :] * weights[0:1, :]
    for lag in range(1, TAPS):
        moved = rows[pl.ds(EDGE - lag, EDGE), :] * weights[lag : lag + 1, :]
        total = total + moved * edge_ref[side, lag - 1]
    return total.astype(BF16).astype(F32)


def pair_kernel(
    members, feat_ref, kvg_ref, cot_ref, own_up_ref, up_ref, down_ref, taps_ref, keep_r_ref, edge_ref,
    mixed_ref, grads_ref, kv_ref, sums_ref,
    left, right, rows,
):
    member = pl.program_id(1)
    tile = pl.program_id(0)
    lanes = pl.ds(pl.multiple_of(tile * TILE, TILE), TILE)
    base = member * STRETCH

    def own(first, count):
        return pl.ds(pl.multiple_of(base + first, EDGE), count)

    is_last = lax.axis_index("ctx") == members - 1

    @pl.when(member == 0)
    def _():
        left[...] = up_ref[pl.ds(0, TAIL), lanes]

    @pl.when((member == 1) & is_last)
    def _():
        left[...] = own_up_ref[pl.ds(0, TAIL), lanes]

    @pl.when((member == 1) & jnp.logical_not(is_last))
    def _():
        left[...] = down_ref[pl.ds(0, TAIL), lanes]

    @pl.when(member == 1)
    def _():
        right[...] = up_ref[pl.ds(TAIL, HEAD), lanes]

    @pl.when((member == 0) & is_last)
    def _():
        right[...] = own_up_ref[pl.ds(TAIL, HEAD), lanes]

    @pl.when((member == 0) & jnp.logical_not(is_last))
    def _():
        right[...] = down_ref[pl.ds(TAIL, HEAD), lanes]

    inner = pl.ds(EDGE, STRETCH - EDGE)
    for side in range(2):
        place = pl.ds(side * STRETCH, EDGE)
        if side == 0:
            cot = cot_ref[own(0, EDGE), lanes]
        else:
            cot = right[pl.ds(144 + 3 * EDGE, EDGE), :]
        fixed = []
        for stream in range(3):
            if side == 0:
                before = left[pl.ds(128 + stream * EDGE, EDGE), :]
                after = feat_ref[stream, own(0, EDGE), lanes]
            else:
                before = feat_ref[stream, own(STRETCH - EDGE, EDGE), lanes]
                after = right[pl.ds(144 + stream * EDGE, EDGE), :]
            rows[pl.ds(0, EDGE), :] = before.astype(F32)
            rows[pl.ds(EDGE, EDGE), :] = after.astype(F32)
            fixed.append(edge_conv(rows, taps_ref[stream, :, lanes], edge_ref.at[member], side))
        grads_ref[member, place, lanes] = (cot.astype(F32) * fixed[0]).astype(BF16)
        kv_ref[member, 0, place, lanes] = fixed[1].astype(BF16)
        kv_ref[member, 1, place, lanes] = fixed[2].astype(BF16)
        mixed_ref[member, pl.ds(128 + side * STRETCH, EDGE), lanes] = (fixed[1] * fixed[2]).astype(BF16)
    keys = kvg_ref[0, own(EDGE, STRETCH - EDGE), lanes]
    values = kvg_ref[1, own(EDGE, STRETCH - EDGE), lanes]
    kv_ref[member, 0, inner, lanes] = keys
    kv_ref[member, 1, inner, lanes] = values
    mixed_ref[member, pl.ds(0, 128), lanes] = left[pl.ds(0, 128), :]
    mixed_ref[member, pl.ds(128 + EDGE, STRETCH - EDGE), lanes] = (keys.astype(F32) * values.astype(F32)).astype(BF16)
    mixed_ref[member, pl.ds(400, 112), lanes] = jnp.zeros((112, TILE), BF16)
    grads_ref[member, inner, lanes] = kvg_ref[2, own(EDGE, STRETCH - EDGE), lanes]
    grads_ref[member, pl.ds(STRETCH + EDGE, 128), lanes] = right[pl.ds(EDGE, 128), :]
    grads_ref[member, pl.ds(400, 112), lanes] = jnp.zeros((112, TILE), BF16)

    @pl.when(member == 1)
    def _():
        pair_sums(mixed_ref, grads_ref, keep_r_ref, sums_ref, tile, lanes)


def pair_sums(mixed_ref, grads_ref, keep_r_ref, sums_ref, tile, lanes):
    lane = lax.broadcasted_iota(jnp.int32, (128, TILE), 1)
    row = lax.broadcasted_iota(jnp.int32, (128, TILE), 0)
    lane_group = lane // GROUP
    near = lane + row >= 127
    turn = jnp.where(lane + row == 127, 1.0, 0.0).astype(BF16)
    sources = []
    for member in range(2):
        turned = [
            lax.dot_general(
                mixed_ref[member, pl.ds(piece * 128, 128), lanes], turn, (((0,), (0,)), ((), ())),
                preferred_element_type=F32,
            ).astype(BF16)
            for piece in range(3)
        ]
        for block in range(2):
            sources.append(jnp.concatenate([turned[block + 1], turned[block]], axis=1))
    for group in range(PER_TILE):
        choose = jnp.where(lane_group == group, 1.0, 0.0).astype(BF16)
        total = jnp.zeros((128, TILE), F32)
        for member in range(2):
            for block in range(2):
                chosen = grads_ref[member, pl.ds(block * 128, 128), lanes] * choose
                pair = jnp.dot(chosen, sources[member * 2 + block], preferred_element_type=F32)
                pair = jnp.where(near, pair[:, :128], pair[:, 128:])
                total = total + pair * keep_r_ref[member, block]
        lined_up = pltpu.roll(total, 1, 1, stride=1, stride_axis=0)
        sums_ref[pl.ds(tile * PER_TILE + group, 1), :] = jnp.sum(lined_up, axis=0, keepdims=True)


def conv_kernel(
    members, first_tile, feat_ref, mixed_ref, grads_ref, kv_ref, cot_ref, own_up_ref, up_ref, down_ref,
    taps_ref, skip_ref, forward_ref, backward_ref, keep_f_ref, keep_b_ref, shifted_ref,
    previous_ref, out_ref, sums_ref,
    cots, stack,
):
    del previous_ref
    member = pl.program_id(1)
    tile = first_tile + pl.program_id(0)
    lanes = pl.ds(pl.multiple_of(tile * TILE, TILE), TILE)
    base = member * STRETCH

    def own(first, count):
        return pl.ds(pl.multiple_of(base + first, EDGE), count)

    is_last = lax.axis_index("ctx") == members - 1
    first_group = tile * PER_TILE
    lane_group = lax.broadcasted_iota(jnp.int32, (128, TILE), 1) // GROUP
    skip = skip_ref[:, lanes]
    after = pl.ds(TAIL + 144 + 3 * EDGE, EDGE)
    beyond = pl.ds(STRETCH, EDGE)
    cots[pl.ds(0, STRETCH), :] = cot_ref[own(0, STRETCH), lanes].astype(F32)

    @pl.when(member == 1)
    def _():
        cots[beyond, :] = up_ref[after, lanes].astype(F32)

    @pl.when((member == 0) & is_last)
    def _():
        cots[beyond, :] = own_up_ref[after, lanes].astype(F32)

    @pl.when((member == 0) & jnp.logical_not(is_last))
    def _():
        cots[beyond, :] = down_ref[after, lanes].astype(F32)

    def convolved(table_ref, keep_ref, window, block):
        height = 128 if block < 2 else EDGE
        keep = keep_ref[member, block, pl.ds(0, height), :]
        result = jnp.zeros((height, TILE), F32)
        for group in range(PER_TILE):
            matrix = table_ref[first_group + group, pl.ds(0, height), :] * keep
            product = jnp.dot(matrix, window, preferred_element_type=F32)
            result = jnp.where(lane_group[:height] == group, product, result)
        return result

    for block in range(3):
        height = 128 if block < 2 else EDGE
        place = pl.ds(block * 128, height)
        medium = convolved(forward_ref, keep_f_ref, mixed_ref[member, pl.ds(block * 128, 256), lanes], block)
        medium = medium + skip * mixed_ref[member, pl.ds(block * 128 + 128, height), lanes].astype(F32)
        grad_conv = convolved(backward_ref, keep_b_ref, grads_ref[member, pl.ds(block * 128, 256), lanes], block)
        grad_conv = grad_conv + skip * grads_ref[member, place, lanes].astype(F32)
        for stream in range(3):
            if stream == 0:
                product = cots[place, :] * medium
            else:
                product = grad_conv * kv_ref[member, 2 - stream, place, lanes].astype(F32)
            stack[stream, place, :] = product.astype(BF16).astype(F32)

    @pl.when(member == 0)
    def _():
        sums_ref[...] = jnp.zeros(sums_ref.shape, F32)

    for stream in range(3):
        weights = taps_ref[stream, :, lanes]
        partial = [jnp.zeros((8, TILE), F32) for _ in range(TAPS)]
        for chunk in range(0, STRETCH, 64):
            source = feat_ref[stream, own(chunk, 64), lanes].astype(F32)
            total = jnp.zeros((64, TILE), F32)
            for lag in range(TAPS):
                later = stack[stream, pl.ds(chunk + lag, 64), :]
                if lag > 0:
                    later = later * shifted_ref[member, lag - 1, pl.ds(chunk, 64), :]
                total = total + later * weights[lag : lag + 1, :]
                partial[lag] = partial[lag] + jnp.sum((later * source).reshape(8, 8, TILE), axis=0)
            out_ref[stream, pl.ds(chunk, 64), :] = total.astype(BF16)
        for lag in range(TAPS):
            row = pl.ds(stream * 8 + lag, 1)
            sums_ref[row, :] += jnp.sum(partial[lag], axis=0, keepdims=True)
    bias = jnp.sum(
        grads_ref[member, pl.ds(0, STRETCH), lanes].astype(F32) * mixed_ref[member, pl.ds(128, STRETCH), lanes].astype(F32),
        axis=0, keepdims=True,
    )
    sums_ref[pl.ds(7, 1), :] += bias


def turn_kernel(scale, gathered_ref, out_ref):
    out_ref[...] = gathered_ref[...].T * scale


def along(block, axis, route):
    return lax.ppermute(block, axis, route)


def routes_z():
    return [
        [(i, i // 8 * 8 + 7 - i % 8) for i in range(32)],
        [(i, i ^ 1) for i in range(32)],
        [(i, i ^ 2) for i in range(32)],
    ]


def routes_x():
    return [[(i, (3 - i // 8) * 8 + i % 8) for i in range(32)], [(i, i ^ 8) for i in range(32)]]


def shards(features, short_filter, medium_filter, skip_bias, cotangent, doc_lengths):
    members = lax.axis_size("ctx")
    tp = lax.axis_index("tp")
    channels = features.shape[2]
    tiles = channels // TILE
    scale = 1.0 / math.sqrt(2 * STRETCH * members)
    streams = jnp.transpose(features, (1, 0, 2))
    weights = jnp.transpose(short_filter, (1, 0, 2))
    smem = pl.BlockSpec(memory_space=pltpu.SMEM)
    shape = jax.ShapeDtypeStruct
    params = pltpu.CompilerParams(vmem_limit_bytes=40 * 1024 * 1024)

    whole = pl.BlockSpec(memory_space=pltpu.VMEM)
    anywhere = pl.BlockSpec(memory_space=pl.ANY)
    pay_up, pay_down = pl.pallas_call(
        functools.partial(payload_kernel, members),
        in_specs=[smem, anywhere, anywhere, whole],
        out_specs=[whole, whole],
        out_shape=[shape((TAIL + HEAD, channels), BF16), shape((TAIL + HEAD, channels), BF16)],
        scratch_shapes=[
            pltpu.VMEM((tiles, 3, 2 * STRETCH, TILE), BF16),
            pltpu.VMEM((tiles, 2 * STRETCH, TILE), BF16),
            pltpu.VMEM((2, TAPS - 1, STRETCH, TILE), F32),
            pltpu.VMEM((STRETCH + 8, TILE), F32),
            pltpu.SemaphoreType.DMA((tiles,)),
            pltpu.SemaphoreType.DMA((tiles,)),
        ],
        compiler_params=pltpu.CompilerParams(vmem_limit_bytes=56 * 1024 * 1024),
        cost_estimate=pl.CostEstimate(flops=20_000_000, bytes_accessed=2_800_000, transcendentals=0),
        name="payload_rows",
    )(doc_lengths, streams, cotangent, weights)

    got_up = lax.ppermute(pay_up, "ctx", [(i, i + 1) for i in range(members - 1)])
    got_down = lax.ppermute(pay_down, "ctx", [(i + 1, i) for i in range(members - 1)])

    kvg = pl.pallas_call(
        functools.partial(own_kernel, members),
        grid=(tiles,),
        in_specs=[
            smem,
            pl.BlockSpec((3, 2 * STRETCH, TILE), lambda l: (0, 0, l)),
            pl.BlockSpec((2 * STRETCH, TILE), lambda l: (0, l)),
            pl.BlockSpec((3, TAPS, TILE), lambda l: (0, 0, l)),
        ],
        out_specs=pl.BlockSpec((3, 2 * STRETCH, TILE), lambda l: (0, 0, l)),
        out_shape=shape((3, 2 * STRETCH, channels), BF16),
        scratch_shapes=[
            pltpu.VMEM((2, TAPS - 1, STRETCH, TILE), F32),
            pltpu.VMEM((STRETCH + 8, TILE), F32),
        ],
        compiler_params=params,
        cost_estimate=pl.CostEstimate(flops=40_000_000, bytes_accessed=4_500_000, transcendentals=0),
        name="own_rows",
    )(doc_lengths, streams, cotangent, weights)

    groups = channels // GROUP
    tables = pl.pallas_call(
        functools.partial(tables_kernel, members),
        grid=(tiles,),
        in_specs=[smem, pl.BlockSpec(medium_filter.shape, lambda l: (0, 0))],
        out_specs=[
            pl.BlockSpec((PER_TILE, 128, 256), lambda l: (l, 0, 0)),
            pl.BlockSpec((PER_TILE, 128, 256), lambda l: (l, 0, 0)),
            pl.BlockSpec((2, 3, 128, 256), lambda l: (0, 0, 0, 0)),
            pl.BlockSpec((2, 3, 128, 256), lambda l: (0, 0, 0, 0)),
            pl.BlockSpec((2, 2, 128, 128), lambda l: (0, 0, 0, 0)),
            pl.BlockSpec((2, TAPS - 1, STRETCH, TILE), lambda l: (0, 0, 0, 0)),
            pl.BlockSpec((2, 2, TAPS - 1, EDGE, TILE), lambda l: (0, 0, 0, 0, 0)),
        ],
        out_shape=[
            shape((groups, 128, 256), BF16),
            shape((groups, 128, 256), BF16),
            shape((2, 3, 128, 256), BF16),
            shape((2, 3, 128, 256), BF16),
            shape((2, 2, 128, 128), F32),
            shape((2, TAPS - 1, STRETCH, TILE), F32),
            shape((2, 2, TAPS - 1, EDGE, TILE), F32),
        ],
        scratch_shapes=[
            pltpu.VMEM((256, 256), F32),
            pltpu.VMEM((256, 256), F32),
            pltpu.VMEM((384, TILE), F32),
        ],
        compiler_params=params,
        cost_estimate=pl.CostEstimate(flops=20_000_000, bytes_accessed=7_000_000, transcendentals=0),
        name="tables",
    )(doc_lengths, medium_filter)

    forward, backward, keep_f, keep_b, keep_r, shifted, edge = tables
    mixed, grads, kv, taps = pl.pallas_call(
        functools.partial(pair_kernel, members),
        grid=(tiles, 2),
        in_specs=[whole] * 9,
        out_specs=[whole] * 4,
        out_shape=[
            shape((2, 512, channels), BF16),
            shape((2, 512, channels), BF16),
            shape((2, 2, STRETCH + EDGE, channels), BF16),
            shape((groups, LAGS), F32),
        ],
        scratch_shapes=[
            pltpu.VMEM((TAIL, TILE), BF16),
            pltpu.VMEM((HEAD, TILE), BF16),
            pltpu.VMEM((2 * EDGE, TILE), F32),
        ],
        compiler_params=params,
        cost_estimate=pl.CostEstimate(flops=500_000_000, bytes_accessed=10_000_000, transcendentals=0),
        name="pair_rows",
    )(streams, kvg, cotangent, pay_up, got_up, got_down, weights, keep_r, edge)

    def convolve(first, count, mixed, grads, previous):
        return pl.pallas_call(
            functools.partial(conv_kernel, members, first),
            grid=(count, 2),
            in_specs=[whole] * 15 + [anywhere],
            out_specs=[
                pl.BlockSpec((3, STRETCH, TILE), lambda l, m: (0, m, first + l)),
                pl.BlockSpec((24, TILE), lambda l, m: (0, l)),
            ],
            out_shape=[
                shape((3, 2 * STRETCH, channels), BF16),
                shape((24, count * TILE), F32),
            ],
            input_output_aliases={15: 0} if first > 0 else {},
            scratch_shapes=[
                pltpu.VMEM((STRETCH + EDGE, TILE), F32),
                pltpu.VMEM((3, STRETCH + EDGE, TILE), F32),
            ],
            compiler_params=params,
            cost_estimate=pl.CostEstimate(flops=count * 100_000_000, bytes_accessed=count * 2_500_000, transcendentals=0),
            name=f"conv_rows_{first}",
        )(
            streams, mixed, grads, kv, cotangent, pay_up, got_up, got_down,
            weights, skip_bias.reshape(1, channels), forward, backward, keep_f, keep_b, shifted, previous,
        )

    parts = []
    grad_streams = kvg
    for route, (first, count) in zip(routes_x() + routes_z()[:1], ((0, 1), (1, 1), (2, 2))):
        other = along(taps, "ctx", route)
        grad_streams, part = convolve(first, count, mixed, grads, grad_streams)
        taps, mixed, grads, part = lax.optimization_barrier((taps + other, mixed, grads, part))
        parts.append(part)

    sums = jnp.concatenate(parts, axis=1)
    routes = routes_z()[1:] + routes_z()[:1] + routes_x()
    flip = 1
    for step, route in enumerate(routes):
        if step < 2:
            both = jnp.concatenate([sums, taps.reshape(8, channels)], axis=0)
            other = along(both, "ctx", route)
            both = both + other
            sums, taps = both[:24], both[24:].reshape(groups, LAGS)
        else:
            other = along(sums, "ctx", route)
            next_taps = along(taps, "tp", [(i, i ^ flip) for i in range(lax.axis_size("tp"))])
            upper = (tp // flip) % 2 == 1
            taps = jnp.concatenate(
                [jnp.where(upper, next_taps, taps), jnp.where(upper, taps, next_taps)], axis=0
            )
            sums = sums + other
            flip *= 2
        sums, taps = lax.optimization_barrier((sums, taps))
    grad_medium = pl.pallas_call(
        functools.partial(turn_kernel, scale),
        out_shape=shape(medium_filter.shape, F32),
        name="turn",
    )(taps)
    short = jnp.transpose(sums.reshape(3, 8, channels)[:, :TAPS], (1, 0, 2)) * scale
    return (jnp.transpose(grad_streams, (1, 0, 2)), short, grad_medium, sums[7] * scale)


def solution(mesh):
    in_specs = (P("ctx", None, "tp"), P(None, None, "tp"), P(), P("tp"), P("ctx", "tp"), P())
    out_specs = (P("ctx", None, "tp"), P(None, None, "tp"), P(), P("tp"))
    return jax.shard_map(shards, mesh=mesh, in_specs=in_specs, out_specs=out_specs, check_vma=False)
```

```python
import functools
import math

import jax
import jax.numpy as jnp
from jax import lax
from jax.experimental import pallas as pl
from jax.experimental.pallas import tpu as pltpu
from jax.sharding import PartitionSpec as P

STRETCH = 256
TILE = 128
GROUP = 16
PER_TILE = TILE // GROUP
LAGS = 128
TAPS = 7
EDGE = 16
TAIL = 128 + 3 * EDGE
HEAD = 144 + 4 * EDGE
DOCS = 64
F32 = jnp.float32
BF16 = jnp.bfloat16


def base_of(device, members, member):
    first = device * STRETCH
    second = (2 * members - 1 - device) * STRETCH
    if isinstance(member, int):
        return first if member == 0 else second
    return jnp.where(member == 0, first, second)


def lane_starts(lengths_ref, base, count):
    position = (base + lax.broadcasted_iota(jnp.int32, (8, count), 1)).astype(F32)
    found = jnp.zeros((8, count), F32)
    running = jnp.int32(0)
    for doc in range(DOCS):
        here = running.astype(F32)
        found = jnp.where(position >= here, here, found)
        running = running + lengths_ref[doc]
    return found


def row_starts(starts, block):
    row = starts[0:1, block * 128 : (block + 1) * 128]
    return jnp.broadcast_to(row, (128, 128)).T


def row_positions(base, block):
    return (base + block * 128 + lax.broadcasted_iota(jnp.int32, (128, 128), 0)).astype(F32)


def conv_rows(rows, weights, masks, member, first, count):
    total = rows[pl.ds(8 + first, count), :] * weights[0:1, :]
    for lag in range(1, TAPS):
        moved = rows[pl.ds(8 + first - lag, count), :] * weights[lag : lag + 1, :]
        total = total + moved * masks[member, lag - 1, pl.ds(first, count), :]
    return total.astype(BF16)


def own_masks(members, lengths_ref, masks):
    for member in range(2):
        base = base_of(lax.axis_index("ctx"), members, member)
        starts = lane_starts(lengths_ref, base, STRETCH)
        for block in range(2):
            offset = row_positions(base, block) - row_starts(starts, block)
            for lag in range(1, TAPS):
                masks[member, lag - 1, pl.ds(block * 128, 128), :] = jnp.where(offset >= lag, 1.0, 0.0)


def payload_kernel(
    members, lengths_ref, feat_hbm, cot_hbm, taps_ref, up_ref, down_ref, feat, cots, masks, rows, feat_sem, cot_sem,
):
    tiles = feat.shape[0]
    copies = []
    for tile in range(tiles):
        lanes = pl.ds(tile * TILE, TILE)
        copies.append((
            pltpu.make_async_copy(feat_hbm.at[:, :, lanes], feat.at[tile], feat_sem.at[tile]),
            pltpu.make_async_copy(cot_hbm.at[:, lanes], cots.at[tile], cot_sem.at[tile]),
        ))
        copies[-1][0].start()
        copies[-1][1].start()
    own_masks(members, lengths_ref, masks)
    rows[pl.ds(0, 8), :] = jnp.zeros((8, TILE), F32)
    for tile in range(tiles):
        lanes = pl.ds(tile * TILE, TILE)
        copies[tile][0].wait()
        copies[tile][1].wait()
        for member in range(2):
            first = member * STRETCH
            tail_ref = up_ref if member == 0 else down_ref
            head_ref = down_ref if member == 0 else up_ref
            rows[pl.ds(8, 144), :] = feat[tile, 0, pl.ds(first, 144), :].astype(F32)
            weights = taps_ref[0, :, lanes]
            for chunk in range(0, 144, 48):
                query = conv_rows(rows, weights, masks, member, chunk, 48).astype(F32)
                cot = cots[tile, pl.ds(first + chunk, 48), :].astype(F32)
                head_ref[pl.ds(TAIL + chunk, 48), lanes] = (cot * query).astype(BF16)
            for stream in (1, 2):
                rows[pl.ds(8 + 112, 144), :] = feat[tile, stream, pl.ds(first + 112, 144), :].astype(F32)
                weights = taps_ref[stream, :, lanes]
                for chunk in range(0, 128, 64):
                    part = conv_rows(rows, weights, masks, member, 128 + chunk, 64)
                    place = pl.ds(chunk, 64)
                    if stream == 2:
                        part = (tail_ref[place, lanes].astype(F32) * part.astype(F32)).astype(BF16)
                    tail_ref[place, lanes] = part
            for stream in range(3):
                tail_ref[pl.ds(128 + stream * EDGE, EDGE), lanes] = feat[
                    tile, stream, pl.ds(first + STRETCH - EDGE, EDGE), :
                ]
                head_ref[pl.ds(TAIL + 144 + stream * EDGE, EDGE), lanes] = feat[
                    tile, stream, pl.ds(first, EDGE), :
                ]
            head_ref[pl.ds(TAIL + 144 + 3 * EDGE, EDGE), lanes] = cots[tile, pl.ds(first, EDGE), :]


def own_kernel(members, lengths_ref, feat_ref, cot_ref, taps_ref, kvg_ref, masks, rows):
    @pl.when(pl.program_id(0) == 0)
    def _():
        own_masks(members, lengths_ref, masks)

    rows[pl.ds(0, 8), :] = jnp.zeros((8, TILE), F32)
    for member in range(2):
        first = member * STRETCH
        for stream in range(3):
            rows[pl.ds(8, STRETCH), :] = feat_ref[stream, pl.ds(first, STRETCH), :].astype(F32)
            weights = taps_ref[stream]
            for chunk in range(0, STRETCH, 64):
                rounded = conv_rows(rows, weights, masks, member, chunk, 64)
                if stream == 0:
                    cot = cot_ref[pl.ds(first + chunk, 64), :].astype(F32)
                    rounded = (cot * rounded.astype(F32)).astype(BF16)
                    kvg_ref[2, pl.ds(first + chunk, 64), :] = rounded
                else:
                    kvg_ref[stream - 1, pl.ds(first + chunk, 64), :] = rounded


def tables_kernel(
    members, lengths_ref, medium_ref,
    forward_ref, backward_ref, keep_f_ref, keep_b_ref, keep_r_ref, shifted_ref, edge_ref,
    forward_rows, backward_rows, offsets, medium, medium_sem,
):
    device = lax.axis_index("ctx")

    @pl.when(pl.program_id(0) == 0)
    def _():
        copy = pltpu.make_async_copy(medium_ref, medium, medium_sem)
        copy.start()
        lag = lax.broadcasted_iota(jnp.int32, (LAGS, 256), 0)
        lane = lax.broadcasted_iota(jnp.int32, (LAGS, 256), 1)
        copy.wait()
        taps = medium[...].astype(BF16)
        dims = (((0,), (0,)), ((), ()))
        place_f = jnp.where(lane == LAGS - lag, 1.0, 0.0).astype(BF16)
        place_b = jnp.where(lane == lag, 1.0, 0.0).astype(BF16)
        forward_rows[...] = lax.dot_general(taps, place_f, dims, preferred_element_type=F32)
        backward_rows[...] = lax.dot_general(taps, place_b, dims, preferred_element_type=F32)
        wide = lax.broadcasted_iota(jnp.int32, (128, 256), 1)
        tall = lax.broadcasted_iota(jnp.int32, (128, 256), 0)
        narrow = lax.broadcasted_iota(jnp.int32, (128, 128), 1)
        for member in range(2):
            base = base_of(device, members, member)
            starts = lane_starts(lengths_ref, base, 512)
            for block in range(3):
                begin = row_starts(starts, block)
                begin = jnp.concatenate([begin, begin], axis=1)
                source = (base + (block - 1) * 128 + wide).astype(F32)
                keep_f_ref[member, block] = jnp.where(source >= begin, 1.0, 0.0).astype(BF16)
                if block < 2:
                    turned = jnp.where(
                        narrow + tall[:, :128] >= 127,
                        base + block * 128 + 127 - narrow, base + (block - 1) * 128 + 127 - narrow,
                    ).astype(F32)
                    keep_r_ref[member, block] = jnp.where(turned >= begin[:, :128], 1.0, 0.0)
                own = (base + block * 128 + tall).astype(F32)
                target = jnp.broadcast_to(starts[0:1, block * 128 : block * 128 + 256], (128, 256))
                keep_b_ref[member, block] = jnp.where(own >= target, 1.0, 0.0).astype(BF16)
                offsets[pl.ds(block * 128, 128), :] = row_positions(base, block) - begin[:, :128]
            for lag in range(1, TAPS):
                shifted_ref[member, lag - 1] = jnp.where(
                    offsets[pl.ds(lag, STRETCH), :] >= lag, 1.0, 0.0
                )
                for side in range(2):
                    edge_ref[member, side, lag - 1] = jnp.where(
                        offsets[pl.ds(side * STRETCH, EDGE), :] >= lag, 1.0, 0.0
                    )

    first = pl.multiple_of(lax.axis_index("tp") * 32 + pl.program_id(0) * PER_TILE, PER_TILE)
    rows_f = forward_rows[pl.ds(first, PER_TILE), :]
    rows_b = backward_rows[pl.ds(first, PER_TILE), :]
    for group in range(PER_TILE):
        for rows, out_ref in ((rows_f, forward_ref), (rows_b, backward_ref)):
            spread = jnp.broadcast_to(rows[group : group + 1, :], (128, 256))
            out_ref[group] = pltpu.roll(spread, 0, 1, stride=1, stride_axis=0).astype(BF16)


def edge_conv(rows, weights, edge_ref, side):
    total = rows[pl.ds(EDGE, EDGE), :] * weights[0:1, :]
    for lag in range(1, TAPS):
        moved = rows[pl.ds(EDGE - lag, EDGE), :] * weights[lag : lag + 1, :]
        total = total + moved * edge_ref[side, lag - 1]
    return total.astype(BF16).astype(F32)


def pair_kernel(
    members, feat_ref, kvg_ref, cot_ref, own_up_ref, up_ref, down_ref, taps_ref, keep_r_ref, edge_ref,
    mixed_ref, grads_ref, kv_ref, sums_ref,
    left, right, rows,
):
    member = pl.program_id(1)
    tile = pl.program_id(0)
    lanes = pl.ds(pl.multiple_of(tile * TILE, TILE), TILE)
    base = member * STRETCH

    def own(first, count):
        return pl.ds(pl.multiple_of(base + first, EDGE), count)

    is_last = lax.axis_index("ctx") == members - 1

    @pl.when(member == 0)
    def _():
        left[...] = up_ref[pl.ds(0, TAIL), lanes]

    @pl.when((member == 1) & is_last)
    def _():
        left[...] = own_up_ref[pl.ds(0, TAIL), lanes]

    @pl.when((member == 1) & jnp.logical_not(is_last))
    def _():
        left[...] = down_ref[pl.ds(0, TAIL), lanes]

    @pl.when(member == 1)
    def _():
        right[...] = up_ref[pl.ds(TAIL, HEAD), lanes]

    @pl.when((member == 0) & is_last)
    def _():
        right[...] = own_up_ref[pl.ds(TAIL, HEAD), lanes]

    @pl.when((member == 0) & jnp.logical_not(is_last))
    def _():
        right[...] = down_ref[pl.ds(TAIL, HEAD), lanes]

    inner = pl.ds(EDGE, STRETCH - EDGE)
    for side in range(2):
        place = pl.ds(side * STRETCH, EDGE)
        if side == 0:
            cot = cot_ref[own(0, EDGE), lanes]
        else:
            cot = right[pl.ds(144 + 3 * EDGE, EDGE), :]
        fixed = []
        for stream in range(3):
            if side == 0:
                before = left[pl.ds(128 + stream * EDGE, EDGE), :]
                after = feat_ref[stream, own(0, EDGE), lanes]
            else:
                before = feat_ref[stream, own(STRETCH - EDGE, EDGE), lanes]
                after = right[pl.ds(144 + stream * EDGE, EDGE), :]
            rows[pl.ds(0, EDGE), :] = before.astype(F32)
            rows[pl.ds(EDGE, EDGE), :] = after.astype(F32)
            fixed.append(edge_conv(rows, taps_ref[stream, :, lanes], edge_ref.at[member], side))
        grads_ref[member, place, lanes] = (cot.astype(F32) * fixed[0]).astype(BF16)
        kv_ref[member, 0, place, lanes] = fixed[1].astype(BF16)
        kv_ref[member, 1, place, lanes] = fixed[2].astype(BF16)
        mixed_ref[member, pl.ds(128 + side * STRETCH, EDGE), lanes] = (fixed[1] * fixed[2]).astype(BF16)
    keys = kvg_ref[0, own(EDGE, STRETCH - EDGE), lanes]
    values = kvg_ref[1, own(EDGE, STRETCH - EDGE), lanes]
    kv_ref[member, 0, inner, lanes] = keys
    kv_ref[member, 1, inner, lanes] = values
    mixed_ref[member, pl.ds(0, 128), lanes] = left[pl.ds(0, 128), :]
    mixed_ref[member, pl.ds(128 + EDGE, STRETCH - EDGE), lanes] = (keys.astype(F32) * values.astype(F32)).astype(BF16)
    mixed_ref[member, pl.ds(400, 112), lanes] = jnp.zeros((112, TILE), BF16)
    grads_ref[member, inner, lanes] = kvg_ref[2, own(EDGE, STRETCH - EDGE), lanes]
    grads_ref[member, pl.ds(STRETCH + EDGE, 128), lanes] = right[pl.ds(EDGE, 128), :]
    grads_ref[member, pl.ds(400, 112), lanes] = jnp.zeros((112, TILE), BF16)

    @pl.when(member == 1)
    def _():
        pair_sums(mixed_ref, grads_ref, keep_r_ref, sums_ref, tile, lanes)


def pair_sums(mixed_ref, grads_ref, keep_r_ref, sums_ref, tile, lanes):
    lane = lax.broadcasted_iota(jnp.int32, (128, TILE), 1)
    row = lax.broadcasted_iota(jnp.int32, (128, TILE), 0)
    lane_group = lane // GROUP
    near = lane + row >= 127
    turn = jnp.where(lane + row == 127, 1.0, 0.0).astype(BF16)
    sources = []
    for member in range(2):
        turned = [
            lax.dot_general(
                mixed_ref[member, pl.ds(piece * 128, 128), lanes], turn, (((0,), (0,)), ((), ())),
                preferred_element_type=F32,
            ).astype(BF16)
            for piece in range(3)
        ]
        for block in range(2):
            sources.append(jnp.concatenate([turned[block + 1], turned[block]], axis=1))
    for group in range(PER_TILE):
        choose = jnp.where(lane_group == group, 1.0, 0.0).astype(BF16)
        total = jnp.zeros((128, TILE), F32)
        for member in range(2):
            for block in range(2):
                chosen = grads_ref[member, pl.ds(block * 128, 128), lanes] * choose
                pair = jnp.dot(chosen, sources[member * 2 + block], preferred_element_type=F32)
                pair = jnp.where(near, pair[:, :128], pair[:, 128:])
                total = total + pair * keep_r_ref[member, block]
        lined_up = pltpu.roll(total, 1, 1, stride=1, stride_axis=0)
        sums_ref[pl.ds(tile * PER_TILE + group, 1), :] = jnp.sum(lined_up, axis=0, keepdims=True)


def conv_kernel(
    members, first_tile, feat_ref, mixed_ref, grads_ref, kv_ref, cot_ref, own_up_ref, up_ref, down_ref,
    taps_ref, skip_ref, forward_ref, backward_ref, keep_f_ref, keep_b_ref, shifted_ref,
    previous_ref, out_ref, sums_ref,
    cots, stack,
):
    del previous_ref
    member = pl.program_id(1)
    tile = first_tile + pl.program_id(0)
    lanes = pl.ds(pl.multiple_of(tile * TILE, TILE), TILE)
    base = member * STRETCH

    def own(first, count):
        return pl.ds(pl.multiple_of(base + first, EDGE), count)

    is_last = lax.axis_index("ctx") == members - 1
    first_group = tile * PER_TILE
    lane_group = lax.broadcasted_iota(jnp.int32, (128, TILE), 1) // GROUP
    skip = skip_ref[:, lanes]
    after = pl.ds(TAIL + 144 + 3 * EDGE, EDGE)
    beyond = pl.ds(STRETCH, EDGE)
    cots[pl.ds(0, STRETCH), :] = cot_ref[own(0, STRETCH), lanes].astype(F32)

    @pl.when(member == 1)
    def _():
        cots[beyond, :] = up_ref[after, lanes].astype(F32)

    @pl.when((member == 0) & is_last)
    def _():
        cots[beyond, :] = own_up_ref[after, lanes].astype(F32)

    @pl.when((member == 0) & jnp.logical_not(is_last))
    def _():
        cots[beyond, :] = down_ref[after, lanes].astype(F32)

    def convolved(table_ref, keep_ref, window, block):
        height = 128 if block < 2 else EDGE
        keep = keep_ref[member, block, pl.ds(0, height), :]
        result = jnp.zeros((height, TILE), F32)
        for group in range(PER_TILE):
            matrix = table_ref[first_group + group, pl.ds(0, height), :] * keep
            product = jnp.dot(matrix, window, preferred_element_type=F32)
            result = jnp.where(lane_group[:height] == group, product, result)
        return result

    for block in range(3):
        height = 128 if block < 2 else EDGE
        place = pl.ds(block * 128, height)
        medium = convolved(forward_ref, keep_f_ref, mixed_ref[member, pl.ds(block * 128, 256), lanes], block)
        medium = medium + skip * mixed_ref[member, pl.ds(block * 128 + 128, height), lanes].astype(F32)
        grad_conv = convolved(backward_ref, keep_b_ref, grads_ref[member, pl.ds(block * 128, 256), lanes], block)
        grad_conv = grad_conv + skip * grads_ref[member, place, lanes].astype(F32)
        for stream in range(3):
            if stream == 0:
                product = cots[place, :] * medium
            else:
                product = grad_conv * kv_ref[member, 2 - stream, place, lanes].astype(F32)
            stack[stream, place, :] = product.astype(BF16).astype(F32)

    @pl.when(member == 0)
    def _():
        sums_ref[...] = jnp.zeros(sums_ref.shape, F32)

    for stream in range(3):
        weights = taps_ref[stream, :, lanes]
        partial = [jnp.zeros((8, TILE), F32) for _ in range(TAPS)]
        for chunk in range(0, STRETCH, 64):
            source = feat_ref[stream, own(chunk, 64), lanes].astype(F32)
            total = jnp.zeros((64, TILE), F32)
            for lag in range(TAPS):
                later = stack[stream, pl.ds(chunk + lag, 64), :]
                if lag > 0:
                    later = later * shifted_ref[member, lag - 1, pl.ds(chunk, 64), :]
                total = total + later * weights[lag : lag + 1, :]
                partial[lag] = partial[lag] + jnp.sum((later * source).reshape(8, 8, TILE), axis=0)
            out_ref[stream, pl.ds(chunk, 64), :] = total.astype(BF16)
        for lag in range(TAPS):
            row = pl.ds(stream * 8 + lag, 1)
            sums_ref[row, :] += jnp.sum(partial[lag], axis=0, keepdims=True)
    bias = jnp.sum(
        grads_ref[member, pl.ds(0, STRETCH), lanes].astype(F32) * mixed_ref[member, pl.ds(128, STRETCH), lanes].astype(F32),
        axis=0, keepdims=True,
    )
    sums_ref[pl.ds(7, 1), :] += bias


def final_kernel(scale, flip, taps_ref, next_taps_ref, sums_ref, other_ref, medium_ref, short_ref, bias_ref):
    half = taps_ref.shape[0]
    upper = (lax.axis_index("tp") // flip) % 2 == 1

    @pl.when(upper)
    def _():
        medium_ref[:, pl.ds(half, half)] = taps_ref[...].T * scale
        medium_ref[:, pl.ds(0, half)] = next_taps_ref[...].T * scale

    @pl.when(jnp.logical_not(upper))
    def _():
        medium_ref[:, pl.ds(0, half)] = taps_ref[...].T * scale
        medium_ref[:, pl.ds(half, half)] = next_taps_ref[...].T * scale

    total = (sums_ref[...] + other_ref[...]) * scale
    for stream in range(3):
        short_ref[stream] = total[stream * 8 : stream * 8 + TAPS]
    bias_ref[...] = total[TAPS : TAPS + 1]


def along(block, axis, route):
    return lax.ppermute(block, axis, route)


def routes_z():
    return [
        [(i, i // 8 * 8 + 7 - i % 8) for i in range(32)],
        [(i, i ^ 1) for i in range(32)],
        [(i, i ^ 2) for i in range(32)],
    ]


def routes_x():
    return [[(i, (3 - i // 8) * 8 + i % 8) for i in range(32)], [(i, i ^ 8) for i in range(32)]]


def shards(features, short_filter, medium_filter, skip_bias, cotangent, doc_lengths):
    members = lax.axis_size("ctx")
    tp = lax.axis_index("tp")
    channels = features.shape[2]
    tiles = channels // TILE
    scale = 1.0 / math.sqrt(2 * STRETCH * members)
    streams = jnp.transpose(features, (1, 0, 2))
    weights = jnp.transpose(short_filter, (1, 0, 2))
    smem = pl.BlockSpec(memory_space=pltpu.SMEM)
    shape = jax.ShapeDtypeStruct
    params = pltpu.CompilerParams(vmem_limit_bytes=16 * 1024 * 1024)

    whole = pl.BlockSpec(memory_space=pltpu.VMEM)
    anywhere = pl.BlockSpec(memory_space=pl.ANY)
    pay_up, pay_down = pl.pallas_call(
        functools.partial(payload_kernel, members),
        in_specs=[smem, anywhere, anywhere, whole],
        out_specs=[whole, whole],
        out_shape=[shape((TAIL + HEAD, channels), BF16), shape((TAIL + HEAD, channels), BF16)],
        scratch_shapes=[
            pltpu.VMEM((tiles, 3, 2 * STRETCH, TILE), BF16),
            pltpu.VMEM((tiles, 2 * STRETCH, TILE), BF16),
            pltpu.VMEM((2, TAPS - 1, STRETCH, TILE), F32),
            pltpu.VMEM((STRETCH + 8, TILE), F32),
            pltpu.SemaphoreType.DMA((tiles,)),
            pltpu.SemaphoreType.DMA((tiles,)),
        ],
        compiler_params=pltpu.CompilerParams(vmem_limit_bytes=56 * 1024 * 1024),
        cost_estimate=pl.CostEstimate(flops=20_000_000, bytes_accessed=2_800_000, transcendentals=0),
        name="payload_rows",
    )(doc_lengths, streams, cotangent, weights)

    got_up = lax.ppermute(pay_up, "ctx", [(i, i + 1) for i in range(members - 1)])
    got_down = lax.ppermute(pay_down, "ctx", [(i + 1, i) for i in range(members - 1)])

    kvg = pl.pallas_call(
        functools.partial(own_kernel, members),
        grid=(tiles,),
        in_specs=[
            smem,
            pl.BlockSpec((3, 2 * STRETCH, TILE), lambda l: (0, 0, l)),
            pl.BlockSpec((2 * STRETCH, TILE), lambda l: (0, l)),
            pl.BlockSpec((3, TAPS, TILE), lambda l: (0, 0, l)),
        ],
        out_specs=pl.BlockSpec((3, 2 * STRETCH, TILE), lambda l: (0, 0, l)),
        out_shape=shape((3, 2 * STRETCH, channels), BF16),
        scratch_shapes=[
            pltpu.VMEM((2, TAPS - 1, STRETCH, TILE), F32),
            pltpu.VMEM((STRETCH + 8, TILE), F32),
        ],
        compiler_params=params,
        cost_estimate=pl.CostEstimate(flops=40_000_000, bytes_accessed=4_500_000, transcendentals=0),
        name="own_rows",
    )(doc_lengths, streams, cotangent, weights)

    groups = channels // GROUP
    tables = pl.pallas_call(
        functools.partial(tables_kernel, members),
        grid=(tiles,),
        in_specs=[smem, anywhere],
        out_specs=[
            pl.BlockSpec((PER_TILE, 128, 256), lambda l: (l, 0, 0)),
            pl.BlockSpec((PER_TILE, 128, 256), lambda l: (l, 0, 0)),
            pl.BlockSpec((2, 3, 128, 256), lambda l: (0, 0, 0, 0)),
            pl.BlockSpec((2, 3, 128, 256), lambda l: (0, 0, 0, 0)),
            pl.BlockSpec((2, 2, 128, 128), lambda l: (0, 0, 0, 0)),
            pl.BlockSpec((2, TAPS - 1, STRETCH, TILE), lambda l: (0, 0, 0, 0)),
            pl.BlockSpec((2, 2, TAPS - 1, EDGE, TILE), lambda l: (0, 0, 0, 0, 0)),
        ],
        out_shape=[
            shape((groups, 128, 256), BF16),
            shape((groups, 128, 256), BF16),
            shape((2, 3, 128, 256), BF16),
            shape((2, 3, 128, 256), BF16),
            shape((2, 2, 128, 128), F32),
            shape((2, TAPS - 1, STRETCH, TILE), F32),
            shape((2, 2, TAPS - 1, EDGE, TILE), F32),
        ],
        scratch_shapes=[
            pltpu.VMEM((256, 256), F32),
            pltpu.VMEM((256, 256), F32),
            pltpu.VMEM((384, TILE), F32),
            pltpu.VMEM(medium_filter.shape, F32),
            pltpu.SemaphoreType.DMA,
        ],
        compiler_params=params,
        cost_estimate=pl.CostEstimate(flops=20_000_000, bytes_accessed=7_000_000, transcendentals=0),
        name="tables",
    )(doc_lengths, medium_filter)

    forward, backward, keep_f, keep_b, keep_r, shifted, edge = tables
    mixed, grads, kv, taps = pl.pallas_call(
        functools.partial(pair_kernel, members),
        grid=(tiles, 2),
        in_specs=[whole] * 9,
        out_specs=[whole] * 4,
        out_shape=[
            shape((2, 512, channels), BF16),
            shape((2, 512, channels), BF16),
            shape((2, 2, STRETCH + EDGE, channels), BF16),
            shape((groups, LAGS), F32),
        ],
        scratch_shapes=[
            pltpu.VMEM((TAIL, TILE), BF16),
            pltpu.VMEM((HEAD, TILE), BF16),
            pltpu.VMEM((2 * EDGE, TILE), F32),
        ],
        compiler_params=params,
        cost_estimate=pl.CostEstimate(flops=500_000_000, bytes_accessed=10_000_000, transcendentals=0),
        name="pair_rows",
    )(streams, kvg, cotangent, pay_up, got_up, got_down, weights, keep_r, edge)

    def convolve(first, count, mixed, grads, previous):
        return pl.pallas_call(
            functools.partial(conv_kernel, members, first),
            grid=(count, 2),
            in_specs=[whole] * 15 + [anywhere],
            out_specs=[
                pl.BlockSpec((3, STRETCH, TILE), lambda l, m: (0, m, first + l)),
                pl.BlockSpec((24, TILE), lambda l, m: (0, l)),
            ],
            out_shape=[
                shape((3, 2 * STRETCH, channels), BF16),
                shape((24, count * TILE), F32),
            ],
            input_output_aliases={15: 0} if first > 0 else {},
            scratch_shapes=[
                pltpu.VMEM((STRETCH + EDGE, TILE), F32),
                pltpu.VMEM((3, STRETCH + EDGE, TILE), F32),
            ],
            compiler_params=params,
            cost_estimate=pl.CostEstimate(flops=count * 100_000_000, bytes_accessed=count * 2_500_000, transcendentals=0),
            name=f"conv_rows_{first}",
        )(
            streams, mixed, grads, kv, cotangent, pay_up, got_up, got_down,
            weights, skip_bias.reshape(1, channels), forward, backward, keep_f, keep_b, shifted, previous,
        )

    parts = []
    grad_streams = kvg
    for route, (first, count) in zip(routes_x() + routes_z()[1:2], ((0, 1), (1, 1), (2, 2))):
        other = along(taps, "ctx", route)
        grad_streams, part = convolve(first, count, mixed, grads, grad_streams)
        taps, mixed, grads, part = lax.optimization_barrier((taps + other, mixed, grads, part))
        parts.append(part)

    sums = jnp.concatenate(parts, axis=1)
    routes = routes_z()[2:] + routes_z()[:2] + routes_x()
    flip = 1
    for step, route in enumerate(routes):
        if step < 2:
            both = jnp.concatenate([sums, taps.reshape(8, channels)], axis=0)
            other = along(both, "ctx", route)
            both = both + other
            sums, taps = both[:24], both[24:].reshape(groups, LAGS)
        else:
            other = along(sums, "ctx", route)
            next_taps = along(taps, "tp", [(i, i ^ flip) for i in range(lax.axis_size("tp"))])
            if step < len(routes) - 1:
                upper = (tp // flip) % 2 == 1
                taps = jnp.concatenate(
                    [jnp.where(upper, next_taps, taps), jnp.where(upper, taps, next_taps)], axis=0
                )
                sums = sums + other
                flip *= 2
        sums, taps = lax.optimization_barrier((sums, taps))
    grad_medium, short, bias = pl.pallas_call(
        functools.partial(final_kernel, scale, flip),
        in_specs=[whole] * 4,
        out_shape=[
            shape(medium_filter.shape, F32), shape((3, TAPS, channels), F32), shape((1, channels), F32),
        ],
        compiler_params=params,
        name="final",
    )(taps, next_taps, sums, other)
    return (
        jnp.transpose(grad_streams, (1, 0, 2)), jnp.transpose(short, (1, 0, 2)), grad_medium,
        bias.reshape(channels),
    )


def solution(mesh):
    in_specs = (P("ctx", None, "tp"), P(None, None, "tp"), P(), P("tp"), P("ctx", "tp"), P())
    out_specs = (P("ctx", None, "tp"), P(None, None, "tp"), P(), P("tp"))
    return jax.shard_map(shards, mesh=mesh, in_specs=in_specs, out_specs=out_specs, check_vma=False)
```

```python
import functools
import math

import jax
import jax.numpy as jnp
from jax import lax
from jax.experimental import pallas as pl
from jax.experimental.pallas import tpu as pltpu
from jax.sharding import PartitionSpec as P

STRETCH = 256
TILE = 128
GROUP = 16
PER_TILE = TILE // GROUP
LAGS = 128
TAPS = 7
EDGE = 16
TAIL = 128 + 2 * EDGE
HEAD = 128 + 2 * EDGE
REACH = TAPS - 1
NEAR = 8
DOCS = 64
F32 = jnp.float32
BF16 = jnp.bfloat16


def base_of(device, members, member):
    first = device * STRETCH
    second = (2 * members - 1 - device) * STRETCH
    if isinstance(member, int):
        return first if member == 0 else second
    return jnp.where(member == 0, first, second)


def lane_starts(lengths_ref, base, count):
    position = base + lax.broadcasted_iota(jnp.int32, (8, count), 1)
    found = jnp.zeros((8, count), jnp.int32)
    running = jnp.int32(0)
    for doc in range(DOCS):
        found = jnp.where(position >= running, running, found)
        running = running + lengths_ref[doc]
    return found.astype(F32)


def row_starts(starts, block):
    row = starts[0:1, block * 128 : (block + 1) * 128]
    return jnp.broadcast_to(row, (128, 128)).T


def row_positions(base, block):
    return (base + block * 128 + lax.broadcasted_iota(jnp.int32, (128, 128), 0)).astype(F32)


def conv_rows(rows, weights, masks, member, first, count):
    total = rows[pl.ds(8 + first, count), :] * weights[0:1, :]
    for lag in range(1, TAPS):
        moved = rows[pl.ds(8 + first - lag, count), :] * weights[lag : lag + 1, :]
        total = total + moved * masks[member, lag - 1, pl.ds(first, count), :]
    return total.astype(BF16)


def own_masks(members, lengths_ref, masks):
    for member in range(2):
        base = base_of(lax.axis_index("ctx"), members, member)
        starts = lane_starts(lengths_ref, base, STRETCH)
        for block in range(2):
            offset = row_positions(base, block) - row_starts(starts, block)
            for lag in range(1, TAPS):
                masks[member, lag - 1, pl.ds(block * 128, 128), :] = jnp.where(offset >= lag, 1.0, 0.0)


def payload_kernel(
    members, lengths_hbm, feat_hbm, cot_hbm, taps_hbm, up_hbm, down_hbm,
    lengths_ref, taps_ref, up_ref, down_ref, feat, cots, masks, rows, grads, sems,
):
    copies = []

    def fetch(source, target):
        copies.append(pltpu.make_async_copy(source, target, sems.at[len(copies)]))
        copies[-1].start()
        return copies[-1]

    def fetch_rows(stream, first, count):
        place = pl.ds(first, count)
        return fetch(feat_hbm.at[stream, place, :], feat.at[stream, place, :])

    fetch(lengths_hbm, lengths_ref)
    fetch(taps_hbm, taps_ref)
    needed = {}
    for member in range(2):
        first = member * STRETCH
        head = pl.ds(first, 144)
        needed[member, "head"] = [fetch_rows(0, first, 144), fetch(cot_hbm.at[head, :], cots.at[head, :])]
    for member in range(2):
        first = member * STRETCH
        needed[member, "tail"] = [fetch_rows(stream, first + 112, 144) for stream in (1, 2)]
    edges = []
    for member in range(2):
        first = member * STRETCH
        edges.append(fetch_rows(0, first + STRETCH - EDGE, EDGE))
        edges += [fetch_rows(stream, first, EDGE) for stream in (1, 2)]

    copies[0].wait()
    own_masks(members, lengths_ref, masks)
    copies[1].wait()
    rows[pl.ds(0, 8), :] = jnp.zeros((8, TILE), F32)
    tiles = [pl.ds(tile * TILE, TILE) for tile in range(up_ref.shape[1] // TILE)]
    for member in range(2):
        head_ref = down_ref if member == 0 else up_ref
        first = member * STRETCH
        for copy in needed[member, "head"]:
            copy.wait()
        for lanes in tiles:
            rows[pl.ds(8, 144), :] = feat[0, pl.ds(first, 144), lanes].astype(F32)
            weights = taps_ref[0, :, lanes]
            for chunk in range(0, 144, 48):
                query = conv_rows(rows, weights, masks, member, chunk, 48).astype(F32)
                cot = cots[pl.ds(first + chunk, 48), lanes].astype(F32)
                grads[pl.ds(chunk, 48), :] = cot * query
            head_ref[pl.ds(TAIL, 128), lanes] = grads[pl.ds(REACH, 128), :].astype(BF16)
    sent = []
    big = pl.ds(TAIL, 128)
    for source, target in ((up_ref, up_hbm), (down_ref, down_hbm)):
        sent.append(fetch(source.at[big, :], target.at[big, :]))
    for member in range(2):
        tail_ref = up_ref if member == 0 else down_ref
        first = member * STRETCH
        for copy in needed[member, "tail"]:
            copy.wait()
        for lanes in tiles:
            for stream in (1, 2):
                rows[pl.ds(8 + 112, 144), :] = feat[stream, pl.ds(first + 112, 144), lanes].astype(F32)
                weights = taps_ref[stream, :, lanes]
                for chunk in range(0, 128, 64):
                    part = conv_rows(rows, weights, masks, member, 128 + chunk, 64)
                    place = pl.ds(chunk, 64)
                    if stream == 2:
                        part = (tail_ref[place, lanes].astype(F32) * part.astype(F32)).astype(BF16)
                    tail_ref[place, lanes] = part
    for copy in edges:
        copy.wait()
    for member in range(2):
        tail_ref = up_ref if member == 0 else down_ref
        head_ref = down_ref if member == 0 else up_ref
        first = member * STRETCH
        last = [feat[stream, pl.ds(first + STRETCH - EDGE, EDGE), :].astype(F32)[NEAR:] for stream in range(3)]
        ahead = [feat[stream, pl.ds(first, EDGE), :].astype(F32)[:NEAR] for stream in range(3)]
        ahead.append(cots[pl.ds(first, EDGE), :].astype(F32)[:NEAR])
        for pair in range(2):
            place = 128 + pair * EDGE
            two = jnp.concatenate([last[2 * pair], last[min(2 * pair + 1, 2)]], axis=0)
            tail_ref[pl.ds(place, EDGE), :] = two.astype(BF16)
            two = jnp.concatenate([ahead[2 * pair], ahead[2 * pair + 1]], axis=0)
            head_ref[pl.ds(TAIL + place, EDGE), :] = two.astype(BF16)
    for source, target in ((up_ref, up_hbm), (down_ref, down_hbm)):
        for part in (pl.ds(0, TAIL), pl.ds(TAIL + 128, 2 * EDGE)):
            sent.append(fetch(source.at[part, :], target.at[part, :]))
    for copy in sent:
        copy.wait()


def own_kernel(members, lengths_ref, feat_ref, cot_ref, taps_ref, kvg_ref, masks, rows):
    @pl.when(pl.program_id(0) == 0)
    def _():
        own_masks(members, lengths_ref, masks)

    rows[pl.ds(0, 8), :] = jnp.zeros((8, TILE), F32)
    for member in range(2):
        first = member * STRETCH
        for stream in range(3):
            rows[pl.ds(8, STRETCH), :] = feat_ref[stream, pl.ds(first, STRETCH), :].astype(F32)
            weights = taps_ref[stream]
            for chunk in range(0, STRETCH, 64):
                rounded = conv_rows(rows, weights, masks, member, chunk, 64)
                if stream == 0:
                    cot = cot_ref[pl.ds(first + chunk, 64), :].astype(F32)
                    rounded = (cot * rounded.astype(F32)).astype(BF16)
                    kvg_ref[2, pl.ds(first + chunk, 64), :] = rounded
                else:
                    kvg_ref[stream - 1, pl.ds(first + chunk, 64), :] = rounded


def tables_kernel(
    members, lengths_ref, medium_ref,
    forward_ref, backward_ref, keep_f_ref, keep_b_ref, keep_r_ref, shifted_ref, edge_ref,
    forward_rows, backward_rows, offsets, medium, medium_sem,
):
    device = lax.axis_index("ctx")

    @pl.when(pl.program_id(0) == 0)
    def _():
        copy = pltpu.make_async_copy(medium_ref, medium, medium_sem)
        copy.start()
        lag = lax.broadcasted_iota(jnp.int32, (LAGS, 256), 0)
        lane = lax.broadcasted_iota(jnp.int32, (LAGS, 256), 1)
        copy.wait()
        taps = medium[...].astype(BF16)
        dims = (((0,), (0,)), ((), ()))
        place_f = jnp.where(lane == LAGS - lag, 1.0, 0.0).astype(BF16)
        place_b = jnp.where(lane == lag, 1.0, 0.0).astype(BF16)
        forward_rows[...] = lax.dot_general(taps, place_f, dims, preferred_element_type=F32)
        backward_rows[...] = lax.dot_general(taps, place_b, dims, preferred_element_type=F32)
        wide = lax.broadcasted_iota(jnp.int32, (128, 256), 1)
        tall = lax.broadcasted_iota(jnp.int32, (128, 256), 0)
        narrow = lax.broadcasted_iota(jnp.int32, (128, 128), 1)
        for member in range(2):
            base = base_of(device, members, member)
            starts = lane_starts(lengths_ref, base, 512)
            for block in range(3):
                begin = row_starts(starts, block)
                begin = jnp.concatenate([begin, begin], axis=1)
                source = (base + (block - 1) * 128 + wide).astype(F32)
                keep_f_ref[member, block] = jnp.where(source >= begin, 1.0, 0.0).astype(BF16)
                if block < 2:
                    turned = jnp.where(
                        narrow + tall[:, :128] >= 127,
                        base + block * 128 + 127 - narrow, base + (block - 1) * 128 + 127 - narrow,
                    ).astype(F32)
                    keep_r_ref[member, block] = jnp.where(turned >= begin[:, :128], 1.0, 0.0)
                own = (base + block * 128 + tall).astype(F32)
                target = jnp.broadcast_to(starts[0:1, block * 128 : block * 128 + 256], (128, 256))
                keep_b_ref[member, block] = jnp.where(own >= target, 1.0, 0.0).astype(BF16)
                offsets[pl.ds(block * 128, 128), :] = row_positions(base, block) - begin[:, :128]
            for lag in range(1, TAPS):
                shifted_ref[member, lag - 1] = jnp.where(
                    offsets[pl.ds(lag, STRETCH), :] >= lag, 1.0, 0.0
                )
                for side in range(2):
                    edge_ref[member, side, lag - 1] = jnp.where(
                        offsets[pl.ds(side * STRETCH, EDGE), :] >= lag, 1.0, 0.0
                    )

    first = pl.multiple_of(lax.axis_index("tp") * 32 + pl.program_id(0) * PER_TILE, PER_TILE)
    rows_f = forward_rows[pl.ds(first, PER_TILE), :]
    rows_b = backward_rows[pl.ds(first, PER_TILE), :]
    for group in range(PER_TILE):
        for rows, out_ref in ((rows_f, forward_ref), (rows_b, backward_ref)):
            spread = jnp.broadcast_to(rows[group : group + 1, :], (128, 256))
            out_ref[group] = pltpu.roll(spread, 0, 1, stride=1, stride_axis=0).astype(BF16)


def edge_conv(rows, weights, edge_ref, side):
    total = rows[pl.ds(NEAR, EDGE), :] * weights[0:1, :]
    for lag in range(1, TAPS):
        moved = rows[pl.ds(NEAR - lag, EDGE), :] * weights[lag : lag + 1, :]
        total = total + moved * edge_ref[side, lag - 1]
    return total.astype(BF16).astype(F32)


def pair_kernel(
    members, feat_ref, kvg_ref, cot_ref, own_up_ref, up_ref, down_ref, taps_ref, keep_r_ref, edge_ref,
    mixed_ref, grads_ref, kv_ref, sums_ref,
    left, right, rows, beyond,
):
    member = pl.program_id(1)
    tile = pl.program_id(0)
    lanes = pl.ds(pl.multiple_of(tile * TILE, TILE), TILE)
    base = member * STRETCH

    def own(first, count):
        return pl.ds(pl.multiple_of(base + first, EDGE), count)

    is_last = lax.axis_index("ctx") == members - 1

    @pl.when(member == 0)
    def _():
        left[...] = up_ref[pl.ds(0, TAIL), lanes]

    @pl.when((member == 1) & is_last)
    def _():
        left[...] = own_up_ref[pl.ds(0, TAIL), lanes]

    @pl.when((member == 1) & jnp.logical_not(is_last))
    def _():
        left[...] = down_ref[pl.ds(0, TAIL), lanes]

    @pl.when(member == 1)
    def _():
        right[...] = up_ref[pl.ds(TAIL, HEAD), lanes]

    @pl.when((member == 0) & is_last)
    def _():
        right[...] = own_up_ref[pl.ds(TAIL, HEAD), lanes]

    @pl.when((member == 0) & jnp.logical_not(is_last))
    def _():
        right[...] = down_ref[pl.ds(TAIL, HEAD), lanes]

    inner = pl.ds(EDGE, STRETCH - EDGE)
    for side in range(2):
        place = pl.ds(side * STRETCH, EDGE)
        if side == 0:
            cot = cot_ref[own(0, EDGE), lanes].astype(F32)
        else:
            cot = right[pl.ds(144, EDGE), :].astype(F32)[NEAR:]
        fixed = []
        for stream in range(3):
            place_two, half = pl.ds(128 + stream // 2 * EDGE, EDGE), stream % 2 * NEAR
            if side == 0:
                rows[pl.ds(0, NEAR), :] = left[place_two, :].astype(F32)[half : half + NEAR]
                rows[pl.ds(NEAR, EDGE), :] = feat_ref[stream, own(0, EDGE), lanes].astype(F32)
            else:
                rows[pl.ds(0, NEAR), :] = feat_ref[stream, own(STRETCH - EDGE, EDGE), lanes].astype(F32)[NEAR:]
                rows[pl.ds(NEAR, NEAR), :] = right[place_two, :].astype(F32)[half : half + NEAR]
                rows[pl.ds(EDGE, NEAR), :] = jnp.zeros((NEAR, TILE), F32)
            fixed.append(edge_conv(rows, taps_ref[stream, :, lanes], edge_ref.at[member], side))
        if side == 0:
            grads_ref[member, place, lanes] = (cot * fixed[0]).astype(BF16)
        else:
            beyond[pl.ds(0, NEAR), :] = cot * fixed[0][:NEAR]
            beyond[pl.ds(REACH, 128), :] = right[pl.ds(0, 128), :].astype(F32)
            beyond[pl.ds(REACH + 128, 144 - REACH - 128), :] = jnp.zeros((144 - REACH - 128, TILE), F32)
            grads_ref[member, pl.ds(STRETCH, 144), lanes] = beyond[...].astype(BF16)
        kv_ref[member, 0, place, lanes] = fixed[1].astype(BF16)
        kv_ref[member, 1, place, lanes] = fixed[2].astype(BF16)
        mixed_ref[member, pl.ds(128 + side * STRETCH, EDGE), lanes] = (fixed[1] * fixed[2]).astype(BF16)
    keys = kvg_ref[0, own(EDGE, STRETCH - EDGE), lanes]
    values = kvg_ref[1, own(EDGE, STRETCH - EDGE), lanes]
    kv_ref[member, 0, inner, lanes] = keys
    kv_ref[member, 1, inner, lanes] = values
    mixed_ref[member, pl.ds(0, 128), lanes] = left[pl.ds(0, 128), :]
    mixed_ref[member, pl.ds(128 + EDGE, STRETCH - EDGE), lanes] = (keys.astype(F32) * values.astype(F32)).astype(BF16)
    mixed_ref[member, pl.ds(400, 112), lanes] = jnp.zeros((112, TILE), BF16)
    grads_ref[member, inner, lanes] = kvg_ref[2, own(EDGE, STRETCH - EDGE), lanes]
    grads_ref[member, pl.ds(400, 112), lanes] = jnp.zeros((112, TILE), BF16)

    @pl.when(member == 1)
    def _():
        pair_sums(mixed_ref, grads_ref, keep_r_ref, sums_ref, tile, lanes)


def pair_sums(mixed_ref, grads_ref, keep_r_ref, sums_ref, tile, lanes):
    lane = lax.broadcasted_iota(jnp.int32, (128, TILE), 1)
    row = lax.broadcasted_iota(jnp.int32, (128, TILE), 0)
    lane_group = lane // GROUP
    near = lane + row >= 127
    turn = jnp.where(lane + row == 127, 1.0, 0.0).astype(BF16)
    sources = []
    for member in range(2):
        turned = [
            lax.dot_general(
                mixed_ref[member, pl.ds(piece * 128, 128), lanes], turn, (((0,), (0,)), ((), ())),
                preferred_element_type=F32,
            ).astype(BF16)
            for piece in range(3)
        ]
        for block in range(2):
            sources.append(jnp.concatenate([turned[block + 1], turned[block]], axis=1))
    for group in range(PER_TILE):
        choose = jnp.where(lane_group == group, 1.0, 0.0).astype(BF16)
        total = jnp.zeros((128, TILE), F32)
        for member in range(2):
            for block in range(2):
                chosen = grads_ref[member, pl.ds(block * 128, 128), lanes] * choose
                pair = jnp.dot(chosen, sources[member * 2 + block], preferred_element_type=F32)
                pair = jnp.where(near, pair[:, :128], pair[:, 128:])
                total = total + pair * keep_r_ref[member, block]
        lined_up = pltpu.roll(total, 1, 1, stride=1, stride_axis=0)
        sums_ref[pl.ds(tile * PER_TILE + group, 1), :] = jnp.sum(lined_up, axis=0, keepdims=True)


def conv_kernel(
    members, first_tile, feat_ref, mixed_ref, grads_ref, kv_ref, cot_ref, own_up_ref, up_ref, down_ref,
    taps_ref, skip_ref, forward_ref, backward_ref, keep_f_ref, keep_b_ref, shifted_ref,
    previous_ref, out_ref, sums_ref,
    cots, stack,
):
    del previous_ref
    member = pl.program_id(1)
    tile = first_tile + pl.program_id(0)
    lanes = pl.ds(pl.multiple_of(tile * TILE, TILE), TILE)
    base = member * STRETCH

    def own(first, count):
        return pl.ds(pl.multiple_of(base + first, EDGE), count)

    is_last = lax.axis_index("ctx") == members - 1
    first_group = tile * PER_TILE
    lane_group = lax.broadcasted_iota(jnp.int32, (128, TILE), 1) // GROUP
    skip = skip_ref[:, lanes]
    after = pl.ds(TAIL + 144, EDGE)
    beyond = pl.ds(STRETCH, NEAR)
    cots[pl.ds(STRETCH + NEAR, NEAR), :] = jnp.zeros((NEAR, TILE), F32)
    cots[pl.ds(0, STRETCH), :] = cot_ref[own(0, STRETCH), lanes].astype(F32)

    @pl.when(member == 1)
    def _():
        cots[beyond, :] = up_ref[after, lanes].astype(F32)[NEAR:]

    @pl.when((member == 0) & is_last)
    def _():
        cots[beyond, :] = own_up_ref[after, lanes].astype(F32)[NEAR:]

    @pl.when((member == 0) & jnp.logical_not(is_last))
    def _():
        cots[beyond, :] = down_ref[after, lanes].astype(F32)[NEAR:]

    def convolved(table_ref, keep_ref, window, block):
        height = 128 if block < 2 else EDGE
        keep = keep_ref[member, block, pl.ds(0, height), :]
        matrix = table_ref[pl.ds(first_group, PER_TILE), pl.ds(0, height), :] * keep[None]
        product = jnp.dot(matrix.reshape(PER_TILE * height, 256), window, preferred_element_type=F32)
        result = product[:height]
        for group in range(1, PER_TILE):
            result = jnp.where(lane_group[:height] == group, product[group * height : (group + 1) * height], result)
        return result

    for block in range(3):
        height = 128 if block < 2 else EDGE
        place = pl.ds(block * 128, height)
        medium = convolved(forward_ref, keep_f_ref, mixed_ref[member, pl.ds(block * 128, 256), lanes], block)
        medium = medium + skip * mixed_ref[member, pl.ds(block * 128 + 128, height), lanes].astype(F32)
        grad_conv = convolved(backward_ref, keep_b_ref, grads_ref[member, pl.ds(block * 128, 256), lanes], block)
        grad_conv = grad_conv + skip * grads_ref[member, place, lanes].astype(F32)
        for stream in range(3):
            if stream == 0:
                product = cots[place, :] * medium
            else:
                product = grad_conv * kv_ref[member, 2 - stream, place, lanes].astype(F32)
            stack[stream, place, :] = product.astype(BF16).astype(F32)

    @pl.when(member == 0)
    def _():
        sums_ref[...] = jnp.zeros(sums_ref.shape, F32)

    for stream in range(3):
        weights = taps_ref[stream, :, lanes]
        partial = [jnp.zeros((8, TILE), F32) for _ in range(TAPS)]
        for chunk in range(0, STRETCH, 64):
            source = feat_ref[stream, own(chunk, 64), lanes].astype(F32)
            total = jnp.zeros((64, TILE), F32)
            for lag in range(TAPS):
                later = stack[stream, pl.ds(chunk + lag, 64), :]
                if lag > 0:
                    later = later * shifted_ref[member, lag - 1, pl.ds(chunk, 64), :]
                total = total + later * weights[lag : lag + 1, :]
                partial[lag] = partial[lag] + jnp.sum((later * source).reshape(8, 8, TILE), axis=0)
            out_ref[stream, pl.ds(chunk, 64), :] = total.astype(BF16)
        for lag in range(TAPS):
            row = pl.ds(stream * 8 + lag, 1)
            sums_ref[row, :] += jnp.sum(partial[lag], axis=0, keepdims=True)
    bias = jnp.sum(
        grads_ref[member, pl.ds(0, STRETCH), lanes].astype(F32) * mixed_ref[member, pl.ds(128, STRETCH), lanes].astype(F32),
        axis=0, keepdims=True,
    )
    sums_ref[pl.ds(7, 1), :] += bias


def final_kernel(scale, flip, taps_ref, next_taps_ref, sums_ref, other_ref, medium_ref, short_ref, bias_ref):
    half = taps_ref.shape[0]
    upper = (lax.axis_index("tp") // flip) % 2 == 1

    @pl.when(upper)
    def _():
        medium_ref[:, pl.ds(half, half)] = taps_ref[...].T * scale
        medium_ref[:, pl.ds(0, half)] = next_taps_ref[...].T * scale

    @pl.when(jnp.logical_not(upper))
    def _():
        medium_ref[:, pl.ds(0, half)] = taps_ref[...].T * scale
        medium_ref[:, pl.ds(half, half)] = next_taps_ref[...].T * scale

    total = (sums_ref[...] + other_ref[...]) * scale
    for stream in range(3):
        short_ref[stream] = total[stream * 8 : stream * 8 + TAPS]
    bias_ref[...] = total[TAPS : TAPS + 1]


def along(block, axis, route):
    return lax.ppermute(block, axis, route)


def routes_z():
    return [
        [(i, i // 8 * 8 + 7 - i % 8) for i in range(32)],
        [(i, i ^ 1) for i in range(32)],
        [(i, i ^ 2) for i in range(32)],
    ]


def routes_x():
    return [[(i, (3 - i // 8) * 8 + i % 8) for i in range(32)], [(i, i ^ 8) for i in range(32)]]


def shards(features, short_filter, medium_filter, skip_bias, cotangent, doc_lengths):
    members = lax.axis_size("ctx")
    tp = lax.axis_index("tp")
    channels = features.shape[2]
    tiles = channels // TILE
    scale = 1.0 / math.sqrt(2 * STRETCH * members)
    streams = jnp.transpose(features, (1, 0, 2))
    weights = jnp.transpose(short_filter, (1, 0, 2))
    smem = pl.BlockSpec(memory_space=pltpu.SMEM)
    shape = jax.ShapeDtypeStruct
    params = pltpu.CompilerParams(vmem_limit_bytes=16 * 1024 * 1024)

    whole = pl.BlockSpec(memory_space=pltpu.VMEM)
    anywhere = pl.BlockSpec(memory_space=pl.ANY)
    pay_up, pay_down = pl.pallas_call(
        functools.partial(payload_kernel, members),
        in_specs=[anywhere] * 4,
        out_specs=[anywhere] * 2,
        out_shape=[shape((TAIL + HEAD, channels), BF16), shape((TAIL + HEAD, channels), BF16)],
        scratch_shapes=[
            pltpu.SMEM((DOCS,), jnp.int32),
            pltpu.VMEM((3, TAPS, channels), F32),
            pltpu.VMEM((TAIL + HEAD, channels), BF16),
            pltpu.VMEM((TAIL + HEAD, channels), BF16),
            pltpu.VMEM((3, 2 * STRETCH, channels), BF16),
            pltpu.VMEM((2 * STRETCH, channels), BF16),
            pltpu.VMEM((2, TAPS - 1, STRETCH, TILE), F32),
            pltpu.VMEM((STRETCH + 8, TILE), F32),
            pltpu.VMEM((144, TILE), F32),
            pltpu.SemaphoreType.DMA((22,)),
        ],
        compiler_params=pltpu.CompilerParams(vmem_limit_bytes=56 * 1024 * 1024),
        cost_estimate=pl.CostEstimate(flops=20_000_000, bytes_accessed=2_800_000, transcendentals=0),
        name="payload_rows",
    )(doc_lengths, streams, cotangent, weights)

    got_up = lax.ppermute(pay_up, "ctx", [(i, i + 1) for i in range(members - 1)])
    got_down = lax.ppermute(pay_down, "ctx", [(i + 1, i) for i in range(members - 1)])

    kvg = pl.pallas_call(
        functools.partial(own_kernel, members),
        grid=(tiles,),
        in_specs=[
            smem,
            pl.BlockSpec((3, 2 * STRETCH, TILE), lambda l: (0, 0, l)),
            pl.BlockSpec((2 * STRETCH, TILE), lambda l: (0, l)),
            pl.BlockSpec((3, TAPS, TILE), lambda l: (0, 0, l)),
        ],
        out_specs=pl.BlockSpec((3, 2 * STRETCH, TILE), lambda l: (0, 0, l)),
        out_shape=shape((3, 2 * STRETCH, channels), BF16),
        scratch_shapes=[
            pltpu.VMEM((2, TAPS - 1, STRETCH, TILE), F32),
            pltpu.VMEM((STRETCH + 8, TILE), F32),
        ],
        compiler_params=params,
        cost_estimate=pl.CostEstimate(flops=40_000_000, bytes_accessed=4_500_000, transcendentals=0),
        name="own_rows",
    )(doc_lengths, streams, cotangent, weights)

    groups = channels // GROUP
    tables = pl.pallas_call(
        functools.partial(tables_kernel, members),
        grid=(tiles,),
        in_specs=[smem, anywhere],
        out_specs=[
            pl.BlockSpec((PER_TILE, 128, 256), lambda l: (l, 0, 0)),
            pl.BlockSpec((PER_TILE, 128, 256), lambda l: (l, 0, 0)),
            pl.BlockSpec((2, 3, 128, 256), lambda l: (0, 0, 0, 0)),
            pl.BlockSpec((2, 3, 128, 256), lambda l: (0, 0, 0, 0)),
            pl.BlockSpec((2, 2, 128, 128), lambda l: (0, 0, 0, 0)),
            pl.BlockSpec((2, TAPS - 1, STRETCH, TILE), lambda l: (0, 0, 0, 0)),
            pl.BlockSpec((2, 2, TAPS - 1, EDGE, TILE), lambda l: (0, 0, 0, 0, 0)),
        ],
        out_shape=[
            shape((groups, 128, 256), BF16),
            shape((groups, 128, 256), BF16),
            shape((2, 3, 128, 256), BF16),
            shape((2, 3, 128, 256), BF16),
            shape((2, 2, 128, 128), F32),
            shape((2, TAPS - 1, STRETCH, TILE), F32),
            shape((2, 2, TAPS - 1, EDGE, TILE), F32),
        ],
        scratch_shapes=[
            pltpu.VMEM((256, 256), F32),
            pltpu.VMEM((256, 256), F32),
            pltpu.VMEM((384, TILE), F32),
            pltpu.VMEM(medium_filter.shape, F32),
            pltpu.SemaphoreType.DMA,
        ],
        compiler_params=params,
        cost_estimate=pl.CostEstimate(flops=20_000_000, bytes_accessed=7_000_000, transcendentals=0),
        name="tables",
    )(doc_lengths, medium_filter)

    forward, backward, keep_f, keep_b, keep_r, shifted, edge = tables
    mixed, grads, kv, taps = pl.pallas_call(
        functools.partial(pair_kernel, members),
        grid=(tiles, 2),
        in_specs=[whole] * 9,
        out_specs=[whole] * 4,
        out_shape=[
            shape((2, 512, channels), BF16),
            shape((2, 512, channels), BF16),
            shape((2, 2, STRETCH + EDGE, channels), BF16),
            shape((groups, LAGS), F32),
        ],
        scratch_shapes=[
            pltpu.VMEM((TAIL, TILE), BF16),
            pltpu.VMEM((HEAD, TILE), BF16),
            pltpu.VMEM((NEAR + EDGE, TILE), F32),
            pltpu.VMEM((144, TILE), F32),
        ],
        compiler_params=params,
        cost_estimate=pl.CostEstimate(flops=500_000_000, bytes_accessed=10_000_000, transcendentals=0),
        name="pair_rows",
    )(streams, kvg, cotangent, pay_up, got_up, got_down, weights, keep_r, edge)

    def convolve(first, count, mixed, grads, previous):
        return pl.pallas_call(
            functools.partial(conv_kernel, members, first),
            grid=(count, 2),
            in_specs=[whole] * 15 + [anywhere],
            out_specs=[
                pl.BlockSpec((3, STRETCH, TILE), lambda l, m: (0, m, first + l)),
                pl.BlockSpec((24, TILE), lambda l, m: (0, l)),
            ],
            out_shape=[
                shape((3, 2 * STRETCH, channels), BF16),
                shape((24, count * TILE), F32),
            ],
            input_output_aliases={15: 0} if first > 0 else {},
            scratch_shapes=[
                pltpu.VMEM((STRETCH + EDGE, TILE), F32),
                pltpu.VMEM((3, STRETCH + EDGE, TILE), F32),
            ],
            compiler_params=params,
            cost_estimate=pl.CostEstimate(flops=count * 100_000_000, bytes_accessed=count * 2_500_000, transcendentals=0),
            name=f"conv_rows_{first}",
        )(
            streams, mixed, grads, kv, cotangent, pay_up, got_up, got_down,
            weights, skip_bias.reshape(1, channels), forward, backward, keep_f, keep_b, shifted, previous,
        )

    parts = []
    grad_streams = kvg
    for route, (first, count) in zip(routes_x() + routes_z()[1:2], ((0, 1), (1, 1), (2, 2))):
        other = along(taps, "ctx", route)
        grad_streams, part = convolve(first, count, mixed, grads, grad_streams)
        taps, mixed, grads, part = lax.optimization_barrier((taps + other, mixed, grads, part))
        parts.append(part)

    sums = jnp.concatenate(parts, axis=1)
    routes = routes_z()[2:] + routes_z()[:2] + routes_x()
    flip = 1
    for step, route in enumerate(routes):
        if step < 2:
            both = jnp.concatenate([sums, taps.reshape(8, channels)], axis=0)
            other = along(both, "ctx", route)
            both = both + other
            sums, taps = both[:24], both[24:].reshape(groups, LAGS)
        else:
            other = along(sums, "ctx", route)
            next_taps = along(taps, "tp", [(i, i ^ flip) for i in range(lax.axis_size("tp"))])
            if step < len(routes) - 1:
                upper = (tp // flip) % 2 == 1
                taps = jnp.concatenate(
                    [jnp.where(upper, next_taps, taps), jnp.where(upper, taps, next_taps)], axis=0
                )
                sums = sums + other
                flip *= 2
        sums, taps = lax.optimization_barrier((sums, taps))
    grad_medium, short, bias = pl.pallas_call(
        functools.partial(final_kernel, scale, flip),
        in_specs=[whole] * 4,
        out_shape=[
            shape(medium_filter.shape, F32), shape((3, TAPS, channels), F32), shape((1, channels), F32),
        ],
        compiler_params=params,
        name="final",
    )(taps, next_taps, sums, other)
    return (
        jnp.transpose(grad_streams, (1, 0, 2)), jnp.transpose(short, (1, 0, 2)), grad_medium,
        bias.reshape(channels),
    )


def solution(mesh):
    in_specs = (P("ctx", None, "tp"), P(None, None, "tp"), P(), P("tp"), P("ctx", "tp"), P())
    out_specs = (P("ctx", None, "tp"), P(None, None, "tp"), P(), P("tp"))
    return jax.shard_map(shards, mesh=mesh, in_specs=in_specs, out_specs=out_specs, check_vma=False)
```

```python
import functools
import math

import jax
import jax.numpy as jnp
from jax import lax
from jax.experimental import pallas as pl
from jax.experimental.pallas import tpu as pltpu
from jax.sharding import PartitionSpec as P

STRETCH = 256
TILE = 128
GROUP = 16
PER_TILE = TILE // GROUP
LAGS = 128
TAPS = 7
EDGE = 16
TAIL = 128 + 2 * EDGE
HEAD = 128 + 2 * EDGE
REACH = TAPS - 1
NEAR = 8
DOCS = 64
F32 = jnp.float32
BF16 = jnp.bfloat16


def base_of(device, members, member):
    first = device * STRETCH
    second = (2 * members - 1 - device) * STRETCH
    if isinstance(member, int):
        return first if member == 0 else second
    return jnp.where(member == 0, first, second)


def lane_starts(lengths_ref, base, count):
    position = base + lax.broadcasted_iota(jnp.int32, (8, count), 1)
    found = jnp.zeros((8, count), jnp.int32)
    running = jnp.int32(0)
    for doc in range(DOCS):
        found = jnp.where(position >= running, running, found)
        running = running + lengths_ref[doc]
    return found.astype(F32)


def row_starts(starts, block):
    row = starts[0:1, block * 128 : (block + 1) * 128]
    return jnp.broadcast_to(row, (128, 128)).T


def row_positions(base, block):
    return (base + block * 128 + lax.broadcasted_iota(jnp.int32, (128, 128), 0)).astype(F32)


def conv_rows(rows, weights, masks, member, first, count):
    total = rows[pl.ds(8 + first, count), :] * weights[0:1, :]
    for lag in range(1, TAPS):
        moved = rows[pl.ds(8 + first - lag, count), :] * weights[lag : lag + 1, :]
        total = total + moved * masks[member, lag - 1, pl.ds(first, count), :]
    return total.astype(BF16)


def own_masks(members, lengths_ref, masks):
    for member in range(2):
        base = base_of(lax.axis_index("ctx"), members, member)
        starts = lane_starts(lengths_ref, base, STRETCH)
        for block in range(2):
            offset = row_positions(base, block) - row_starts(starts, block)
            for lag in range(1, TAPS):
                masks[member, lag - 1, pl.ds(block * 128, 128), :] = jnp.where(offset >= lag, 1.0, 0.0)


def payload_kernel(
    members, lengths_hbm, feat_hbm, cot_hbm, taps_hbm, up_hbm, down_hbm,
    lengths_ref, taps_ref, up_ref, down_ref, feat, cots, masks, rows, grads, sems,
):
    copies = []

    def fetch(source, target):
        copies.append(pltpu.make_async_copy(source, target, sems.at[len(copies)]))
        copies[-1].start()
        return copies[-1]

    def fetch_rows(stream, first, count):
        place = pl.ds(first, count)
        return fetch(feat_hbm.at[stream, place, :], feat.at[stream, place, :])

    fetch(lengths_hbm, lengths_ref)
    fetch(taps_hbm, taps_ref)
    needed = {}
    for member in range(2):
        first = member * STRETCH
        head = pl.ds(first, 144)
        needed[member, "head"] = [fetch_rows(0, first, 144), fetch(cot_hbm.at[head, :], cots.at[head, :])]
    for member in range(2):
        first = member * STRETCH
        needed[member, "tail"] = [fetch_rows(stream, first + 112, 144) for stream in (1, 2)]
    edges = []
    for member in range(2):
        first = member * STRETCH
        edges.append(fetch_rows(0, first + STRETCH - EDGE, EDGE))
        edges += [fetch_rows(stream, first, EDGE) for stream in (1, 2)]

    copies[0].wait()
    own_masks(members, lengths_ref, masks)
    copies[1].wait()
    rows[pl.ds(0, 8), :] = jnp.zeros((8, TILE), F32)
    tiles = [pl.ds(tile * TILE, TILE) for tile in range(up_ref.shape[1] // TILE)]
    for member in range(2):
        head_ref = down_ref if member == 0 else up_ref
        first = member * STRETCH
        for copy in needed[member, "head"]:
            copy.wait()
        for lanes in tiles:
            rows[pl.ds(8, 144), :] = feat[0, pl.ds(first, 144), lanes].astype(F32)
            weights = taps_ref[0, :, lanes]
            for chunk in range(0, 144, 48):
                query = conv_rows(rows, weights, masks, member, chunk, 48).astype(F32)
                cot = cots[pl.ds(first + chunk, 48), lanes].astype(F32)
                grads[pl.ds(chunk, 48), :] = cot * query
            head_ref[pl.ds(TAIL, 128), lanes] = grads[pl.ds(REACH, 128), :].astype(BF16)
    sent = []
    big = pl.ds(TAIL, 128)
    for source, target in ((up_ref, up_hbm), (down_ref, down_hbm)):
        sent.append(fetch(source.at[big, :], target.at[big, :]))
    for member in range(2):
        tail_ref = up_ref if member == 0 else down_ref
        first = member * STRETCH
        for copy in needed[member, "tail"]:
            copy.wait()
        for lanes in tiles:
            for stream in (1, 2):
                rows[pl.ds(8 + 112, 144), :] = feat[stream, pl.ds(first + 112, 144), lanes].astype(F32)
                weights = taps_ref[stream, :, lanes]
                for chunk in range(0, 128, 64):
                    part = conv_rows(rows, weights, masks, member, 128 + chunk, 64)
                    place = pl.ds(chunk, 64)
                    if stream == 2:
                        part = (tail_ref[place, lanes].astype(F32) * part.astype(F32)).astype(BF16)
                    tail_ref[place, lanes] = part
    for copy in edges:
        copy.wait()
    for member in range(2):
        tail_ref = up_ref if member == 0 else down_ref
        head_ref = down_ref if member == 0 else up_ref
        first = member * STRETCH
        last = [feat[stream, pl.ds(first + STRETCH - EDGE, EDGE), :].astype(F32)[NEAR:] for stream in range(3)]
        ahead = [feat[stream, pl.ds(first, EDGE), :].astype(F32)[:NEAR] for stream in range(3)]
        ahead.append(cots[pl.ds(first, EDGE), :].astype(F32)[:NEAR])
        for pair in range(2):
            place = 128 + pair * EDGE
            two = jnp.concatenate([last[2 * pair], last[min(2 * pair + 1, 2)]], axis=0)
            tail_ref[pl.ds(place, EDGE), :] = two.astype(BF16)
            two = jnp.concatenate([ahead[2 * pair], ahead[2 * pair + 1]], axis=0)
            head_ref[pl.ds(TAIL + place, EDGE), :] = two.astype(BF16)
    for source, target in ((up_ref, up_hbm), (down_ref, down_hbm)):
        for part in (pl.ds(0, TAIL), pl.ds(TAIL + 128, 2 * EDGE)):
            sent.append(fetch(source.at[part, :], target.at[part, :]))
    for copy in sent:
        copy.wait()


def own_kernel(members, lengths_ref, feat_ref, cot_ref, taps_ref, kvg_ref, masks, rows):
    @pl.when(pl.program_id(0) == 0)
    def _():
        own_masks(members, lengths_ref, masks)

    rows[pl.ds(0, 8), :] = jnp.zeros((8, TILE), F32)
    for member in range(2):
        first = member * STRETCH
        for stream in range(3):
            rows[pl.ds(8, STRETCH), :] = feat_ref[stream, pl.ds(first, STRETCH), :].astype(F32)
            weights = taps_ref[stream]
            for chunk in range(0, STRETCH, 64):
                rounded = conv_rows(rows, weights, masks, member, chunk, 64)
                if stream == 0:
                    cot = cot_ref[pl.ds(first + chunk, 64), :].astype(F32)
                    rounded = (cot * rounded.astype(F32)).astype(BF16)
                    kvg_ref[2, pl.ds(first + chunk, 64), :] = rounded
                else:
                    kvg_ref[stream - 1, pl.ds(first + chunk, 64), :] = rounded


def tables_kernel(
    members, lengths_ref, medium_ref,
    forward_ref, backward_ref, keep_f_ref, keep_b_ref, keep_r_ref, shifted_ref, edge_ref,
    forward_rows, backward_rows, offsets, medium, medium_sem,
):
    device = lax.axis_index("ctx")

    @pl.when(pl.program_id(0) == 0)
    def _():
        copy = pltpu.make_async_copy(medium_ref, medium, medium_sem)
        copy.start()
        lag = lax.broadcasted_iota(jnp.int32, (LAGS, 256), 0)
        lane = lax.broadcasted_iota(jnp.int32, (LAGS, 256), 1)
        copy.wait()
        taps = medium[...].astype(BF16)
        dims = (((0,), (0,)), ((), ()))
        place_f = jnp.where(lane == LAGS - lag, 1.0, 0.0).astype(BF16)
        place_b = jnp.where(lane == lag, 1.0, 0.0).astype(BF16)
        forward_rows[...] = lax.dot_general(taps, place_f, dims, preferred_element_type=F32)
        backward_rows[...] = lax.dot_general(taps, place_b, dims, preferred_element_type=F32)
        wide = lax.broadcasted_iota(jnp.int32, (128, 256), 1)
        tall = lax.broadcasted_iota(jnp.int32, (128, 256), 0)
        narrow = lax.broadcasted_iota(jnp.int32, (128, 128), 1)
        for member in range(2):
            base = base_of(device, members, member)
            starts = lane_starts(lengths_ref, base, 512)
            for block in range(3):
                begin = row_starts(starts, block)
                begin = jnp.concatenate([begin, begin], axis=1)
                source = (base + (block - 1) * 128 + wide).astype(F32)
                keep_f_ref[member, block] = jnp.where(source >= begin, 1.0, 0.0).astype(BF16)
                if block < 2:
                    turned = jnp.where(
                        narrow + tall[:, :128] >= 127,
                        base + block * 128 + 127 - narrow, base + (block - 1) * 128 + 127 - narrow,
                    ).astype(F32)
                    keep_r_ref[member, block] = jnp.where(turned >= begin[:, :128], 1.0, 0.0)
                own = (base + block * 128 + tall).astype(F32)
                target = jnp.broadcast_to(starts[0:1, block * 128 : block * 128 + 256], (128, 256))
                keep_b_ref[member, block] = jnp.where(own >= target, 1.0, 0.0).astype(BF16)
                offsets[pl.ds(block * 128, 128), :] = row_positions(base, block) - begin[:, :128]
            for lag in range(1, TAPS):
                shifted_ref[member, lag - 1] = jnp.where(
                    offsets[pl.ds(lag, STRETCH), :] >= lag, 1.0, 0.0
                )
                for side in range(2):
                    edge_ref[member, side, lag - 1] = jnp.where(
                        offsets[pl.ds(side * STRETCH, EDGE), :] >= lag, 1.0, 0.0
                    )

    first = pl.multiple_of(lax.axis_index("tp") * 32 + pl.program_id(0) * PER_TILE, PER_TILE)
    rows_f = forward_rows[pl.ds(first, PER_TILE), :]
    rows_b = backward_rows[pl.ds(first, PER_TILE), :]
    for group in range(PER_TILE):
        for rows, out_ref in ((rows_f, forward_ref), (rows_b, backward_ref)):
            spread = jnp.broadcast_to(rows[group : group + 1, :], (128, 256))
            out_ref[group] = pltpu.roll(spread, 0, 1, stride=1, stride_axis=0).astype(BF16)


def edge_conv(rows, weights, edge_ref, side):
    total = rows[pl.ds(NEAR, EDGE), :] * weights[0:1, :]
    for lag in range(1, TAPS):
        moved = rows[pl.ds(NEAR - lag, EDGE), :] * weights[lag : lag + 1, :]
        total = total + moved * edge_ref[side, lag - 1]
    return total.astype(BF16).astype(F32)


def pair_kernel(
    members, feat_ref, kvg_ref, cot_ref, own_up_ref, up_ref, down_ref, taps_ref, keep_r_ref, edge_ref,
    mixed_ref, grads_ref, kv_ref, sums_ref,
    left, right, rows, beyond,
):
    member = pl.program_id(1)
    tile = pl.program_id(0)
    lanes = pl.ds(pl.multiple_of(tile * TILE, TILE), TILE)
    base = member * STRETCH

    def own(first, count):
        return pl.ds(pl.multiple_of(base + first, EDGE), count)

    is_last = lax.axis_index("ctx") == members - 1

    @pl.when(member == 0)
    def _():
        left[...] = up_ref[pl.ds(0, TAIL), lanes]

    @pl.when((member == 1) & is_last)
    def _():
        left[...] = own_up_ref[pl.ds(0, TAIL), lanes]

    @pl.when((member == 1) & jnp.logical_not(is_last))
    def _():
        left[...] = down_ref[pl.ds(0, TAIL), lanes]

    @pl.when(member == 1)
    def _():
        right[...] = up_ref[pl.ds(TAIL, HEAD), lanes]

    @pl.when((member == 0) & is_last)
    def _():
        right[...] = own_up_ref[pl.ds(TAIL, HEAD), lanes]

    @pl.when((member == 0) & jnp.logical_not(is_last))
    def _():
        right[...] = down_ref[pl.ds(TAIL, HEAD), lanes]

    inner = pl.ds(EDGE, STRETCH - EDGE)
    for side in range(2):
        place = pl.ds(side * STRETCH, EDGE)
        if side == 0:
            cot = cot_ref[own(0, EDGE), lanes].astype(F32)
        else:
            cot = right[pl.ds(144, EDGE), :].astype(F32)[NEAR:]
        fixed = []
        for stream in range(3):
            place_two, half = pl.ds(128 + stream // 2 * EDGE, EDGE), stream % 2 * NEAR
            if side == 0:
                rows[pl.ds(0, NEAR), :] = left[place_two, :].astype(F32)[half : half + NEAR]
                rows[pl.ds(NEAR, EDGE), :] = feat_ref[stream, own(0, EDGE), lanes].astype(F32)
            else:
                rows[pl.ds(0, NEAR), :] = feat_ref[stream, own(STRETCH - EDGE, EDGE), lanes].astype(F32)[NEAR:]
                rows[pl.ds(NEAR, NEAR), :] = right[place_two, :].astype(F32)[half : half + NEAR]
                rows[pl.ds(EDGE, NEAR), :] = jnp.zeros((NEAR, TILE), F32)
            fixed.append(edge_conv(rows, taps_ref[stream, :, lanes], edge_ref.at[member], side))
        if side == 0:
            grads_ref[member, place, lanes] = (cot * fixed[0]).astype(BF16)
        else:
            beyond[pl.ds(0, NEAR), :] = cot * fixed[0][:NEAR]
            beyond[pl.ds(REACH, 128), :] = right[pl.ds(0, 128), :].astype(F32)
            beyond[pl.ds(REACH + 128, 144 - REACH - 128), :] = jnp.zeros((144 - REACH - 128, TILE), F32)
            grads_ref[member, pl.ds(STRETCH, 144), lanes] = beyond[...].astype(BF16)
        kv_ref[member, 0, place, lanes] = fixed[1].astype(BF16)
        kv_ref[member, 1, place, lanes] = fixed[2].astype(BF16)
        mixed_ref[member, pl.ds(128 + side * STRETCH, EDGE), lanes] = (fixed[1] * fixed[2]).astype(BF16)
    keys = kvg_ref[0, own(EDGE, STRETCH - EDGE), lanes]
    values = kvg_ref[1, own(EDGE, STRETCH - EDGE), lanes]
    kv_ref[member, 0, inner, lanes] = keys
    kv_ref[member, 1, inner, lanes] = values
    mixed_ref[member, pl.ds(0, 128), lanes] = left[pl.ds(0, 128), :]
    mixed_ref[member, pl.ds(128 + EDGE, STRETCH - EDGE), lanes] = (keys.astype(F32) * values.astype(F32)).astype(BF16)
    mixed_ref[member, pl.ds(400, 112), lanes] = jnp.zeros((112, TILE), BF16)
    grads_ref[member, inner, lanes] = kvg_ref[2, own(EDGE, STRETCH - EDGE), lanes]
    grads_ref[member, pl.ds(400, 112), lanes] = jnp.zeros((112, TILE), BF16)

    @pl.when(member == 1)
    def _():
        pair_sums(mixed_ref, grads_ref, keep_r_ref, sums_ref, tile, lanes)


def pair_sums(mixed_ref, grads_ref, keep_r_ref, sums_ref, tile, lanes):
    lane = lax.broadcasted_iota(jnp.int32, (128, TILE), 1)
    row = lax.broadcasted_iota(jnp.int32, (128, TILE), 0)
    lane_group = lane // GROUP
    near = lane + row >= 127
    turn = jnp.where(lane + row == 127, 1.0, 0.0).astype(BF16)
    sources = []
    for member in range(2):
        turned = [
            lax.dot_general(
                mixed_ref[member, pl.ds(piece * 128, 128), lanes], turn, (((0,), (0,)), ((), ())),
                preferred_element_type=F32,
            ).astype(BF16)
            for piece in range(3)
        ]
        for block in range(2):
            sources.append(jnp.concatenate([turned[block + 1], turned[block]], axis=1))
    for group in range(PER_TILE):
        choose = jnp.where(lane_group == group, 1.0, 0.0).astype(BF16)
        total = jnp.zeros((128, TILE), F32)
        for member in range(2):
            for block in range(2):
                chosen = grads_ref[member, pl.ds(block * 128, 128), lanes] * choose
                pair = jnp.dot(chosen, sources[member * 2 + block], preferred_element_type=F32)
                pair = jnp.where(near, pair[:, :128], pair[:, 128:])
                total = total + pair * keep_r_ref[member, block]
        lined_up = pltpu.roll(total, 1, 1, stride=1, stride_axis=0)
        sums_ref[pl.ds(tile * PER_TILE + group, 1), :] = jnp.sum(lined_up, axis=0, keepdims=True)


def conv_kernel(
    members, first_tile, feat_ref, mixed_ref, grads_ref, kv_ref, cot_ref, own_up_ref, up_ref, down_ref,
    taps_ref, skip_ref, forward_ref, backward_ref, keep_f_ref, keep_b_ref, shifted_ref,
    stack_ref, sums_ref,
    cots, stack,
):
    member = pl.program_id(1)
    tile = first_tile + pl.program_id(0)
    lanes = pl.ds(pl.multiple_of(tile * TILE, TILE), TILE)
    base = member * STRETCH

    def own(first, count):
        return pl.ds(pl.multiple_of(base + first, EDGE), count)

    is_last = lax.axis_index("ctx") == members - 1
    first_group = tile * PER_TILE
    lane_group = lax.broadcasted_iota(jnp.int32, (128, TILE), 1) // GROUP
    skip = skip_ref[:, lanes]
    after = pl.ds(TAIL + 144, EDGE)
    beyond = pl.ds(STRETCH, NEAR)
    cots[pl.ds(STRETCH + NEAR, NEAR), :] = jnp.zeros((NEAR, TILE), F32)
    cots[pl.ds(0, STRETCH), :] = cot_ref[own(0, STRETCH), lanes].astype(F32)

    @pl.when(member == 1)
    def _():
        cots[beyond, :] = up_ref[after, lanes].astype(F32)[NEAR:]

    @pl.when((member == 0) & is_last)
    def _():
        cots[beyond, :] = own_up_ref[after, lanes].astype(F32)[NEAR:]

    @pl.when((member == 0) & jnp.logical_not(is_last))
    def _():
        cots[beyond, :] = down_ref[after, lanes].astype(F32)[NEAR:]

    def convolved(table_ref, keep_ref, window, block):
        height = 128 if block < 2 else EDGE
        keep = keep_ref[member, block, pl.ds(0, height), :]
        matrix = table_ref[pl.ds(first_group, PER_TILE), pl.ds(0, height), :] * keep[None]
        product = jnp.dot(matrix.reshape(PER_TILE * height, 256), window, preferred_element_type=F32)
        result = product[:height]
        for group in range(1, PER_TILE):
            result = jnp.where(lane_group[:height] == group, product[group * height : (group + 1) * height], result)
        return result

    for block in range(3):
        height = 128 if block < 2 else EDGE
        place = pl.ds(block * 128, height)
        medium = convolved(forward_ref, keep_f_ref, mixed_ref[member, pl.ds(block * 128, 256), lanes], block)
        medium = medium + skip * mixed_ref[member, pl.ds(block * 128 + 128, height), lanes].astype(F32)
        grad_conv = convolved(backward_ref, keep_b_ref, grads_ref[member, pl.ds(block * 128, 256), lanes], block)
        grad_conv = grad_conv + skip * grads_ref[member, place, lanes].astype(F32)
        for stream in range(3):
            if stream == 0:
                product = cots[place, :] * medium
            else:
                product = grad_conv * kv_ref[member, 2 - stream, place, lanes].astype(F32)
            product = product.astype(BF16)
            stack[stream, place, :] = product.astype(F32)
            stack_ref[member, stream, place, pl.ds(pl.multiple_of(pl.program_id(0) * TILE, TILE), TILE)] = product

    @pl.when(member == 0)
    def _():
        sums_ref[...] = jnp.zeros(sums_ref.shape, F32)

    for stream in range(3):
        partial = [jnp.zeros((8, TILE), F32) for _ in range(TAPS)]
        for chunk in range(0, STRETCH, 64):
            source = feat_ref[stream, own(chunk, 64), lanes].astype(F32)
            for lag in range(TAPS):
                later = stack[stream, pl.ds(chunk + lag, 64), :] * source
                if lag > 0:
                    later = later * shifted_ref[member, lag - 1, pl.ds(chunk, 64), :]
                partial[lag] = partial[lag] + jnp.sum(later.reshape(8, 8, TILE), axis=0)
        for lag in range(TAPS):
            row = pl.ds(stream * 8 + lag, 1)
            sums_ref[row, :] += jnp.sum(partial[lag], axis=0, keepdims=True)
    bias = jnp.sum(
        grads_ref[member, pl.ds(0, STRETCH), lanes].astype(F32) * mixed_ref[member, pl.ds(128, STRETCH), lanes].astype(F32),
        axis=0, keepdims=True,
    )
    sums_ref[pl.ds(7, 1), :] += bias


def adjoint_kernel(pieces, *refs):
    stack_refs, (taps_ref, shifted_ref, previous_ref, out_ref, stack) = refs[:pieces], refs[pieces:]
    del previous_ref
    tile, member = pl.program_id(0), pl.program_id(1)
    if pieces == 1:
        stack[...] = stack_refs[0][member, :, :, pl.ds(pl.multiple_of(tile * TILE, TILE), TILE)].astype(F32)
    for piece in range(pieces if pieces > 1 else 0):
        @pl.when(tile == piece)
        def _():
            stack[...] = stack_refs[piece][member].astype(F32)
    for stream in range(3):
        weights = taps_ref[stream]
        for chunk in range(0, STRETCH, 64):
            total = stack[stream, pl.ds(chunk, 64), :] * weights[0:1, :]
            for lag in range(1, TAPS):
                later = stack[stream, pl.ds(chunk + lag, 64), :] * shifted_ref[member, lag - 1, pl.ds(chunk, 64), :]
                total = total + later * weights[lag : lag + 1, :]
            out_ref[stream, pl.ds(chunk, 64), :] = total.astype(BF16)


def final_kernel(scale, flip, taps_ref, next_taps_ref, sums_ref, other_ref, medium_ref, short_ref, bias_ref):
    half = taps_ref.shape[0]
    upper = (lax.axis_index("tp") // flip) % 2 == 1

    @pl.when(upper)
    def _():
        medium_ref[:, pl.ds(half, half)] = taps_ref[...].T * scale
        medium_ref[:, pl.ds(0, half)] = next_taps_ref[...].T * scale

    @pl.when(jnp.logical_not(upper))
    def _():
        medium_ref[:, pl.ds(0, half)] = taps_ref[...].T * scale
        medium_ref[:, pl.ds(half, half)] = next_taps_ref[...].T * scale

    total = (sums_ref[...] + other_ref[...]) * scale
    for stream in range(3):
        short_ref[stream] = total[stream * 8 : stream * 8 + TAPS]
    bias_ref[...] = total[TAPS : TAPS + 1]


def along(block, axis, route):
    return lax.ppermute(block, axis, route)


def routes_z():
    return [
        [(i, i // 8 * 8 + 7 - i % 8) for i in range(32)],
        [(i, i ^ 1) for i in range(32)],
        [(i, i ^ 2) for i in range(32)],
    ]


def routes_x():
    return [[(i, (3 - i // 8) * 8 + i % 8) for i in range(32)], [(i, i ^ 8) for i in range(32)]]


def shards(features, short_filter, medium_filter, skip_bias, cotangent, doc_lengths):
    members = lax.axis_size("ctx")
    tp = lax.axis_index("tp")
    channels = features.shape[2]
    tiles = channels // TILE
    scale = 1.0 / math.sqrt(2 * STRETCH * members)
    streams = jnp.transpose(features, (1, 0, 2))
    weights = jnp.transpose(short_filter, (1, 0, 2))
    smem = pl.BlockSpec(memory_space=pltpu.SMEM)
    shape = jax.ShapeDtypeStruct
    params = pltpu.CompilerParams(vmem_limit_bytes=16 * 1024 * 1024)

    whole = pl.BlockSpec(memory_space=pltpu.VMEM)
    anywhere = pl.BlockSpec(memory_space=pl.ANY)
    pay_up, pay_down = pl.pallas_call(
        functools.partial(payload_kernel, members),
        in_specs=[anywhere] * 4,
        out_specs=[anywhere] * 2,
        out_shape=[shape((TAIL + HEAD, channels), BF16), shape((TAIL + HEAD, channels), BF16)],
        scratch_shapes=[
            pltpu.SMEM((DOCS,), jnp.int32),
            pltpu.VMEM((3, TAPS, channels), F32),
            pltpu.VMEM((TAIL + HEAD, channels), BF16),
            pltpu.VMEM((TAIL + HEAD, channels), BF16),
            pltpu.VMEM((3, 2 * STRETCH, channels), BF16),
            pltpu.VMEM((2 * STRETCH, channels), BF16),
            pltpu.VMEM((2, TAPS - 1, STRETCH, TILE), F32),
            pltpu.VMEM((STRETCH + 8, TILE), F32),
            pltpu.VMEM((144, TILE), F32),
            pltpu.SemaphoreType.DMA((22,)),
        ],
        compiler_params=pltpu.CompilerParams(vmem_limit_bytes=56 * 1024 * 1024),
        cost_estimate=pl.CostEstimate(flops=20_000_000, bytes_accessed=2_800_000, transcendentals=0),
        name="payload_rows",
    )(doc_lengths, streams, cotangent, weights)

    got_up = lax.ppermute(pay_up, "ctx", [(i, i + 1) for i in range(members - 1)])
    got_down = lax.ppermute(pay_down, "ctx", [(i + 1, i) for i in range(members - 1)])

    kvg = pl.pallas_call(
        functools.partial(own_kernel, members),
        grid=(tiles,),
        in_specs=[
            smem,
            pl.BlockSpec((3, 2 * STRETCH, TILE), lambda l: (0, 0, l)),
            pl.BlockSpec((2 * STRETCH, TILE), lambda l: (0, l)),
            pl.BlockSpec((3, TAPS, TILE), lambda l: (0, 0, l)),
        ],
        out_specs=pl.BlockSpec((3, 2 * STRETCH, TILE), lambda l: (0, 0, l)),
        out_shape=shape((3, 2 * STRETCH, channels), BF16),
        scratch_shapes=[
            pltpu.VMEM((2, TAPS - 1, STRETCH, TILE), F32),
            pltpu.VMEM((STRETCH + 8, TILE), F32),
        ],
        compiler_params=params,
        cost_estimate=pl.CostEstimate(flops=40_000_000, bytes_accessed=4_500_000, transcendentals=0),
        name="own_rows",
    )(doc_lengths, streams, cotangent, weights)

    groups = channels // GROUP
    tables = pl.pallas_call(
        functools.partial(tables_kernel, members),
        grid=(tiles,),
        in_specs=[smem, anywhere],
        out_specs=[
            pl.BlockSpec((PER_TILE, 128, 256), lambda l: (l, 0, 0)),
            pl.BlockSpec((PER_TILE, 128, 256), lambda l: (l, 0, 0)),
            pl.BlockSpec((2, 3, 128, 256), lambda l: (0, 0, 0, 0)),
            pl.BlockSpec((2, 3, 128, 256), lambda l: (0, 0, 0, 0)),
            pl.BlockSpec((2, 2, 128, 128), lambda l: (0, 0, 0, 0)),
            pl.BlockSpec((2, TAPS - 1, STRETCH, TILE), lambda l: (0, 0, 0, 0)),
            pl.BlockSpec((2, 2, TAPS - 1, EDGE, TILE), lambda l: (0, 0, 0, 0, 0)),
        ],
        out_shape=[
            shape((groups, 128, 256), BF16),
            shape((groups, 128, 256), BF16),
            shape((2, 3, 128, 256), BF16),
            shape((2, 3, 128, 256), BF16),
            shape((2, 2, 128, 128), F32),
            shape((2, TAPS - 1, STRETCH, TILE), F32),
            shape((2, 2, TAPS - 1, EDGE, TILE), F32),
        ],
        scratch_shapes=[
            pltpu.VMEM((256, 256), F32),
            pltpu.VMEM((256, 256), F32),
            pltpu.VMEM((384, TILE), F32),
            pltpu.VMEM(medium_filter.shape, F32),
            pltpu.SemaphoreType.DMA,
        ],
        compiler_params=params,
        cost_estimate=pl.CostEstimate(flops=20_000_000, bytes_accessed=7_000_000, transcendentals=0),
        name="tables",
    )(doc_lengths, medium_filter)

    forward, backward, keep_f, keep_b, keep_r, shifted, edge = tables
    mixed, grads, kv, taps = pl.pallas_call(
        functools.partial(pair_kernel, members),
        grid=(tiles, 2),
        in_specs=[whole] * 9,
        out_specs=[whole] * 4,
        out_shape=[
            shape((2, 512, channels), BF16),
            shape((2, 512, channels), BF16),
            shape((2, 2, STRETCH + EDGE, channels), BF16),
            shape((groups, LAGS), F32),
        ],
        scratch_shapes=[
            pltpu.VMEM((TAIL, TILE), BF16),
            pltpu.VMEM((HEAD, TILE), BF16),
            pltpu.VMEM((NEAR + EDGE, TILE), F32),
            pltpu.VMEM((144, TILE), F32),
        ],
        compiler_params=params,
        cost_estimate=pl.CostEstimate(flops=500_000_000, bytes_accessed=10_000_000, transcendentals=0),
        name="pair_rows",
    )(streams, kvg, cotangent, pay_up, got_up, got_down, weights, keep_r, edge)

    def convolve(first, count, mixed, grads):
        return pl.pallas_call(
            functools.partial(conv_kernel, members, first),
            grid=(count, 2),
            in_specs=[whole] * 15,
            out_specs=[
                whole,
                pl.BlockSpec((24, TILE), lambda l, m: (0, l)),
            ],
            out_shape=[
                shape((2, 3, STRETCH + EDGE, count * TILE), BF16),
                shape((24, count * TILE), F32),
            ],
            scratch_shapes=[
                pltpu.VMEM((STRETCH + EDGE, TILE), F32),
                pltpu.VMEM((3, STRETCH + EDGE, TILE), F32),
            ],
            compiler_params=params,
            cost_estimate=pl.CostEstimate(flops=count * 100_000_000, bytes_accessed=count * 2_500_000, transcendentals=0),
            name=f"conv_rows_{first}",
        )(
            streams, mixed, grads, kv, cotangent, pay_up, got_up, got_down,
            weights, skip_bias.reshape(1, channels), forward, backward, keep_f, keep_b, shifted,
        )

    parts, stacks = [], []
    for route, (first, count) in zip(routes_x() + routes_z()[1:2], ((0, 1), (1, 1), (2, 2))):
        other = along(taps, "ctx", route)
        stack, part = convolve(first, count, mixed, grads)
        stacks.append(stack)
        taps, mixed, grads, part = lax.optimization_barrier((taps + other, mixed, grads, part))
        parts.append(part)

    def adjoint(first, pieces, previous):
        return pl.pallas_call(
            functools.partial(adjoint_kernel, len(pieces)),
            grid=(2, 2),
            in_specs=[whole] * len(pieces) + [
                pl.BlockSpec((3, TAPS, TILE), lambda l, m: (0, 0, first + l)), whole, anywhere,
            ],
            out_specs=pl.BlockSpec((3, STRETCH, TILE), lambda l, m: (0, m, first + l)),
            out_shape=shape((3, 2 * STRETCH, channels), BF16),
            input_output_aliases={len(pieces) + 2: 0} if first > 0 else {},
            scratch_shapes=[pltpu.VMEM((3, STRETCH + EDGE, TILE), F32)],
            compiler_params=params,
            cost_estimate=pl.CostEstimate(flops=20_000_000, bytes_accessed=4_000_000, transcendentals=0),
            name=f"adjoint_rows_{first}",
        )(*pieces, weights, shifted, previous)

    sums = jnp.concatenate(parts, axis=1)
    grad_streams = kvg
    routes = routes_z()[2:] + routes_z()[:2] + routes_x()
    flip = 1
    for step, route in enumerate(routes):
        if step < 2:
            both = jnp.concatenate([sums, taps.reshape(8, channels)], axis=0)
            other = along(both, "ctx", route)
            both = both + other
            sums, taps = both[:24], both[24:].reshape(groups, LAGS)
        else:
            other = along(sums, "ctx", route)
            next_taps = along(taps, "tp", [(i, i ^ flip) for i in range(lax.axis_size("tp"))])
            if step < len(routes) - 1:
                upper = (tp // flip) % 2 == 1
                taps = jnp.concatenate(
                    [jnp.where(upper, next_taps, taps), jnp.where(upper, taps, next_taps)], axis=0
                )
                sums = sums + other
                flip *= 2
        if step < 2:
            grad_streams = adjoint(2 * step, stacks[2 * step : 2 * step + 2], grad_streams)
        sums, taps, grad_streams = lax.optimization_barrier((sums, taps, grad_streams))
    grad_medium, short, bias = pl.pallas_call(
        functools.partial(final_kernel, scale, flip),
        in_specs=[whole] * 4,
        out_shape=[
            shape(medium_filter.shape, F32), shape((3, TAPS, channels), F32), shape((1, channels), F32),
        ],
        compiler_params=params,
        name="final",
    )(taps, next_taps, sums, other)
    return (
        jnp.transpose(grad_streams, (1, 0, 2)), jnp.transpose(short, (1, 0, 2)), grad_medium,
        bias.reshape(channels),
    )


def solution(mesh):
    in_specs = (P("ctx", None, "tp"), P(None, None, "tp"), P(), P("tp"), P("ctx", "tp"), P())
    out_specs = (P("ctx", None, "tp"), P(None, None, "tp"), P(), P("tp"))
    return jax.shard_map(shards, mesh=mesh, in_specs=in_specs, out_specs=out_specs, check_vma=False)
```

```python
import functools
import math

import jax
import jax.numpy as jnp
from jax import lax
from jax.experimental import pallas as pl
from jax.experimental.pallas import tpu as pltpu
from jax.sharding import PartitionSpec as P

STRETCH = 256
TILE = 128
GROUP = 16
PER_TILE = TILE // GROUP
LAGS = 128
TAPS = 7
EDGE = 16
TAIL = 128 + 2 * EDGE
HEAD = 128 + 2 * EDGE
REACH = TAPS - 1
NEAR = 8
DOCS = 64
F32 = jnp.float32
BF16 = jnp.bfloat16


def base_of(device, members, member):
    first = device * STRETCH
    second = (2 * members - 1 - device) * STRETCH
    if isinstance(member, int):
        return first if member == 0 else second
    return jnp.where(member == 0, first, second)


def lane_starts(lengths_ref, base, count):
    position = base + lax.broadcasted_iota(jnp.int32, (8, count), 1)
    found = jnp.zeros((8, count), jnp.int32)
    running = jnp.int32(0)
    for doc in range(DOCS):
        found = jnp.where(position >= running, running, found)
        running = running + lengths_ref[doc]
    return found.astype(F32)


def row_starts(starts, block):
    row = starts[0:1, block * 128 : (block + 1) * 128]
    return jnp.broadcast_to(row, (128, 128)).T


def row_positions(base, block):
    return (base + block * 128 + lax.broadcasted_iota(jnp.int32, (128, 128), 0)).astype(F32)


def conv_rows(rows, weights, masks, member, first, count):
    total = rows[pl.ds(8 + first, count), :] * weights[0:1, :]
    for lag in range(1, TAPS):
        moved = rows[pl.ds(8 + first - lag, count), :] * weights[lag : lag + 1, :]
        total = total + moved * masks[member, lag - 1, pl.ds(first, count), :]
    return total.astype(BF16)


def own_masks(members, lengths_ref, masks):
    for member in range(2):
        base = base_of(lax.axis_index("ctx"), members, member)
        starts = lane_starts(lengths_ref, base, STRETCH)
        for block in range(2):
            offset = row_positions(base, block) - row_starts(starts, block)
            for lag in range(1, TAPS):
                masks[member, lag - 1, pl.ds(block * 128, 128), :] = jnp.where(offset >= lag, 1.0, 0.0)


def payload_kernel(
    members, lengths_hbm, feat_hbm, cot_hbm, taps_hbm, up_hbm, down_hbm,
    lengths_ref, taps_ref, up_ref, down_ref, feat, cots, masks, rows, grads, sems,
):
    copies = []

    def fetch(source, target):
        copies.append(pltpu.make_async_copy(source, target, sems.at[len(copies)]))
        copies[-1].start()
        return copies[-1]

    def fetch_rows(stream, first, count):
        place = pl.ds(first, count)
        return fetch(feat_hbm.at[stream, place, :], feat.at[stream, place, :])

    fetch(lengths_hbm, lengths_ref)
    fetch(taps_hbm, taps_ref)
    needed = {}
    for member in range(2):
        first = member * STRETCH
        head = pl.ds(first, 144)
        needed[member, "head"] = [fetch_rows(0, first, 144), fetch(cot_hbm.at[head, :], cots.at[head, :])]
    for member in range(2):
        first = member * STRETCH
        needed[member, "tail"] = [fetch_rows(stream, first + 112, 144) for stream in (1, 2)]
    edges = []
    for member in range(2):
        first = member * STRETCH
        edges.append(fetch_rows(0, first + STRETCH - EDGE, EDGE))
        edges += [fetch_rows(stream, first, EDGE) for stream in (1, 2)]

    copies[0].wait()
    own_masks(members, lengths_ref, masks)
    copies[1].wait()
    rows[pl.ds(0, 8), :] = jnp.zeros((8, TILE), F32)
    tiles = [pl.ds(tile * TILE, TILE) for tile in range(up_ref.shape[1] // TILE)]
    for member in range(2):
        head_ref = down_ref if member == 0 else up_ref
        first = member * STRETCH
        for copy in needed[member, "head"]:
            copy.wait()
        for lanes in tiles:
            rows[pl.ds(8, 144), :] = feat[0, pl.ds(first, 144), lanes].astype(F32)
            weights = taps_ref[0, :, lanes]
            for chunk in range(0, 144, 48):
                query = conv_rows(rows, weights, masks, member, chunk, 48).astype(F32)
                cot = cots[pl.ds(first + chunk, 48), lanes].astype(F32)
                grads[pl.ds(chunk, 48), :] = cot * query
            head_ref[pl.ds(TAIL, 128), lanes] = grads[pl.ds(REACH, 128), :].astype(BF16)
    sent = []
    big = pl.ds(TAIL, 128)
    for source, target in ((up_ref, up_hbm), (down_ref, down_hbm)):
        sent.append(fetch(source.at[big, :], target.at[big, :]))
    for member in range(2):
        tail_ref = up_ref if member == 0 else down_ref
        first = member * STRETCH
        for copy in needed[member, "tail"]:
            copy.wait()
        for lanes in tiles:
            for stream in (1, 2):
                rows[pl.ds(8 + 112, 144), :] = feat[stream, pl.ds(first + 112, 144), lanes].astype(F32)
                weights = taps_ref[stream, :, lanes]
                for chunk in range(0, 128, 64):
                    part = conv_rows(rows, weights, masks, member, 128 + chunk, 64)
                    place = pl.ds(chunk, 64)
                    if stream == 2:
                        part = (tail_ref[place, lanes].astype(F32) * part.astype(F32)).astype(BF16)
                    tail_ref[place, lanes] = part
    for copy in edges:
        copy.wait()
    for member in range(2):
        tail_ref = up_ref if member == 0 else down_ref
        head_ref = down_ref if member == 0 else up_ref
        first = member * STRETCH
        last = [feat[stream, pl.ds(first + STRETCH - EDGE, EDGE), :].astype(F32)[NEAR:] for stream in range(3)]
        ahead = [feat[stream, pl.ds(first, EDGE), :].astype(F32)[:NEAR] for stream in range(3)]
        ahead.append(cots[pl.ds(first, EDGE), :].astype(F32)[:NEAR])
        for pair in range(2):
            place = 128 + pair * EDGE
            two = jnp.concatenate([last[2 * pair], last[min(2 * pair + 1, 2)]], axis=0)
            tail_ref[pl.ds(place, EDGE), :] = two.astype(BF16)
            two = jnp.concatenate([ahead[2 * pair], ahead[2 * pair + 1]], axis=0)
            head_ref[pl.ds(TAIL + place, EDGE), :] = two.astype(BF16)
    for source, target in ((up_ref, up_hbm), (down_ref, down_hbm)):
        for part in (pl.ds(0, TAIL), pl.ds(TAIL + 128, 2 * EDGE)):
            sent.append(fetch(source.at[part, :], target.at[part, :]))
    for copy in sent:
        copy.wait()


def own_kernel(members, lengths_ref, feat_ref, cot_ref, taps_ref, kvg_ref, masks, rows):
    @pl.when(pl.program_id(0) == 0)
    def _():
        own_masks(members, lengths_ref, masks)

    rows[pl.ds(0, 8), :] = jnp.zeros((8, TILE), F32)
    for member in range(2):
        first = member * STRETCH
        for stream in range(3):
            rows[pl.ds(8, STRETCH), :] = feat_ref[stream, pl.ds(first, STRETCH), :].astype(F32)
            weights = taps_ref[stream]
            for chunk in range(0, STRETCH, 64):
                rounded = conv_rows(rows, weights, masks, member, chunk, 64)
                if stream == 0:
                    cot = cot_ref[pl.ds(first + chunk, 64), :].astype(F32)
                    rounded = (cot * rounded.astype(F32)).astype(BF16)
                    kvg_ref[2, pl.ds(first + chunk, 64), :] = rounded
                else:
                    kvg_ref[stream - 1, pl.ds(first + chunk, 64), :] = rounded


def tables_kernel(
    members, lengths_ref, medium_ref,
    forward_ref, backward_ref, keep_f_ref, keep_b_ref, keep_r_ref, shifted_ref, edge_ref,
    forward_rows, backward_rows, offsets, medium, medium_sem,
):
    device = lax.axis_index("ctx")

    @pl.when(pl.program_id(0) == 0)
    def _():
        copy = pltpu.make_async_copy(medium_ref, medium, medium_sem)
        copy.start()
        lag = lax.broadcasted_iota(jnp.int32, (LAGS, 256), 0)
        lane = lax.broadcasted_iota(jnp.int32, (LAGS, 256), 1)
        copy.wait()
        taps = medium[...].astype(BF16)
        dims = (((0,), (0,)), ((), ()))
        place_f = jnp.where(lane == LAGS - lag, 1.0, 0.0).astype(BF16)
        place_b = jnp.where(lane == lag, 1.0, 0.0).astype(BF16)
        forward_rows[...] = lax.dot_general(taps, place_f, dims, preferred_element_type=F32)
        backward_rows[...] = lax.dot_general(taps, place_b, dims, preferred_element_type=F32)
        wide = lax.broadcasted_iota(jnp.int32, (128, 256), 1)
        tall = lax.broadcasted_iota(jnp.int32, (128, 256), 0)
        narrow = lax.broadcasted_iota(jnp.int32, (128, 128), 1)
        for member in range(2):
            base = base_of(device, members, member)
            starts = lane_starts(lengths_ref, base, 512)
            for block in range(3):
                begin = row_starts(starts, block)
                begin = jnp.concatenate([begin, begin], axis=1)
                source = (base + (block - 1) * 128 + wide).astype(F32)
                keep_f_ref[member, block] = jnp.where(source >= begin, 1.0, 0.0).astype(BF16)
                if block < 2:
                    turned = jnp.where(
                        narrow + tall[:, :128] >= 127,
                        base + block * 128 + 127 - narrow, base + (block - 1) * 128 + 127 - narrow,
                    ).astype(F32)
                    keep_r_ref[member, block] = jnp.where(turned >= begin[:, :128], 1.0, 0.0)
                own = (base + block * 128 + tall).astype(F32)
                target = jnp.broadcast_to(starts[0:1, block * 128 : block * 128 + 256], (128, 256))
                keep_b_ref[member, block] = jnp.where(own >= target, 1.0, 0.0).astype(BF16)
                offsets[pl.ds(block * 128, 128), :] = row_positions(base, block) - begin[:, :128]
            for lag in range(1, TAPS):
                shifted_ref[member, lag - 1] = jnp.where(
                    offsets[pl.ds(lag, STRETCH), :] >= lag, 1.0, 0.0
                )
                for side in range(2):
                    edge_ref[member, side, lag - 1] = jnp.where(
                        offsets[pl.ds(side * STRETCH, EDGE), :] >= lag, 1.0, 0.0
                    )

    first = pl.multiple_of(lax.axis_index("tp") * 32 + pl.program_id(0) * PER_TILE, PER_TILE)
    rows_f = forward_rows[pl.ds(first, PER_TILE), :]
    rows_b = backward_rows[pl.ds(first, PER_TILE), :]
    for group in range(PER_TILE):
        for rows, out_ref in ((rows_f, forward_ref), (rows_b, backward_ref)):
            spread = jnp.broadcast_to(rows[group : group + 1, :], (128, 256))
            out_ref[group] = pltpu.roll(spread, 0, 1, stride=1, stride_axis=0).astype(BF16)


def edge_conv(rows, weights, edge_ref, side):
    total = rows[pl.ds(NEAR, EDGE), :] * weights[0:1, :]
    for lag in range(1, TAPS):
        moved = rows[pl.ds(NEAR - lag, EDGE), :] * weights[lag : lag + 1, :]
        total = total + moved * edge_ref[side, lag - 1]
    return total.astype(BF16).astype(F32)


def pair_kernel(
    members, feat_ref, kvg_ref, cot_ref, own_up_ref, up_ref, down_ref, taps_ref, keep_r_ref, edge_ref,
    mixed_ref, grads_ref, kv_ref, sums_ref,
    left, right, rows, beyond,
):
    member = pl.program_id(1)
    tile = pl.program_id(0)
    lanes = pl.ds(pl.multiple_of(tile * TILE, TILE), TILE)
    base = member * STRETCH

    def own(first, count):
        return pl.ds(pl.multiple_of(base + first, EDGE), count)

    is_last = lax.axis_index("ctx") == members - 1

    @pl.when(member == 0)
    def _():
        left[...] = up_ref[pl.ds(0, TAIL), lanes]

    @pl.when((member == 1) & is_last)
    def _():
        left[...] = own_up_ref[pl.ds(0, TAIL), lanes]

    @pl.when((member == 1) & jnp.logical_not(is_last))
    def _():
        left[...] = down_ref[pl.ds(0, TAIL), lanes]

    @pl.when(member == 1)
    def _():
        right[...] = up_ref[pl.ds(TAIL, HEAD), lanes]

    @pl.when((member == 0) & is_last)
    def _():
        right[...] = own_up_ref[pl.ds(TAIL, HEAD), lanes]

    @pl.when((member == 0) & jnp.logical_not(is_last))
    def _():
        right[...] = down_ref[pl.ds(TAIL, HEAD), lanes]

    inner = pl.ds(EDGE, STRETCH - EDGE)
    for side in range(2):
        place = pl.ds(side * STRETCH, EDGE)
        if side == 0:
            cot = cot_ref[own(0, EDGE), lanes].astype(F32)
        else:
            cot = right[pl.ds(144, EDGE), :].astype(F32)[NEAR:]
        fixed = []
        for stream in range(3):
            place_two, half = pl.ds(128 + stream // 2 * EDGE, EDGE), stream % 2 * NEAR
            if side == 0:
                rows[pl.ds(0, NEAR), :] = left[place_two, :].astype(F32)[half : half + NEAR]
                rows[pl.ds(NEAR, EDGE), :] = feat_ref[stream, own(0, EDGE), lanes].astype(F32)
            else:
                rows[pl.ds(0, NEAR), :] = feat_ref[stream, own(STRETCH - EDGE, EDGE), lanes].astype(F32)[NEAR:]
                rows[pl.ds(NEAR, NEAR), :] = right[place_two, :].astype(F32)[half : half + NEAR]
                rows[pl.ds(EDGE, NEAR), :] = jnp.zeros((NEAR, TILE), F32)
            fixed.append(edge_conv(rows, taps_ref[stream, :, lanes], edge_ref.at[member], side))
        if side == 0:
            grads_ref[member, place, lanes] = (cot * fixed[0]).astype(BF16)
        else:
            beyond[pl.ds(0, NEAR), :] = cot * fixed[0][:NEAR]
            beyond[pl.ds(REACH, 128), :] = right[pl.ds(0, 128), :].astype(F32)
            beyond[pl.ds(REACH + 128, 144 - REACH - 128), :] = jnp.zeros((144 - REACH - 128, TILE), F32)
            grads_ref[member, pl.ds(STRETCH, 144), lanes] = beyond[...].astype(BF16)
        kv_ref[member, 0, place, lanes] = fixed[1].astype(BF16)
        kv_ref[member, 1, place, lanes] = fixed[2].astype(BF16)
        mixed_ref[member, pl.ds(128 + side * STRETCH, EDGE), lanes] = (fixed[1] * fixed[2]).astype(BF16)
    keys = kvg_ref[0, own(EDGE, STRETCH - EDGE), lanes]
    values = kvg_ref[1, own(EDGE, STRETCH - EDGE), lanes]
    kv_ref[member, 0, inner, lanes] = keys
    kv_ref[member, 1, inner, lanes] = values
    mixed_ref[member, pl.ds(0, 128), lanes] = left[pl.ds(0, 128), :]
    mixed_ref[member, pl.ds(128 + EDGE, STRETCH - EDGE), lanes] = (keys.astype(F32) * values.astype(F32)).astype(BF16)
    mixed_ref[member, pl.ds(400, 112), lanes] = jnp.zeros((112, TILE), BF16)
    grads_ref[member, inner, lanes] = kvg_ref[2, own(EDGE, STRETCH - EDGE), lanes]
    grads_ref[member, pl.ds(400, 112), lanes] = jnp.zeros((112, TILE), BF16)

    @pl.when(member == 1)
    def _():
        pair_sums(mixed_ref, grads_ref, keep_r_ref, sums_ref, tile, lanes)


def pair_sums(mixed_ref, grads_ref, keep_r_ref, sums_ref, tile, lanes):
    lane = lax.broadcasted_iota(jnp.int32, (128, TILE), 1)
    row = lax.broadcasted_iota(jnp.int32, (128, TILE), 0)
    lane_group = lane // GROUP
    near = lane + row >= 127
    turn = jnp.where(lane + row == 127, 1.0, 0.0).astype(BF16)
    sources = []
    for member in range(2):
        turned = [
            lax.dot_general(
                mixed_ref[member, pl.ds(piece * 128, 128), lanes], turn, (((0,), (0,)), ((), ())),
                preferred_element_type=F32,
            ).astype(BF16)
            for piece in range(3)
        ]
        for block in range(2):
            sources.append(jnp.concatenate([turned[block + 1], turned[block]], axis=1))
    for group in range(PER_TILE):
        choose = jnp.where(lane_group == group, 1.0, 0.0).astype(BF16)
        total = jnp.zeros((128, TILE), F32)
        for member in range(2):
            for block in range(2):
                chosen = grads_ref[member, pl.ds(block * 128, 128), lanes] * choose
                pair = jnp.dot(chosen, sources[member * 2 + block], preferred_element_type=F32)
                pair = jnp.where(near, pair[:, :128], pair[:, 128:])
                total = total + pair * keep_r_ref[member, block]
        lined_up = pltpu.roll(total, 1, 1, stride=1, stride_axis=0)
        sums_ref[pl.ds(group, 1), lanes] = jnp.sum(lined_up, axis=0, keepdims=True)


def conv_kernel(
    members, first_tile, feat_ref, mixed_ref, grads_ref, kv_ref, cot_ref, own_up_ref, up_ref, down_ref,
    taps_ref, skip_ref, forward_ref, backward_ref, keep_f_ref, keep_b_ref, shifted_ref,
    stack_ref, sums_ref,
    cots, stack,
):
    member = pl.program_id(1)
    tile = first_tile + pl.program_id(0)
    lanes = pl.ds(pl.multiple_of(tile * TILE, TILE), TILE)
    base = member * STRETCH

    def own(first, count):
        return pl.ds(pl.multiple_of(base + first, EDGE), count)

    is_last = lax.axis_index("ctx") == members - 1
    first_group = tile * PER_TILE
    lane_group = lax.broadcasted_iota(jnp.int32, (128, TILE), 1) // GROUP
    skip = skip_ref[:, lanes]
    after = pl.ds(TAIL + 144, EDGE)
    beyond = pl.ds(STRETCH, NEAR)
    cots[pl.ds(STRETCH + NEAR, NEAR), :] = jnp.zeros((NEAR, TILE), F32)
    cots[pl.ds(0, STRETCH), :] = cot_ref[own(0, STRETCH), lanes].astype(F32)

    @pl.when(member == 1)
    def _():
        cots[beyond, :] = up_ref[after, lanes].astype(F32)[NEAR:]

    @pl.when((member == 0) & is_last)
    def _():
        cots[beyond, :] = own_up_ref[after, lanes].astype(F32)[NEAR:]

    @pl.when((member == 0) & jnp.logical_not(is_last))
    def _():
        cots[beyond, :] = down_ref[after, lanes].astype(F32)[NEAR:]

    def convolved(table_ref, keep_ref, window, block):
        height = 128 if block < 2 else EDGE
        keep = keep_ref[member, block, pl.ds(0, height), :]
        matrix = table_ref[pl.ds(first_group, PER_TILE), pl.ds(0, height), :] * keep[None]
        product = jnp.dot(matrix.reshape(PER_TILE * height, 256), window, preferred_element_type=F32)
        result = product[:height]
        for group in range(1, PER_TILE):
            result = jnp.where(lane_group[:height] == group, product[group * height : (group + 1) * height], result)
        return result

    for block in range(3):
        height = 128 if block < 2 else EDGE
        place = pl.ds(block * 128, height)
        medium = convolved(forward_ref, keep_f_ref, mixed_ref[member, pl.ds(block * 128, 256), lanes], block)
        medium = medium + skip * mixed_ref[member, pl.ds(block * 128 + 128, height), lanes].astype(F32)
        grad_conv = convolved(backward_ref, keep_b_ref, grads_ref[member, pl.ds(block * 128, 256), lanes], block)
        grad_conv = grad_conv + skip * grads_ref[member, place, lanes].astype(F32)
        for stream in range(3):
            if stream == 0:
                product = cots[place, :] * medium
            else:
                product = grad_conv * kv_ref[member, 2 - stream, place, lanes].astype(F32)
            product = product.astype(BF16)
            stack[stream, place, :] = product.astype(F32)
            stack_ref[member, stream, place, pl.ds(pl.multiple_of(pl.program_id(0) * TILE, TILE), TILE)] = product

    @pl.when(member == 0)
    def _():
        sums_ref[...] = jnp.zeros(sums_ref.shape, F32)

    for stream in range(3):
        partial = [jnp.zeros((8, TILE), F32) for _ in range(TAPS)]
        for chunk in range(0, STRETCH, 64):
            source = feat_ref[stream, own(chunk, 64), lanes].astype(F32)
            for lag in range(TAPS):
                later = stack[stream, pl.ds(chunk + lag, 64), :] * source
                if lag > 0:
                    later = later * shifted_ref[member, lag - 1, pl.ds(chunk, 64), :]
                partial[lag] = partial[lag] + jnp.sum(later.reshape(8, 8, TILE), axis=0)
        for lag in range(TAPS):
            row = pl.ds(stream * 8 + lag, 1)
            sums_ref[row, :] += jnp.sum(partial[lag], axis=0, keepdims=True)
    bias = jnp.sum(
        grads_ref[member, pl.ds(0, STRETCH), lanes].astype(F32) * mixed_ref[member, pl.ds(128, STRETCH), lanes].astype(F32),
        axis=0, keepdims=True,
    )
    sums_ref[pl.ds(7, 1), :] += bias


def adjoint_kernel(pieces, *refs):
    stack_refs, (taps_ref, shifted_ref, previous_ref, out_ref, stack) = refs[:pieces], refs[pieces:]
    del previous_ref
    tile, member = pl.program_id(0), pl.program_id(1)
    if pieces == 1:
        stack[...] = stack_refs[0][member, :, :, pl.ds(pl.multiple_of(tile * TILE, TILE), TILE)].astype(F32)
    for piece in range(pieces if pieces > 1 else 0):
        @pl.when(tile == piece)
        def _():
            stack[...] = stack_refs[piece][member].astype(F32)
    for stream in range(3):
        weights = taps_ref[stream]
        for chunk in range(0, STRETCH, 64):
            total = stack[stream, pl.ds(chunk, 64), :] * weights[0:1, :]
            for lag in range(1, TAPS):
                later = stack[stream, pl.ds(chunk + lag, 64), :] * shifted_ref[member, lag - 1, pl.ds(chunk, 64), :]
                total = total + later * weights[lag : lag + 1, :]
            out_ref[stream, pl.ds(chunk, 64), :] = total.astype(BF16)


def final_kernel(scale, flip, taps_ref, next_taps_ref, sums_ref, other_ref, medium_ref, short_ref, bias_ref):
    half = medium_ref.shape[1] // 2

    def by_group(ref):
        pieces = [
            ref[first : first + PER_TILE, tile * TILE : (tile + 1) * TILE]
            for first in range(0, ref.shape[0], PER_TILE)
            for tile in range(ref.shape[1] // TILE)
        ]
        return jnp.concatenate(pieces, axis=0).T * scale

    upper = (lax.axis_index("tp") // flip) % 2 == 1

    @pl.when(upper)
    def _():
        medium_ref[:, pl.ds(half, half)] = by_group(taps_ref)
        medium_ref[:, pl.ds(0, half)] = by_group(next_taps_ref)

    @pl.when(jnp.logical_not(upper))
    def _():
        medium_ref[:, pl.ds(0, half)] = by_group(taps_ref)
        medium_ref[:, pl.ds(half, half)] = by_group(next_taps_ref)

    total = (sums_ref[...] + other_ref[...]) * scale
    for stream in range(3):
        short_ref[stream] = total[stream * 8 : stream * 8 + TAPS]
    bias_ref[...] = total[TAPS : TAPS + 1]


def along(block, axis, route):
    return lax.ppermute(block, axis, route)


def routes_z():
    return [
        [(i, i // 8 * 8 + 7 - i % 8) for i in range(32)],
        [(i, i ^ 1) for i in range(32)],
        [(i, i ^ 2) for i in range(32)],
    ]


def routes_x():
    return [[(i, (3 - i // 8) * 8 + i % 8) for i in range(32)], [(i, i ^ 8) for i in range(32)]]


def shards(features, short_filter, medium_filter, skip_bias, cotangent, doc_lengths):
    members = lax.axis_size("ctx")
    tp = lax.axis_index("tp")
    channels = features.shape[2]
    tiles = channels // TILE
    scale = 1.0 / math.sqrt(2 * STRETCH * members)
    streams = jnp.transpose(features, (1, 0, 2))
    weights = jnp.transpose(short_filter, (1, 0, 2))
    smem = pl.BlockSpec(memory_space=pltpu.SMEM)
    shape = jax.ShapeDtypeStruct
    params = pltpu.CompilerParams(vmem_limit_bytes=16 * 1024 * 1024)

    whole = pl.BlockSpec(memory_space=pltpu.VMEM)
    anywhere = pl.BlockSpec(memory_space=pl.ANY)
    pay_up, pay_down = pl.pallas_call(
        functools.partial(payload_kernel, members),
        in_specs=[anywhere] * 4,
        out_specs=[anywhere] * 2,
        out_shape=[shape((TAIL + HEAD, channels), BF16), shape((TAIL + HEAD, channels), BF16)],
        scratch_shapes=[
            pltpu.SMEM((DOCS,), jnp.int32),
            pltpu.VMEM((3, TAPS, channels), F32),
            pltpu.VMEM((TAIL + HEAD, channels), BF16),
            pltpu.VMEM((TAIL + HEAD, channels), BF16),
            pltpu.VMEM((3, 2 * STRETCH, channels), BF16),
            pltpu.VMEM((2 * STRETCH, channels), BF16),
            pltpu.VMEM((2, TAPS - 1, STRETCH, TILE), F32),
            pltpu.VMEM((STRETCH + 8, TILE), F32),
            pltpu.VMEM((144, TILE), F32),
            pltpu.SemaphoreType.DMA((22,)),
        ],
        compiler_params=pltpu.CompilerParams(vmem_limit_bytes=56 * 1024 * 1024),
        cost_estimate=pl.CostEstimate(flops=20_000_000, bytes_accessed=2_800_000, transcendentals=0),
        name="payload_rows",
    )(doc_lengths, streams, cotangent, weights)

    got_up = lax.ppermute(pay_up, "ctx", [(i, i + 1) for i in range(members - 1)])
    got_down = lax.ppermute(pay_down, "ctx", [(i + 1, i) for i in range(members - 1)])

    kvg = pl.pallas_call(
        functools.partial(own_kernel, members),
        grid=(tiles,),
        in_specs=[
            smem,
            pl.BlockSpec((3, 2 * STRETCH, TILE), lambda l: (0, 0, l)),
            pl.BlockSpec((2 * STRETCH, TILE), lambda l: (0, l)),
            pl.BlockSpec((3, TAPS, TILE), lambda l: (0, 0, l)),
        ],
        out_specs=pl.BlockSpec((3, 2 * STRETCH, TILE), lambda l: (0, 0, l)),
        out_shape=shape((3, 2 * STRETCH, channels), BF16),
        scratch_shapes=[
            pltpu.VMEM((2, TAPS - 1, STRETCH, TILE), F32),
            pltpu.VMEM((STRETCH + 8, TILE), F32),
        ],
        compiler_params=params,
        cost_estimate=pl.CostEstimate(flops=40_000_000, bytes_accessed=4_500_000, transcendentals=0),
        name="own_rows",
    )(doc_lengths, streams, cotangent, weights)

    groups = channels // GROUP
    tables = pl.pallas_call(
        functools.partial(tables_kernel, members),
        grid=(tiles,),
        in_specs=[smem, anywhere],
        out_specs=[
            pl.BlockSpec((PER_TILE, 128, 256), lambda l: (l, 0, 0)),
            pl.BlockSpec((PER_TILE, 128, 256), lambda l: (l, 0, 0)),
            pl.BlockSpec((2, 3, 128, 256), lambda l: (0, 0, 0, 0)),
            pl.BlockSpec((2, 3, 128, 256), lambda l: (0, 0, 0, 0)),
            pl.BlockSpec((2, 2, 128, 128), lambda l: (0, 0, 0, 0)),
            pl.BlockSpec((2, TAPS - 1, STRETCH, TILE), lambda l: (0, 0, 0, 0)),
            pl.BlockSpec((2, 2, TAPS - 1, EDGE, TILE), lambda l: (0, 0, 0, 0, 0)),
        ],
        out_shape=[
            shape((groups, 128, 256), BF16),
            shape((groups, 128, 256), BF16),
            shape((2, 3, 128, 256), BF16),
            shape((2, 3, 128, 256), BF16),
            shape((2, 2, 128, 128), F32),
            shape((2, TAPS - 1, STRETCH, TILE), F32),
            shape((2, 2, TAPS - 1, EDGE, TILE), F32),
        ],
        scratch_shapes=[
            pltpu.VMEM((256, 256), F32),
            pltpu.VMEM((256, 256), F32),
            pltpu.VMEM((384, TILE), F32),
            pltpu.VMEM(medium_filter.shape, F32),
            pltpu.SemaphoreType.DMA,
        ],
        compiler_params=params,
        cost_estimate=pl.CostEstimate(flops=20_000_000, bytes_accessed=7_000_000, transcendentals=0),
        name="tables",
    )(doc_lengths, medium_filter)

    forward, backward, keep_f, keep_b, keep_r, shifted, edge = tables
    mixed, grads, kv, taps = pl.pallas_call(
        functools.partial(pair_kernel, members),
        grid=(tiles, 2),
        in_specs=[whole] * 9,
        out_specs=[whole] * 4,
        out_shape=[
            shape((2, 512, channels), BF16),
            shape((2, 512, channels), BF16),
            shape((2, 2, STRETCH + EDGE, channels), BF16),
            shape((PER_TILE, channels), F32),
        ],
        scratch_shapes=[
            pltpu.VMEM((TAIL, TILE), BF16),
            pltpu.VMEM((HEAD, TILE), BF16),
            pltpu.VMEM((NEAR + EDGE, TILE), F32),
            pltpu.VMEM((144, TILE), F32),
        ],
        compiler_params=params,
        cost_estimate=pl.CostEstimate(flops=500_000_000, bytes_accessed=10_000_000, transcendentals=0),
        name="pair_rows",
    )(streams, kvg, cotangent, pay_up, got_up, got_down, weights, keep_r, edge)

    def convolve(first, count, mixed, grads):
        return pl.pallas_call(
            functools.partial(conv_kernel, members, first),
            grid=(count, 2),
            in_specs=[whole] * 15,
            out_specs=[
                whole,
                pl.BlockSpec((24, TILE), lambda l, m: (0, l)),
            ],
            out_shape=[
                shape((2, 3, STRETCH + EDGE, count * TILE), BF16),
                shape((24, count * TILE), F32),
            ],
            scratch_shapes=[
                pltpu.VMEM((STRETCH + EDGE, TILE), F32),
                pltpu.VMEM((3, STRETCH + EDGE, TILE), F32),
            ],
            compiler_params=params,
            cost_estimate=pl.CostEstimate(flops=count * 100_000_000, bytes_accessed=count * 2_500_000, transcendentals=0),
            name=f"conv_rows_{first}",
        )(
            streams, mixed, grads, kv, cotangent, pay_up, got_up, got_down,
            weights, skip_bias.reshape(1, channels), forward, backward, keep_f, keep_b, shifted,
        )

    parts, stacks = [], []
    for route, (first, count) in zip(routes_x() + routes_z()[1:2], ((0, 1), (1, 1), (2, 2))):
        other = along(taps, "ctx", route)
        stack, part = convolve(first, count, mixed, grads)
        stacks.append(stack)
        taps, mixed, grads, part = lax.optimization_barrier((taps + other, mixed, grads, part))
        parts.append(part)

    def adjoint(first, pieces, previous):
        return pl.pallas_call(
            functools.partial(adjoint_kernel, len(pieces)),
            grid=(2, 2),
            in_specs=[whole] * len(pieces) + [
                pl.BlockSpec((3, TAPS, TILE), lambda l, m: (0, 0, first + l)), whole, anywhere,
            ],
            out_specs=pl.BlockSpec((3, STRETCH, TILE), lambda l, m: (0, m, first + l)),
            out_shape=shape((3, 2 * STRETCH, channels), BF16),
            input_output_aliases={len(pieces) + 2: 0} if first > 0 else {},
            scratch_shapes=[pltpu.VMEM((3, STRETCH + EDGE, TILE), F32)],
            compiler_params=params,
            cost_estimate=pl.CostEstimate(flops=20_000_000, bytes_accessed=4_000_000, transcendentals=0),
            name=f"adjoint_rows_{first}",
        )(*pieces, weights, shifted, previous)

    sums = jnp.concatenate(parts, axis=1)
    grad_streams = kvg
    routes = routes_z()[2:] + routes_z()[:2] + routes_x()
    flip = 1
    for step, route in enumerate(routes):
        if step < 2:
            both = jnp.concatenate([sums, taps], axis=0)
            other = along(both, "ctx", route)
            both = both + other
            sums, taps = both[:24], both[24:]
        else:
            other = along(sums, "ctx", route)
            next_taps = along(taps, "tp", [(i, i ^ flip) for i in range(lax.axis_size("tp"))])
            if step < len(routes) - 1:
                upper = (tp // flip) % 2 == 1
                taps = jnp.concatenate(
                    [jnp.where(upper, next_taps, taps), jnp.where(upper, taps, next_taps)], axis=0
                )
                sums = sums + other
                flip *= 2
        if step < 2:
            grad_streams = adjoint(2 * step, stacks[2 * step : 2 * step + 2], grad_streams)
        sums, taps, grad_streams = lax.optimization_barrier((sums, taps, grad_streams))
    grad_medium, short, bias = pl.pallas_call(
        functools.partial(final_kernel, scale, flip),
        in_specs=[whole] * 4,
        out_shape=[
            shape(medium_filter.shape, F32), shape((3, TAPS, channels), F32), shape((1, channels), F32),
        ],
        compiler_params=params,
        name="final",
    )(taps, next_taps, sums, other)
    return (
        jnp.transpose(grad_streams, (1, 0, 2)), jnp.transpose(short, (1, 0, 2)), grad_medium,
        bias.reshape(channels),
    )


def solution(mesh):
    in_specs = (P("ctx", None, "tp"), P(None, None, "tp"), P(), P("tp"), P("ctx", "tp"), P())
    out_specs = (P("ctx", None, "tp"), P(None, None, "tp"), P(), P("tp"))
    return jax.shard_map(shards, mesh=mesh, in_specs=in_specs, out_specs=out_specs, check_vma=False)
```

```python
import functools
import math

import jax
import jax.numpy as jnp
from jax import lax
from jax.experimental import pallas as pl
from jax.experimental.pallas import tpu as pltpu
from jax.sharding import PartitionSpec as P

STRETCH = 256
TILE = 128
GROUP = 16
PER_TILE = TILE // GROUP
LAGS = 128
TAPS = 7
EDGE = 16
TAIL = 128 + 2 * EDGE
HEAD = 128 + 2 * EDGE
REACH = TAPS - 1
NEAR = 8
DOCS = 64
F32 = jnp.float32
BF16 = jnp.bfloat16


def base_of(device, members, member):
    first = device * STRETCH
    second = (2 * members - 1 - device) * STRETCH
    if isinstance(member, int):
        return first if member == 0 else second
    return jnp.where(member == 0, first, second)


def lane_starts(lengths_ref, base, count):
    position = base + lax.broadcasted_iota(jnp.int32, (8, count), 1)
    found = jnp.zeros((8, count), jnp.int32)
    running = jnp.int32(0)
    for doc in range(DOCS):
        found = jnp.where(position >= running, running, found)
        running = running + lengths_ref[doc]
    return found.astype(F32)


def row_starts(starts, block):
    row = starts[0:1, block * 128 : (block + 1) * 128]
    return jnp.broadcast_to(row, (128, 128)).T


def row_positions(base, block):
    return (base + block * 128 + lax.broadcasted_iota(jnp.int32, (128, 128), 0)).astype(F32)


def conv_rows(rows, weights, masks, member, first, count):
    total = rows[pl.ds(8 + first, count), :] * weights[0:1, :]
    for lag in range(1, TAPS):
        moved = rows[pl.ds(8 + first - lag, count), :] * weights[lag : lag + 1, :]
        total = total + moved * masks[member, lag - 1, pl.ds(first, count), :]
    return total.astype(BF16)


def own_masks(members, lengths_ref, masks):
    for member in range(2):
        base = base_of(lax.axis_index("ctx"), members, member)
        starts = lane_starts(lengths_ref, base, STRETCH)
        for block in range(2):
            offset = row_positions(base, block) - row_starts(starts, block)
            for lag in range(1, TAPS):
                masks[member, lag - 1, pl.ds(block * 128, 128), :] = jnp.where(offset >= lag, 1.0, 0.0)


def payload_kernel(
    members, lengths_hbm, feat_hbm, cot_hbm, taps_hbm, up_hbm, down_hbm,
    lengths_ref, taps_ref, up_ref, down_ref, feat, cots, masks, rows, grads, sems,
):
    copies = []

    def fetch(source, target):
        copies.append(pltpu.make_async_copy(source, target, sems.at[len(copies)]))
        copies[-1].start()
        return copies[-1]

    def fetch_rows(stream, first, count):
        place = pl.ds(first, count)
        return fetch(feat_hbm.at[stream, place, :], feat.at[stream, place, :])

    fetch(lengths_hbm, lengths_ref)
    fetch(taps_hbm, taps_ref)
    needed = {}
    for member in range(2):
        first = member * STRETCH
        head = pl.ds(first, 144)
        needed[member, "head"] = [fetch_rows(0, first, 144), fetch(cot_hbm.at[head, :], cots.at[head, :])]
    for member in range(2):
        first = member * STRETCH
        needed[member, "tail"] = [fetch_rows(stream, first + 112, 144) for stream in (1, 2)]
    edges = []
    for member in range(2):
        first = member * STRETCH
        edges.append(fetch_rows(0, first + STRETCH - EDGE, EDGE))
        edges += [fetch_rows(stream, first, EDGE) for stream in (1, 2)]

    copies[0].wait()
    own_masks(members, lengths_ref, masks)
    copies[1].wait()
    rows[pl.ds(0, 8), :] = jnp.zeros((8, TILE), F32)
    tiles = [pl.ds(tile * TILE, TILE) for tile in range(up_ref.shape[1] // TILE)]
    for member in range(2):
        head_ref = down_ref if member == 0 else up_ref
        first = member * STRETCH
        for copy in needed[member, "head"]:
            copy.wait()
        for lanes in tiles:
            rows[pl.ds(8, 144), :] = feat[0, pl.ds(first, 144), lanes].astype(F32)
            weights = taps_ref[0, :, lanes]
            for chunk in range(0, 144, 48):
                query = conv_rows(rows, weights, masks, member, chunk, 48).astype(F32)
                cot = cots[pl.ds(first + chunk, 48), lanes].astype(F32)
                grads[pl.ds(chunk, 48), :] = cot * query
            head_ref[pl.ds(TAIL, 128), lanes] = grads[pl.ds(REACH, 128), :].astype(BF16)
    sent = []
    big = pl.ds(TAIL, 128)
    for source, target in ((up_ref, up_hbm), (down_ref, down_hbm)):
        sent.append(fetch(source.at[big, :], target.at[big, :]))
    for member in range(2):
        tail_ref = up_ref if member == 0 else down_ref
        first = member * STRETCH
        for copy in needed[member, "tail"]:
            copy.wait()
        for lanes in tiles:
            for stream in (1, 2):
                rows[pl.ds(8 + 112, 144), :] = feat[stream, pl.ds(first + 112, 144), lanes].astype(F32)
                weights = taps_ref[stream, :, lanes]
                for chunk in range(0, 128, 64):
                    part = conv_rows(rows, weights, masks, member, 128 + chunk, 64)
                    place = pl.ds(chunk, 64)
                    if stream == 2:
                        part = (tail_ref[place, lanes].astype(F32) * part.astype(F32)).astype(BF16)
                    tail_ref[place, lanes] = part
    for copy in edges:
        copy.wait()
    for member in range(2):
        tail_ref = up_ref if member == 0 else down_ref
        head_ref = down_ref if member == 0 else up_ref
        first = member * STRETCH
        last = [feat[stream, pl.ds(first + STRETCH - EDGE, EDGE), :].astype(F32)[NEAR:] for stream in range(3)]
        ahead = [feat[stream, pl.ds(first, EDGE), :].astype(F32)[:NEAR] for stream in range(3)]
        ahead.append(cots[pl.ds(first, EDGE), :].astype(F32)[:NEAR])
        for pair in range(2):
            place = 128 + pair * EDGE
            two = jnp.concatenate([last[2 * pair], last[min(2 * pair + 1, 2)]], axis=0)
            tail_ref[pl.ds(place, EDGE), :] = two.astype(BF16)
            two = jnp.concatenate([ahead[2 * pair], ahead[2 * pair + 1]], axis=0)
            head_ref[pl.ds(TAIL + place, EDGE), :] = two.astype(BF16)
    for source, target in ((up_ref, up_hbm), (down_ref, down_hbm)):
        for part in (pl.ds(0, TAIL), pl.ds(TAIL + 128, 2 * EDGE)):
            sent.append(fetch(source.at[part, :], target.at[part, :]))
    for copy in sent:
        copy.wait()


def own_kernel(members, lengths_ref, feat_ref, cot_ref, taps_ref, kvg_ref, masks, rows):
    @pl.when(pl.program_id(0) == 0)
    def _():
        own_masks(members, lengths_ref, masks)

    rows[pl.ds(0, 8), :] = jnp.zeros((8, TILE), F32)
    for member in range(2):
        first = member * STRETCH
        for stream in range(3):
            rows[pl.ds(8, STRETCH), :] = feat_ref[stream, pl.ds(first, STRETCH), :].astype(F32)
            weights = taps_ref[stream]
            for chunk in range(0, STRETCH, 64):
                rounded = conv_rows(rows, weights, masks, member, chunk, 64)
                if stream == 0:
                    cot = cot_ref[pl.ds(first + chunk, 64), :].astype(F32)
                    rounded = (cot * rounded.astype(F32)).astype(BF16)
                    kvg_ref[2, pl.ds(first + chunk, 64), :] = rounded
                else:
                    kvg_ref[stream - 1, pl.ds(first + chunk, 64), :] = rounded


def tables_kernel(
    members, lengths_ref, medium_ref,
    forward_ref, backward_ref, keep_f_ref, keep_b_ref, keep_r_ref, shifted_ref, edge_ref,
    forward_rows, backward_rows, offsets, medium, medium_sem,
):
    device = lax.axis_index("ctx")

    @pl.when(pl.program_id(0) == 0)
    def _():
        copy = pltpu.make_async_copy(medium_ref, medium, medium_sem)
        copy.start()
        lag = lax.broadcasted_iota(jnp.int32, (LAGS, 256), 0)
        lane = lax.broadcasted_iota(jnp.int32, (LAGS, 256), 1)
        copy.wait()
        taps = medium[...].astype(BF16)
        dims = (((0,), (0,)), ((), ()))
        place_f = jnp.where(lane == LAGS - lag, 1.0, 0.0).astype(BF16)
        place_b = jnp.where(lane == lag, 1.0, 0.0).astype(BF16)
        forward_rows[...] = lax.dot_general(taps, place_f, dims, preferred_element_type=F32)
        backward_rows[...] = lax.dot_general(taps, place_b, dims, preferred_element_type=F32)
        wide = lax.broadcasted_iota(jnp.int32, (128, 256), 1)
        tall = lax.broadcasted_iota(jnp.int32, (128, 256), 0)
        narrow = lax.broadcasted_iota(jnp.int32, (128, 128), 1)
        for member in range(2):
            base = base_of(device, members, member)
            starts = lane_starts(lengths_ref, base, 512)
            for block in range(3):
                begin = row_starts(starts, block)
                begin = jnp.concatenate([begin, begin], axis=1)
                source = (base + (block - 1) * 128 + wide).astype(F32)
                keep_f_ref[member, block] = jnp.where(source >= begin, 1.0, 0.0).astype(BF16)
                if block < 2:
                    turned = jnp.where(
                        narrow + tall[:, :128] >= 127,
                        base + block * 128 + 127 - narrow, base + (block - 1) * 128 + 127 - narrow,
                    ).astype(F32)
                    keep_r_ref[member, block] = jnp.where(turned >= begin[:, :128], 1.0, 0.0)
                own = (base + block * 128 + tall).astype(F32)
                target = jnp.broadcast_to(starts[0:1, block * 128 : block * 128 + 256], (128, 256))
                keep_b_ref[member, block] = jnp.where(own >= target, 1.0, 0.0).astype(BF16)
                offsets[pl.ds(block * 128, 128), :] = row_positions(base, block) - begin[:, :128]
            for lag in range(1, TAPS):
                shifted_ref[member, lag - 1] = jnp.where(
                    offsets[pl.ds(lag, STRETCH), :] >= lag, 1.0, 0.0
                )
                for side in range(2):
                    edge_ref[member, side, lag - 1] = jnp.where(
                        offsets[pl.ds(side * STRETCH, EDGE), :] >= lag, 1.0, 0.0
                    )

    first = pl.multiple_of(lax.axis_index("tp") * 32 + pl.program_id(0) * PER_TILE, PER_TILE)
    rows_f = forward_rows[pl.ds(first, PER_TILE), :]
    rows_b = backward_rows[pl.ds(first, PER_TILE), :]
    for group in range(PER_TILE):
        for rows, out_ref in ((rows_f, forward_ref), (rows_b, backward_ref)):
            spread = jnp.broadcast_to(rows[group : group + 1, :], (128, 256))
            out_ref[group] = pltpu.roll(spread, 0, 1, stride=1, stride_axis=0).astype(BF16)


def edge_conv(rows, weights, edge_ref, side):
    total = rows[pl.ds(NEAR, EDGE), :] * weights[0:1, :]
    for lag in range(1, TAPS):
        moved = rows[pl.ds(NEAR - lag, EDGE), :] * weights[lag : lag + 1, :]
        total = total + moved * edge_ref[side, lag - 1]
    return total.astype(BF16).astype(F32)


def pair_kernel(
    members, feat_ref, kvg_ref, cot_ref, own_up_ref, up_ref, down_ref, taps_ref, keep_r_ref, edge_ref,
    mixed_ref, grads_ref, kv_ref, sums_ref,
    left, right, rows, beyond,
):
    member = pl.program_id(1)
    tile = pl.program_id(0)
    lanes = pl.ds(pl.multiple_of(tile * TILE, TILE), TILE)
    base = member * STRETCH

    def own(first, count):
        return pl.ds(pl.multiple_of(base + first, EDGE), count)

    is_last = lax.axis_index("ctx") == members - 1

    @pl.when(member == 0)
    def _():
        left[...] = up_ref[pl.ds(0, TAIL), lanes]

    @pl.when((member == 1) & is_last)
    def _():
        left[...] = own_up_ref[pl.ds(0, TAIL), lanes]

    @pl.when((member == 1) & jnp.logical_not(is_last))
    def _():
        left[...] = down_ref[pl.ds(0, TAIL), lanes]

    @pl.when(member == 1)
    def _():
        right[...] = up_ref[pl.ds(TAIL, HEAD), lanes]

    @pl.when((member == 0) & is_last)
    def _():
        right[...] = own_up_ref[pl.ds(TAIL, HEAD), lanes]

    @pl.when((member == 0) & jnp.logical_not(is_last))
    def _():
        right[...] = down_ref[pl.ds(TAIL, HEAD), lanes]

    inner = pl.ds(EDGE, STRETCH - EDGE)
    for side in range(2):
        place = pl.ds(side * STRETCH, EDGE)
        if side == 0:
            cot = cot_ref[own(0, EDGE), lanes].astype(F32)
        else:
            cot = right[pl.ds(144, EDGE), :].astype(F32)[NEAR:]
        fixed = []
        for stream in range(3):
            place_two, half = pl.ds(128 + stream // 2 * EDGE, EDGE), stream % 2 * NEAR
            if side == 0:
                rows[pl.ds(0, NEAR), :] = left[place_two, :].astype(F32)[half : half + NEAR]
                rows[pl.ds(NEAR, EDGE), :] = feat_ref[stream, own(0, EDGE), lanes].astype(F32)
            else:
                rows[pl.ds(0, NEAR), :] = feat_ref[stream, own(STRETCH - EDGE, EDGE), lanes].astype(F32)[NEAR:]
                rows[pl.ds(NEAR, NEAR), :] = right[place_two, :].astype(F32)[half : half + NEAR]
                rows[pl.ds(EDGE, NEAR), :] = jnp.zeros((NEAR, TILE), F32)
            fixed.append(edge_conv(rows, taps_ref[stream, :, lanes], edge_ref.at[member], side))
        if side == 0:
            grads_ref[member, place, lanes] = (cot * fixed[0]).astype(BF16)
        else:
            beyond[pl.ds(0, NEAR), :] = cot * fixed[0][:NEAR]
            beyond[pl.ds(REACH, 128), :] = right[pl.ds(0, 128), :].astype(F32)
            beyond[pl.ds(REACH + 128, 144 - REACH - 128), :] = jnp.zeros((144 - REACH - 128, TILE), F32)
            grads_ref[member, pl.ds(STRETCH, 144), lanes] = beyond[...].astype(BF16)
        kv_ref[member, 0, place, lanes] = fixed[1].astype(BF16)
        kv_ref[member, 1, place, lanes] = fixed[2].astype(BF16)
        mixed_ref[member, pl.ds(128 + side * STRETCH, EDGE), lanes] = (fixed[1] * fixed[2]).astype(BF16)
    keys = kvg_ref[0, own(EDGE, STRETCH - EDGE), lanes]
    values = kvg_ref[1, own(EDGE, STRETCH - EDGE), lanes]
    kv_ref[member, 0, inner, lanes] = keys
    kv_ref[member, 1, inner, lanes] = values
    mixed_ref[member, pl.ds(0, 128), lanes] = left[pl.ds(0, 128), :]
    mixed_ref[member, pl.ds(128 + EDGE, STRETCH - EDGE), lanes] = (keys.astype(F32) * values.astype(F32)).astype(BF16)
    mixed_ref[member, pl.ds(400, 112), lanes] = jnp.zeros((112, TILE), BF16)
    grads_ref[member, inner, lanes] = kvg_ref[2, own(EDGE, STRETCH - EDGE), lanes]
    grads_ref[member, pl.ds(400, 112), lanes] = jnp.zeros((112, TILE), BF16)

    @pl.when(member == 1)
    def _():
        pair_sums(mixed_ref, grads_ref, keep_r_ref, sums_ref, tile, lanes)


def pair_sums(mixed_ref, grads_ref, keep_r_ref, sums_ref, tile, lanes):
    lane = lax.broadcasted_iota(jnp.int32, (128, TILE), 1)
    row = lax.broadcasted_iota(jnp.int32, (128, TILE), 0)
    lane_group = lane // GROUP
    near = lane + row >= 127
    turn = jnp.where(lane + row == 127, 1.0, 0.0).astype(BF16)
    sources = []
    for member in range(2):
        turned = [
            lax.dot_general(
                mixed_ref[member, pl.ds(piece * 128, 128), lanes], turn, (((0,), (0,)), ((), ())),
                preferred_element_type=F32,
            ).astype(BF16)
            for piece in range(3)
        ]
        for block in range(2):
            sources.append(jnp.concatenate([turned[block + 1], turned[block]], axis=1))
    for group in range(PER_TILE):
        choose = jnp.where(lane_group == group, 1.0, 0.0).astype(BF16)
        total = jnp.zeros((128, TILE), F32)
        for member in range(2):
            for block in range(2):
                chosen = grads_ref[member, pl.ds(block * 128, 128), lanes] * choose
                pair = jnp.dot(chosen, sources[member * 2 + block], preferred_element_type=F32)
                pair = jnp.where(near, pair[:, :128], pair[:, 128:])
                total = total + pair * keep_r_ref[member, block]
        lined_up = pltpu.roll(total, 1, 1, stride=1, stride_axis=0)
        sums_ref[pl.ds(group, 1), lanes] = jnp.sum(lined_up, axis=0, keepdims=True)


def conv_kernel(
    members, first_tile, feat_ref, mixed_ref, grads_ref, kv_ref, cot_ref, own_up_ref, up_ref, down_ref,
    taps_ref, skip_ref, forward_ref, backward_ref, keep_f_ref, keep_b_ref, shifted_ref,
    stack_ref, sums_ref,
    cots, stack,
):
    member = pl.program_id(1)
    tile = first_tile + pl.program_id(0)
    lanes = pl.ds(pl.multiple_of(tile * TILE, TILE), TILE)
    base = member * STRETCH

    def own(first, count):
        return pl.ds(pl.multiple_of(base + first, EDGE), count)

    is_last = lax.axis_index("ctx") == members - 1
    first_group = tile * PER_TILE
    lane_group = lax.broadcasted_iota(jnp.int32, (128, TILE), 1) // GROUP
    skip = skip_ref[:, lanes]
    after = pl.ds(TAIL + 144, EDGE)
    beyond = pl.ds(STRETCH, NEAR)
    cots[pl.ds(STRETCH + NEAR, NEAR), :] = jnp.zeros((NEAR, TILE), F32)
    cots[pl.ds(0, STRETCH), :] = cot_ref[own(0, STRETCH), lanes].astype(F32)

    @pl.when(member == 1)
    def _():
        cots[beyond, :] = up_ref[after, lanes].astype(F32)[NEAR:]

    @pl.when((member == 0) & is_last)
    def _():
        cots[beyond, :] = own_up_ref[after, lanes].astype(F32)[NEAR:]

    @pl.when((member == 0) & jnp.logical_not(is_last))
    def _():
        cots[beyond, :] = down_ref[after, lanes].astype(F32)[NEAR:]

    def convolved(table_ref, keep_ref, window, block):
        height = 128 if block < 2 else EDGE
        keep = keep_ref[member, block, pl.ds(0, height), :]
        matrix = table_ref[pl.ds(first_group, PER_TILE), pl.ds(0, height), :] * keep[None]
        product = jnp.dot(matrix.reshape(PER_TILE * height, 256), window, preferred_element_type=F32)
        result = product[:height]
        for group in range(1, PER_TILE):
            result = jnp.where(lane_group[:height] == group, product[group * height : (group + 1) * height], result)
        return result

    for block in range(3):
        height = 128 if block < 2 else EDGE
        place = pl.ds(block * 128, height)
        medium = convolved(forward_ref, keep_f_ref, mixed_ref[member, pl.ds(block * 128, 256), lanes], block)
        medium = medium + skip * mixed_ref[member, pl.ds(block * 128 + 128, height), lanes].astype(F32)
        grad_conv = convolved(backward_ref, keep_b_ref, grads_ref[member, pl.ds(block * 128, 256), lanes], block)
        grad_conv = grad_conv + skip * grads_ref[member, place, lanes].astype(F32)
        for stream in range(3):
            if stream == 0:
                product = cots[place, :] * medium
            else:
                product = grad_conv * kv_ref[member, 2 - stream, place, lanes].astype(F32)
            product = product.astype(BF16)
            stack[stream, place, :] = product.astype(F32)
            stack_ref[member, stream, place, pl.ds(pl.multiple_of(pl.program_id(0) * TILE, TILE), TILE)] = product

    @pl.when(member == 0)
    def _():
        sums_ref[...] = jnp.zeros(sums_ref.shape, F32)

    for stream in range(3):
        partial = [jnp.zeros((8, TILE), F32) for _ in range(TAPS)]
        for chunk in range(0, STRETCH, 64):
            source = feat_ref[stream, own(chunk, 64), lanes].astype(F32)
            for lag in range(TAPS):
                later = stack[stream, pl.ds(chunk + lag, 64), :] * source
                if lag > 0:
                    later = later * shifted_ref[member, lag - 1, pl.ds(chunk, 64), :]
                partial[lag] = partial[lag] + jnp.sum(later.reshape(8, 8, TILE), axis=0)
        for lag in range(TAPS):
            row = pl.ds(stream * 8 + lag, 1)
            sums_ref[row, :] += jnp.sum(partial[lag], axis=0, keepdims=True)
    bias = jnp.sum(
        grads_ref[member, pl.ds(0, STRETCH), lanes].astype(F32) * mixed_ref[member, pl.ds(128, STRETCH), lanes].astype(F32),
        axis=0, keepdims=True,
    )
    sums_ref[pl.ds(7, 1), :] += bias


def adjoint_kernel(pieces, *refs):
    stack_refs, (taps_ref, shifted_ref, previous_ref, out_ref, stack) = refs[:pieces], refs[pieces:]
    del previous_ref
    tile, member = pl.program_id(0), pl.program_id(1)
    if pieces == 1:
        stack[...] = stack_refs[0][member, :, :, pl.ds(pl.multiple_of(tile * TILE, TILE), TILE)].astype(F32)
    for piece in range(pieces if pieces > 1 else 0):
        @pl.when(tile == piece)
        def _():
            stack[...] = stack_refs[piece][member].astype(F32)
    for stream in range(3):
        weights = taps_ref[stream]
        for chunk in range(0, STRETCH, 64):
            total = stack[stream, pl.ds(chunk, 64), :] * weights[0:1, :]
            for lag in range(1, TAPS):
                later = stack[stream, pl.ds(chunk + lag, 64), :] * shifted_ref[member, lag - 1, pl.ds(chunk, 64), :]
                total = total + later * weights[lag : lag + 1, :]
            out_ref[stream, pl.ds(chunk, 64), :] = total.astype(BF16)


def final_kernel(scale, flip, taps_ref, next_taps_ref, sums_ref, other_ref, medium_ref, short_ref, bias_ref):
    half = medium_ref.shape[1] // 2

    def by_group(ref):
        pieces = [
            ref[first : first + PER_TILE, tile * TILE : (tile + 1) * TILE]
            for first in range(0, ref.shape[0], PER_TILE)
            for tile in range(ref.shape[1] // TILE)
        ]
        return jnp.concatenate(pieces, axis=0).T * scale

    upper = (lax.axis_index("tp") // flip) % 2 == 1

    @pl.when(upper)
    def _():
        medium_ref[:, pl.ds(half, half)] = by_group(taps_ref)
        medium_ref[:, pl.ds(0, half)] = by_group(next_taps_ref)

    @pl.when(jnp.logical_not(upper))
    def _():
        medium_ref[:, pl.ds(0, half)] = by_group(taps_ref)
        medium_ref[:, pl.ds(half, half)] = by_group(next_taps_ref)

    total = (sums_ref[...] + other_ref[...]) * scale
    for stream in range(3):
        short_ref[stream] = total[stream * 8 : stream * 8 + TAPS]
    bias_ref[...] = total[TAPS : TAPS + 1]


def along(block, axis, route):
    return lax.ppermute(block, axis, route)


def routes_z():
    return [
        [(i, i // 8 * 8 + 7 - i % 8) for i in range(32)],
        [(i, i ^ 1) for i in range(32)],
        [(i, i ^ 2) for i in range(32)],
    ]


def routes_x():
    return [[(i, (3 - i // 8) * 8 + i % 8) for i in range(32)], [(i, i ^ 8) for i in range(32)]]


def shards(features, short_filter, medium_filter, skip_bias, cotangent, doc_lengths):
    members = lax.axis_size("ctx")
    tp = lax.axis_index("tp")
    channels = features.shape[2]
    tiles = channels // TILE
    scale = 1.0 / math.sqrt(2 * STRETCH * members)
    streams = jnp.transpose(features, (1, 0, 2))
    weights = jnp.transpose(short_filter, (1, 0, 2))
    smem = pl.BlockSpec(memory_space=pltpu.SMEM)
    shape = jax.ShapeDtypeStruct
    params = pltpu.CompilerParams(vmem_limit_bytes=16 * 1024 * 1024)

    whole = pl.BlockSpec(memory_space=pltpu.VMEM)
    anywhere = pl.BlockSpec(memory_space=pl.ANY)
    pay_up, pay_down = pl.pallas_call(
        functools.partial(payload_kernel, members),
        in_specs=[anywhere] * 4,
        out_specs=[anywhere] * 2,
        out_shape=[shape((TAIL + HEAD, channels), BF16), shape((TAIL + HEAD, channels), BF16)],
        scratch_shapes=[
            pltpu.SMEM((DOCS,), jnp.int32),
            pltpu.VMEM((3, TAPS, channels), F32),
            pltpu.VMEM((TAIL + HEAD, channels), BF16),
            pltpu.VMEM((TAIL + HEAD, channels), BF16),
            pltpu.VMEM((3, 2 * STRETCH, channels), BF16),
            pltpu.VMEM((2 * STRETCH, channels), BF16),
            pltpu.VMEM((2, TAPS - 1, STRETCH, TILE), F32),
            pltpu.VMEM((STRETCH + 8, TILE), F32),
            pltpu.VMEM((144, TILE), F32),
            pltpu.SemaphoreType.DMA((22,)),
        ],
        compiler_params=pltpu.CompilerParams(vmem_limit_bytes=56 * 1024 * 1024),
        cost_estimate=pl.CostEstimate(flops=20_000_000, bytes_accessed=2_800_000, transcendentals=0),
        name="payload_rows",
    )(doc_lengths, streams, cotangent, weights)

    got_up = lax.ppermute(pay_up, "ctx", [(i, i + 1) for i in range(members - 1)])
    got_down = lax.ppermute(pay_down, "ctx", [(i + 1, i) for i in range(members - 1)])

    kvg = pl.pallas_call(
        functools.partial(own_kernel, members),
        grid=(tiles,),
        in_specs=[
            smem,
            pl.BlockSpec((3, 2 * STRETCH, TILE), lambda l: (0, 0, l)),
            pl.BlockSpec((2 * STRETCH, TILE), lambda l: (0, l)),
            pl.BlockSpec((3, TAPS, TILE), lambda l: (0, 0, l)),
        ],
        out_specs=pl.BlockSpec((3, 2 * STRETCH, TILE), lambda l: (0, 0, l)),
        out_shape=shape((3, 2 * STRETCH, channels), BF16),
        scratch_shapes=[
            pltpu.VMEM((2, TAPS - 1, STRETCH, TILE), F32),
            pltpu.VMEM((STRETCH + 8, TILE), F32),
        ],
        compiler_params=params,
        cost_estimate=pl.CostEstimate(flops=40_000_000, bytes_accessed=4_500_000, transcendentals=0),
        name="own_rows",
    )(doc_lengths, streams, cotangent, weights)

    groups = channels // GROUP
    medium_filter, doc_lengths, kvg = lax.optimization_barrier((medium_filter, doc_lengths, kvg))
    tables = pl.pallas_call(
        functools.partial(tables_kernel, members),
        grid=(tiles,),
        in_specs=[smem, anywhere],
        out_specs=[
            pl.BlockSpec((PER_TILE, 128, 256), lambda l: (l, 0, 0)),
            pl.BlockSpec((PER_TILE, 128, 256), lambda l: (l, 0, 0)),
            pl.BlockSpec((2, 3, 128, 256), lambda l: (0, 0, 0, 0)),
            pl.BlockSpec((2, 3, 128, 256), lambda l: (0, 0, 0, 0)),
            pl.BlockSpec((2, 2, 128, 128), lambda l: (0, 0, 0, 0)),
            pl.BlockSpec((2, TAPS - 1, STRETCH, TILE), lambda l: (0, 0, 0, 0)),
            pl.BlockSpec((2, 2, TAPS - 1, EDGE, TILE), lambda l: (0, 0, 0, 0, 0)),
        ],
        out_shape=[
            shape((groups, 128, 256), BF16),
            shape((groups, 128, 256), BF16),
            shape((2, 3, 128, 256), BF16),
            shape((2, 3, 128, 256), BF16),
            shape((2, 2, 128, 128), F32),
            shape((2, TAPS - 1, STRETCH, TILE), F32),
            shape((2, 2, TAPS - 1, EDGE, TILE), F32),
        ],
        scratch_shapes=[
            pltpu.VMEM((256, 256), F32),
            pltpu.VMEM((256, 256), F32),
            pltpu.VMEM((384, TILE), F32),
            pltpu.VMEM(medium_filter.shape, F32),
            pltpu.SemaphoreType.DMA,
        ],
        compiler_params=params,
        cost_estimate=pl.CostEstimate(flops=20_000_000, bytes_accessed=7_000_000, transcendentals=0),
        name="tables",
    )(doc_lengths, medium_filter)

    forward, backward, keep_f, keep_b, keep_r, shifted, edge = tables
    mixed, grads, kv, taps = pl.pallas_call(
        functools.partial(pair_kernel, members),
        grid=(tiles, 2),
        in_specs=[whole] * 9,
        out_specs=[whole] * 4,
        out_shape=[
            shape((2, 512, channels), BF16),
            shape((2, 512, channels), BF16),
            shape((2, 2, STRETCH + EDGE, channels), BF16),
            shape((PER_TILE, channels), F32),
        ],
        scratch_shapes=[
            pltpu.VMEM((TAIL, TILE), BF16),
            pltpu.VMEM((HEAD, TILE), BF16),
            pltpu.VMEM((NEAR + EDGE, TILE), F32),
            pltpu.VMEM((144, TILE), F32),
        ],
        compiler_params=params,
        cost_estimate=pl.CostEstimate(flops=500_000_000, bytes_accessed=10_000_000, transcendentals=0),
        name="pair_rows",
    )(streams, kvg, cotangent, pay_up, got_up, got_down, weights, keep_r, edge)

    def convolve(first, count, mixed, grads):
        return pl.pallas_call(
            functools.partial(conv_kernel, members, first),
            grid=(count, 2),
            in_specs=[whole] * 15,
            out_specs=[
                whole,
                pl.BlockSpec((24, TILE), lambda l, m: (0, l)),
            ],
            out_shape=[
                shape((2, 3, STRETCH + EDGE, count * TILE), BF16),
                shape((24, count * TILE), F32),
            ],
            scratch_shapes=[
                pltpu.VMEM((STRETCH + EDGE, TILE), F32),
                pltpu.VMEM((3, STRETCH + EDGE, TILE), F32),
            ],
            compiler_params=params,
            cost_estimate=pl.CostEstimate(flops=count * 100_000_000, bytes_accessed=count * 2_500_000, transcendentals=0),
            name=f"conv_rows_{first}",
        )(
            streams, mixed, grads, kv, cotangent, pay_up, got_up, got_down,
            weights, skip_bias.reshape(1, channels), forward, backward, keep_f, keep_b, shifted,
        )

    parts, stacks = [], []
    for route, (first, count) in zip(routes_x() + routes_z()[1:2], ((0, 1), (1, 1), (2, 2))):
        other = along(taps, "ctx", route)
        stack, part = convolve(first, count, mixed, grads)
        stacks.append(stack)
        taps, mixed, grads, part = lax.optimization_barrier((taps + other, mixed, grads, part))
        parts.append(part)

    def adjoint(first, pieces, previous):
        return pl.pallas_call(
            functools.partial(adjoint_kernel, len(pieces)),
            grid=(2, 2),
            in_specs=[whole] * len(pieces) + [
                pl.BlockSpec((3, TAPS, TILE), lambda l, m: (0, 0, first + l)), whole, anywhere,
            ],
            out_specs=pl.BlockSpec((3, STRETCH, TILE), lambda l, m: (0, m, first + l)),
            out_shape=shape((3, 2 * STRETCH, channels), BF16),
            input_output_aliases={len(pieces) + 2: 0} if first > 0 else {},
            scratch_shapes=[pltpu.VMEM((3, STRETCH + EDGE, TILE), F32)],
            compiler_params=params,
            cost_estimate=pl.CostEstimate(flops=20_000_000, bytes_accessed=4_000_000, transcendentals=0),
            name=f"adjoint_rows_{first}",
        )(*pieces, weights, shifted, previous)

    sums = jnp.concatenate(parts, axis=1)
    grad_streams = kvg
    routes = routes_z()[2:] + routes_z()[:2] + routes_x()
    flip = 1
    for step, route in enumerate(routes):
        if step < 2:
            both = jnp.concatenate([sums, taps], axis=0)
            other = along(both, "ctx", route)
            both = both + other
            sums, taps = both[:24], both[24:]
        else:
            other = along(sums, "ctx", route)
            next_taps = along(taps, "tp", [(i, i ^ flip) for i in range(lax.axis_size("tp"))])
            if step < len(routes) - 1:
                upper = (tp // flip) % 2 == 1
                taps = jnp.concatenate(
                    [jnp.where(upper, next_taps, taps), jnp.where(upper, taps, next_taps)], axis=0
                )
                sums = sums + other
                flip *= 2
        if step < 2:
            grad_streams = adjoint(2 * step, stacks[2 * step : 2 * step + 2], grad_streams)
        sums, taps, grad_streams = lax.optimization_barrier((sums, taps, grad_streams))
    grad_medium, short, bias = pl.pallas_call(
        functools.partial(final_kernel, scale, flip),
        in_specs=[whole] * 4,
        out_shape=[
            shape(medium_filter.shape, F32), shape((3, TAPS, channels), F32), shape((1, channels), F32),
        ],
        compiler_params=params,
        name="final",
    )(taps, next_taps, sums, other)
    return (
        jnp.transpose(grad_streams, (1, 0, 2)), jnp.transpose(short, (1, 0, 2)), grad_medium,
        bias.reshape(channels),
    )


def solution(mesh):
    in_specs = (P("ctx", None, "tp"), P(None, None, "tp"), P(), P("tp"), P("ctx", "tp"), P())
    out_specs = (P("ctx", None, "tp"), P(None, None, "tp"), P(), P("tp"))
    return jax.shard_map(shards, mesh=mesh, in_specs=in_specs, out_specs=out_specs, check_vma=False)
```

```python
import functools
import math

import jax
import jax.numpy as jnp
from jax import lax
from jax.experimental import pallas as pl
from jax.experimental.pallas import tpu as pltpu
from jax.sharding import PartitionSpec as P

STRETCH = 256
TILE = 128
GROUP = 16
PER_TILE = TILE // GROUP
LAGS = 128
TAPS = 7
EDGE = 16
TAIL = 128 + 2 * EDGE
HEAD = 128 + 2 * EDGE
REACH = TAPS - 1
NEAR = 8
DOCS = 64
F32 = jnp.float32
BF16 = jnp.bfloat16


def base_of(device, members, member):
    first = device * STRETCH
    second = (2 * members - 1 - device) * STRETCH
    if isinstance(member, int):
        return first if member == 0 else second
    return jnp.where(member == 0, first, second)


def lane_starts(lengths_ref, base, count):
    position = base + lax.broadcasted_iota(jnp.int32, (8, count), 1)
    found = jnp.zeros((8, count), jnp.int32)
    running = jnp.int32(0)
    for doc in range(DOCS):
        found = jnp.where(position >= running, running, found)
        running = running + lengths_ref[doc]
    return found.astype(F32)


def row_starts(starts, block):
    row = starts[0:1, block * 128 : (block + 1) * 128]
    return jnp.broadcast_to(row, (128, 128)).T


def row_positions(base, block):
    return (base + block * 128 + lax.broadcasted_iota(jnp.int32, (128, 128), 0)).astype(F32)


def conv_rows(rows, weights, masks, member, first, count):
    total = rows[pl.ds(8 + first, count), :] * weights[0:1, :]
    for lag in range(1, TAPS):
        moved = rows[pl.ds(8 + first - lag, count), :] * weights[lag : lag + 1, :]
        total = total + moved * masks[member, lag - 1, pl.ds(first, count), :]
    return total.astype(BF16)


def own_masks(members, lengths_ref, masks):
    for member in range(2):
        base = base_of(lax.axis_index("ctx"), members, member)
        starts = lane_starts(lengths_ref, base, STRETCH)
        for block in range(2):
            offset = row_positions(base, block) - row_starts(starts, block)
            for lag in range(1, TAPS):
                masks[member, lag - 1, pl.ds(block * 128, 128), :] = jnp.where(offset >= lag, 1.0, 0.0)


def payload_kernel(
    members, lengths_hbm, feat_hbm, cot_hbm, taps_hbm, up_hbm, down_hbm,
    lengths_ref, taps_ref, up_ref, down_ref, feat, cots, masks, rows, grads, sems,
):
    copies = []

    def fetch(source, target):
        copies.append(pltpu.make_async_copy(source, target, sems.at[len(copies)]))
        copies[-1].start()
        return copies[-1]

    def fetch_rows(stream, first, count):
        place = pl.ds(first, count)
        return fetch(feat_hbm.at[stream, place, :], feat.at[stream, place, :])

    fetch(lengths_hbm, lengths_ref)
    fetch(taps_hbm, taps_ref)
    needed = {}
    for member in range(2):
        first = member * STRETCH
        head = pl.ds(first, 144)
        needed[member, "head"] = [fetch_rows(0, first, 144), fetch(cot_hbm.at[head, :], cots.at[head, :])]
    for member in range(2):
        first = member * STRETCH
        needed[member, "tail"] = [fetch_rows(stream, first + 112, 144) for stream in (1, 2)]
    edges = []
    for member in range(2):
        first = member * STRETCH
        edges.append(fetch_rows(0, first + STRETCH - EDGE, EDGE))
        edges += [fetch_rows(stream, first, EDGE) for stream in (1, 2)]

    copies[0].wait()
    own_masks(members, lengths_ref, masks)
    copies[1].wait()
    rows[pl.ds(0, 8), :] = jnp.zeros((8, TILE), F32)
    tiles = [pl.ds(tile * TILE, TILE) for tile in range(up_ref.shape[1] // TILE)]
    for member in range(2):
        head_ref = down_ref if member == 0 else up_ref
        first = member * STRETCH
        for copy in needed[member, "head"]:
            copy.wait()
        for lanes in tiles:
            rows[pl.ds(8, 144), :] = feat[0, pl.ds(first, 144), lanes].astype(F32)
            weights = taps_ref[0, :, lanes]
            for chunk in range(0, 144, 48):
                query = conv_rows(rows, weights, masks, member, chunk, 48).astype(F32)
                cot = cots[pl.ds(first + chunk, 48), lanes].astype(F32)
                grads[pl.ds(chunk, 48), :] = cot * query
            head_ref[pl.ds(TAIL, 128), lanes] = grads[pl.ds(REACH, 128), :].astype(BF16)
    sent = []
    big = pl.ds(TAIL, 128)
    for source, target in ((up_ref, up_hbm), (down_ref, down_hbm)):
        sent.append(fetch(source.at[big, :], target.at[big, :]))
    for member in range(2):
        tail_ref = up_ref if member == 0 else down_ref
        first = member * STRETCH
        for copy in needed[member, "tail"]:
            copy.wait()
        for lanes in tiles:
            for stream in (1, 2):
                rows[pl.ds(8 + 112, 144), :] = feat[stream, pl.ds(first + 112, 144), lanes].astype(F32)
                weights = taps_ref[stream, :, lanes]
                for chunk in range(0, 128, 64):
                    part = conv_rows(rows, weights, masks, member, 128 + chunk, 64)
                    place = pl.ds(chunk, 64)
                    if stream == 2:
                        part = (tail_ref[place, lanes].astype(F32) * part.astype(F32)).astype(BF16)
                    tail_ref[place, lanes] = part
    for copy in edges:
        copy.wait()
    for member in range(2):
        tail_ref = up_ref if member == 0 else down_ref
        head_ref = down_ref if member == 0 else up_ref
        first = member * STRETCH
        last = [feat[stream, pl.ds(first + STRETCH - EDGE, EDGE), :].astype(F32)[NEAR:] for stream in range(3)]
        ahead = [feat[stream, pl.ds(first, EDGE), :].astype(F32)[:NEAR] for stream in range(3)]
        ahead.append(cots[pl.ds(first, EDGE), :].astype(F32)[:NEAR])
        for pair in range(2):
            place = 128 + pair * EDGE
            two = jnp.concatenate([last[2 * pair], last[min(2 * pair + 1, 2)]], axis=0)
            tail_ref[pl.ds(place, EDGE), :] = two.astype(BF16)
            two = jnp.concatenate([ahead[2 * pair], ahead[2 * pair + 1]], axis=0)
            head_ref[pl.ds(TAIL + place, EDGE), :] = two.astype(BF16)
    for source, target in ((up_ref, up_hbm), (down_ref, down_hbm)):
        for part in (pl.ds(0, TAIL), pl.ds(TAIL + 128, 2 * EDGE)):
            sent.append(fetch(source.at[part, :], target.at[part, :]))
    for copy in sent:
        copy.wait()


def own_kernel(members, lengths_ref, feat_ref, cot_ref, taps_ref, kvg_ref, masks, rows):
    @pl.when(pl.program_id(0) == 0)
    def _():
        own_masks(members, lengths_ref, masks)

    rows[pl.ds(0, 8), :] = jnp.zeros((8, TILE), F32)
    for member in range(2):
        first = member * STRETCH
        for stream in range(3):
            rows[pl.ds(8, STRETCH), :] = feat_ref[stream, pl.ds(first, STRETCH), :].astype(F32)
            weights = taps_ref[stream]
            for chunk in range(0, STRETCH, 64):
                rounded = conv_rows(rows, weights, masks, member, chunk, 64)
                if stream == 0:
                    cot = cot_ref[pl.ds(first + chunk, 64), :].astype(F32)
                    rounded = (cot * rounded.astype(F32)).astype(BF16)
                    kvg_ref[2, pl.ds(first + chunk, 64), :] = rounded
                else:
                    kvg_ref[stream - 1, pl.ds(first + chunk, 64), :] = rounded


def tables_kernel(
    members, lengths_ref, medium_ref,
    forward_ref, backward_ref, keep_f_ref, keep_b_ref, keep_r_ref, shifted_ref, edge_ref,
    forward_rows, backward_rows, offsets, medium, medium_sem,
):
    device = lax.axis_index("ctx")

    @pl.when(pl.program_id(0) == 0)
    def _():
        copy = pltpu.make_async_copy(medium_ref, medium, medium_sem)
        copy.start()
        lag = lax.broadcasted_iota(jnp.int32, (LAGS, 256), 0)
        lane = lax.broadcasted_iota(jnp.int32, (LAGS, 256), 1)
        copy.wait()
        taps = medium[...].astype(BF16)
        dims = (((0,), (0,)), ((), ()))
        place_f = jnp.where(lane == LAGS - lag, 1.0, 0.0).astype(BF16)
        place_b = jnp.where(lane == lag, 1.0, 0.0).astype(BF16)
        forward_rows[...] = lax.dot_general(taps, place_f, dims, preferred_element_type=F32)
        backward_rows[...] = lax.dot_general(taps, place_b, dims, preferred_element_type=F32)
        wide = lax.broadcasted_iota(jnp.int32, (128, 256), 1)
        tall = lax.broadcasted_iota(jnp.int32, (128, 256), 0)
        narrow = lax.broadcasted_iota(jnp.int32, (128, 128), 1)
        for member in range(2):
            base = base_of(device, members, member)
            starts = lane_starts(lengths_ref, base, 512)
            for block in range(3):
                begin = row_starts(starts, block)
                begin = jnp.concatenate([begin, begin], axis=1)
                source = (base + (block - 1) * 128 + wide).astype(F32)
                keep_f_ref[member, block] = jnp.where(source >= begin, 1.0, 0.0).astype(BF16)
                if block < 2:
                    turned = jnp.where(
                        narrow + tall[:, :128] >= 127,
                        base + block * 128 + 127 - narrow, base + (block - 1) * 128 + 127 - narrow,
                    ).astype(F32)
                    keep_r_ref[member, block] = jnp.where(turned >= begin[:, :128], 1.0, 0.0)
                own = (base + block * 128 + tall).astype(F32)
                target = jnp.broadcast_to(starts[0:1, block * 128 : block * 128 + 256], (128, 256))
                keep_b_ref[member, block] = jnp.where(own >= target, 1.0, 0.0).astype(BF16)
                offsets[pl.ds(block * 128, 128), :] = row_positions(base, block) - begin[:, :128]
            for lag in range(1, TAPS):
                shifted_ref[member, lag - 1] = jnp.where(
                    offsets[pl.ds(lag, STRETCH), :] >= lag, 1.0, 0.0
                )
                for side in range(2):
                    edge_ref[member, side, lag - 1] = jnp.where(
                        offsets[pl.ds(side * STRETCH, EDGE), :] >= lag, 1.0, 0.0
                    )

    first = pl.multiple_of(lax.axis_index("tp") * 32 + pl.program_id(0) * PER_TILE, PER_TILE)
    rows_f = forward_rows[pl.ds(first, PER_TILE), :]
    rows_b = backward_rows[pl.ds(first, PER_TILE), :]
    for group in range(PER_TILE):
        for rows, out_ref in ((rows_f, forward_ref), (rows_b, backward_ref)):
            spread = jnp.broadcast_to(rows[group : group + 1, :], (128, 256))
            out_ref[group] = pltpu.roll(spread, 0, 1, stride=1, stride_axis=0).astype(BF16)


def edge_conv(rows, weights, edge_ref, side):
    total = rows[pl.ds(NEAR, EDGE), :] * weights[0:1, :]
    for lag in range(1, TAPS):
        moved = rows[pl.ds(NEAR - lag, EDGE), :] * weights[lag : lag + 1, :]
        total = total + moved * edge_ref[side, lag - 1]
    return total.astype(BF16).astype(F32)


def pair_kernel(
    members, feat_ref, kvg_ref, cot_ref, own_up_ref, up_ref, down_ref, taps_ref, keep_r_ref, edge_ref,
    mixed_ref, grads_ref, kv_ref, sums_ref,
    left, right, rows, beyond,
):
    member = pl.program_id(1)
    tile = pl.program_id(0)
    lanes = pl.ds(pl.multiple_of(tile * TILE, TILE), TILE)
    base = member * STRETCH

    def own(first, count):
        return pl.ds(pl.multiple_of(base + first, EDGE), count)

    is_last = lax.axis_index("ctx") == members - 1

    @pl.when(member == 0)
    def _():
        left[...] = up_ref[pl.ds(0, TAIL), lanes]

    @pl.when((member == 1) & is_last)
    def _():
        left[...] = own_up_ref[pl.ds(0, TAIL), lanes]

    @pl.when((member == 1) & jnp.logical_not(is_last))
    def _():
        left[...] = down_ref[pl.ds(0, TAIL), lanes]

    @pl.when(member == 1)
    def _():
        right[...] = up_ref[pl.ds(TAIL, HEAD), lanes]

    @pl.when((member == 0) & is_last)
    def _():
        right[...] = own_up_ref[pl.ds(TAIL, HEAD), lanes]

    @pl.when((member == 0) & jnp.logical_not(is_last))
    def _():
        right[...] = down_ref[pl.ds(TAIL, HEAD), lanes]

    inner = pl.ds(EDGE, STRETCH - EDGE)
    for side in range(2):
        place = pl.ds(side * STRETCH, EDGE)
        if side == 0:
            cot = cot_ref[own(0, EDGE), lanes].astype(F32)
        else:
            cot = right[pl.ds(144, EDGE), :].astype(F32)[NEAR:]
        fixed = []
        for stream in range(3):
            place_two, half = pl.ds(128 + stream // 2 * EDGE, EDGE), stream % 2 * NEAR
            if side == 0:
                rows[pl.ds(0, NEAR), :] = left[place_two, :].astype(F32)[half : half + NEAR]
                rows[pl.ds(NEAR, EDGE), :] = feat_ref[stream, own(0, EDGE), lanes].astype(F32)
            else:
                rows[pl.ds(0, NEAR), :] = feat_ref[stream, own(STRETCH - EDGE, EDGE), lanes].astype(F32)[NEAR:]
                rows[pl.ds(NEAR, NEAR), :] = right[place_two, :].astype(F32)[half : half + NEAR]
                rows[pl.ds(EDGE, NEAR), :] = jnp.zeros((NEAR, TILE), F32)
            fixed.append(edge_conv(rows, taps_ref[stream, :, lanes], edge_ref.at[member], side))
        if side == 0:
            grads_ref[member, place, lanes] = (cot * fixed[0]).astype(BF16)
        else:
            beyond[pl.ds(0, NEAR), :] = cot * fixed[0][:NEAR]
            beyond[pl.ds(REACH, 128), :] = right[pl.ds(0, 128), :].astype(F32)
            beyond[pl.ds(REACH + 128, 144 - REACH - 128), :] = jnp.zeros((144 - REACH - 128, TILE), F32)
            grads_ref[member, pl.ds(STRETCH, 144), lanes] = beyond[...].astype(BF16)
        kv_ref[member, 0, place, lanes] = fixed[1].astype(BF16)
        kv_ref[member, 1, place, lanes] = fixed[2].astype(BF16)
        mixed_ref[member, pl.ds(128 + side * STRETCH, EDGE), lanes] = (fixed[1] * fixed[2]).astype(BF16)
    keys = kvg_ref[0, own(EDGE, STRETCH - EDGE), lanes]
    values = kvg_ref[1, own(EDGE, STRETCH - EDGE), lanes]
    kv_ref[member, 0, inner, lanes] = keys
    kv_ref[member, 1, inner, lanes] = values
    mixed_ref[member, pl.ds(0, 128), lanes] = left[pl.ds(0, 128), :]
    mixed_ref[member, pl.ds(128 + EDGE, STRETCH - EDGE), lanes] = (keys.astype(F32) * values.astype(F32)).astype(BF16)
    mixed_ref[member, pl.ds(400, 112), lanes] = jnp.zeros((112, TILE), BF16)
    grads_ref[member, inner, lanes] = kvg_ref[2, own(EDGE, STRETCH - EDGE), lanes]
    grads_ref[member, pl.ds(400, 112), lanes] = jnp.zeros((112, TILE), BF16)

    @pl.when(member == 1)
    def _():
        pair_sums(mixed_ref, grads_ref, keep_r_ref, sums_ref, tile, lanes)


def pair_sums(mixed_ref, grads_ref, keep_r_ref, sums_ref, tile, lanes):
    lane = lax.broadcasted_iota(jnp.int32, (128, TILE), 1)
    row = lax.broadcasted_iota(jnp.int32, (128, TILE), 0)
    lane_group = lane // GROUP
    near = lane + row >= 127
    turn = jnp.where(lane + row == 127, 1.0, 0.0).astype(BF16)
    sources = []
    for member in range(2):
        turned = [
            lax.dot_general(
                mixed_ref[member, pl.ds(piece * 128, 128), lanes], turn, (((0,), (0,)), ((), ())),
                preferred_element_type=F32,
            ).astype(BF16)
            for piece in range(3)
        ]
        for block in range(2):
            sources.append(jnp.concatenate([turned[block + 1], turned[block]], axis=1))
    for group in range(PER_TILE):
        choose = jnp.where(lane_group == group, 1.0, 0.0).astype(BF16)
        total = jnp.zeros((128, TILE), F32)
        for member in range(2):
            for block in range(2):
                chosen = grads_ref[member, pl.ds(block * 128, 128), lanes] * choose
                pair = jnp.dot(chosen, sources[member * 2 + block], preferred_element_type=F32)
                pair = jnp.where(near, pair[:, :128], pair[:, 128:])
                total = total + pair * keep_r_ref[member, block]
        lined_up = pltpu.roll(total, 1, 1, stride=1, stride_axis=0)
        sums_ref[pl.ds(group, 1), lanes] = jnp.sum(lined_up, axis=0, keepdims=True)


def conv_kernel(
    members, first_tile, feat_ref, mixed_ref, grads_ref, kv_ref, cot_ref, own_up_ref, up_ref, down_ref,
    taps_ref, skip_ref, forward_ref, backward_ref, keep_f_ref, keep_b_ref, shifted_ref,
    stack_ref, sums_ref,
    cots, stack,
):
    member = pl.program_id(1)
    tile = first_tile + pl.program_id(0)
    lanes = pl.ds(pl.multiple_of(tile * TILE, TILE), TILE)
    base = member * STRETCH

    def own(first, count):
        return pl.ds(pl.multiple_of(base + first, EDGE), count)

    is_last = lax.axis_index("ctx") == members - 1
    first_group = tile * PER_TILE
    lane_group = lax.broadcasted_iota(jnp.int32, (128, TILE), 1) // GROUP
    skip = skip_ref[:, lanes]
    after = pl.ds(TAIL + 144, EDGE)
    beyond = pl.ds(STRETCH, NEAR)
    cots[pl.ds(STRETCH + NEAR, NEAR), :] = jnp.zeros((NEAR, TILE), F32)
    cots[pl.ds(0, STRETCH), :] = cot_ref[own(0, STRETCH), lanes].astype(F32)

    @pl.when(member == 1)
    def _():
        cots[beyond, :] = up_ref[after, lanes].astype(F32)[NEAR:]

    @pl.when((member == 0) & is_last)
    def _():
        cots[beyond, :] = own_up_ref[after, lanes].astype(F32)[NEAR:]

    @pl.when((member == 0) & jnp.logical_not(is_last))
    def _():
        cots[beyond, :] = down_ref[after, lanes].astype(F32)[NEAR:]

    def convolved(table_ref, keep_ref, window, block):
        height = 128 if block < 2 else EDGE
        keep = keep_ref[member, block, pl.ds(0, height), :]
        matrix = table_ref[pl.ds(first_group, PER_TILE), pl.ds(0, height), :] * keep[None]
        product = jnp.dot(matrix.reshape(PER_TILE * height, 256), window, preferred_element_type=F32)
        result = product[:height]
        for group in range(1, PER_TILE):
            result = jnp.where(lane_group[:height] == group, product[group * height : (group + 1) * height], result)
        return result

    for block in range(3):
        height = 128 if block < 2 else EDGE
        place = pl.ds(block * 128, height)
        medium = convolved(forward_ref, keep_f_ref, mixed_ref[member, pl.ds(block * 128, 256), lanes], block)
        medium = medium + skip * mixed_ref[member, pl.ds(block * 128 + 128, height), lanes].astype(F32)
        grad_conv = convolved(backward_ref, keep_b_ref, grads_ref[member, pl.ds(block * 128, 256), lanes], block)
        grad_conv = grad_conv + skip * grads_ref[member, place, lanes].astype(F32)
        for stream in range(3):
            if stream == 0:
                product = cots[place, :] * medium
            else:
                product = grad_conv * kv_ref[member, 2 - stream, place, lanes].astype(F32)
            product = product.astype(BF16)
            stack[stream, place, :] = product.astype(F32)
            stack_ref[member, stream, place, pl.ds(pl.multiple_of(pl.program_id(0) * TILE, TILE), TILE)] = product

    @pl.when(member == 0)
    def _():
        sums_ref[...] = jnp.zeros(sums_ref.shape, F32)

    for stream in range(3):
        partial = [jnp.zeros((8, TILE), F32) for _ in range(TAPS)]
        for chunk in range(0, STRETCH, 64):
            source = feat_ref[stream, own(chunk, 64), lanes].astype(F32)
            for lag in range(TAPS):
                later = stack[stream, pl.ds(chunk + lag, 64), :] * source
                if lag > 0:
                    later = later * shifted_ref[member, lag - 1, pl.ds(chunk, 64), :]
                partial[lag] = partial[lag] + jnp.sum(later.reshape(8, 8, TILE), axis=0)
        for lag in range(TAPS):
            row = pl.ds(stream * 8 + lag, 1)
            sums_ref[row, :] += jnp.sum(partial[lag], axis=0, keepdims=True)
    bias = jnp.sum(
        grads_ref[member, pl.ds(0, STRETCH), lanes].astype(F32) * mixed_ref[member, pl.ds(128, STRETCH), lanes].astype(F32),
        axis=0, keepdims=True,
    )
    sums_ref[pl.ds(7, 1), :] += bias


def adjoint_kernel(pieces, *refs):
    stack_refs, (taps_ref, shifted_ref, previous_ref, out_ref, stack) = refs[:pieces], refs[pieces:]
    del previous_ref
    tile, member = pl.program_id(0), pl.program_id(1)
    if pieces == 1:
        stack[...] = stack_refs[0][member, :, :, pl.ds(pl.multiple_of(tile * TILE, TILE), TILE)].astype(F32)
    for piece in range(pieces if pieces > 1 else 0):
        @pl.when(tile == piece)
        def _():
            stack[...] = stack_refs[piece][member].astype(F32)
    for stream in range(3):
        weights = taps_ref[stream]
        for chunk in range(0, STRETCH, 64):
            total = stack[stream, pl.ds(chunk, 64), :] * weights[0:1, :]
            for lag in range(1, TAPS):
                later = stack[stream, pl.ds(chunk + lag, 64), :] * shifted_ref[member, lag - 1, pl.ds(chunk, 64), :]
                total = total + later * weights[lag : lag + 1, :]
            out_ref[stream, pl.ds(chunk, 64), :] = total.astype(BF16)


def final_kernel(scale, flip, taps_ref, next_taps_ref, sums_ref, other_ref, medium_ref, short_ref, bias_ref):
    half = medium_ref.shape[1] // 2

    def by_group(ref):
        pieces = [
            ref[first : first + PER_TILE, tile * TILE : (tile + 1) * TILE]
            for first in range(0, ref.shape[0], PER_TILE)
            for tile in range(ref.shape[1] // TILE)
        ]
        return jnp.concatenate(pieces, axis=0).T * scale

    upper = (lax.axis_index("tp") // flip) % 2 == 1

    @pl.when(upper)
    def _():
        medium_ref[:, pl.ds(half, half)] = by_group(taps_ref)
        medium_ref[:, pl.ds(0, half)] = by_group(next_taps_ref)

    @pl.when(jnp.logical_not(upper))
    def _():
        medium_ref[:, pl.ds(0, half)] = by_group(taps_ref)
        medium_ref[:, pl.ds(half, half)] = by_group(next_taps_ref)

    total = (sums_ref[...] + other_ref[...]) * scale
    for stream in range(3):
        short_ref[stream] = total[stream * 8 : stream * 8 + TAPS]
    bias_ref[...] = total[TAPS : TAPS + 1]


def along(block, axis, route):
    return lax.ppermute(block, axis, route)


def routes_z():
    return [
        [(i, i // 8 * 8 + 7 - i % 8) for i in range(32)],
        [(i, i ^ 1) for i in range(32)],
        [(i, i ^ 2) for i in range(32)],
    ]


def routes_x():
    return [[(i, (3 - i // 8) * 8 + i % 8) for i in range(32)], [(i, i ^ 8) for i in range(32)]]


def shards(features, short_filter, medium_filter, skip_bias, cotangent, doc_lengths):
    members = lax.axis_size("ctx")
    tp = lax.axis_index("tp")
    channels = features.shape[2]
    tiles = channels // TILE
    scale = 1.0 / math.sqrt(2 * STRETCH * members)
    streams = jnp.transpose(features, (1, 0, 2))
    weights = jnp.transpose(short_filter, (1, 0, 2))
    smem = pl.BlockSpec(memory_space=pltpu.SMEM)
    shape = jax.ShapeDtypeStruct
    params = pltpu.CompilerParams(vmem_limit_bytes=16 * 1024 * 1024)

    whole = pl.BlockSpec(memory_space=pltpu.VMEM)
    anywhere = pl.BlockSpec(memory_space=pl.ANY)
    pay_up, pay_down = pl.pallas_call(
        functools.partial(payload_kernel, members),
        in_specs=[anywhere] * 4,
        out_specs=[anywhere] * 2,
        out_shape=[shape((TAIL + HEAD, channels), BF16), shape((TAIL + HEAD, channels), BF16)],
        scratch_shapes=[
            pltpu.SMEM((DOCS,), jnp.int32),
            pltpu.VMEM((3, TAPS, channels), F32),
            pltpu.VMEM((TAIL + HEAD, channels), BF16),
            pltpu.VMEM((TAIL + HEAD, channels), BF16),
            pltpu.VMEM((3, 2 * STRETCH, channels), BF16),
            pltpu.VMEM((2 * STRETCH, channels), BF16),
            pltpu.VMEM((2, TAPS - 1, STRETCH, TILE), F32),
            pltpu.VMEM((STRETCH + 8, TILE), F32),
            pltpu.VMEM((144, TILE), F32),
            pltpu.SemaphoreType.DMA((22,)),
        ],
        compiler_params=pltpu.CompilerParams(vmem_limit_bytes=56 * 1024 * 1024),
        cost_estimate=pl.CostEstimate(flops=20_000_000, bytes_accessed=2_800_000, transcendentals=0),
        name="payload_rows",
    )(doc_lengths, streams, cotangent, weights)

    got_up = lax.ppermute(pay_up, "ctx", [(i, i + 1) for i in range(members - 1)])
    got_down = lax.ppermute(pay_down, "ctx", [(i + 1, i) for i in range(members - 1)])

    kvg = pl.pallas_call(
        functools.partial(own_kernel, members),
        grid=(tiles,),
        in_specs=[
            smem,
            pl.BlockSpec((3, 2 * STRETCH, TILE), lambda l: (0, 0, l)),
            pl.BlockSpec((2 * STRETCH, TILE), lambda l: (0, l)),
            pl.BlockSpec((3, TAPS, TILE), lambda l: (0, 0, l)),
        ],
        out_specs=pl.BlockSpec((3, 2 * STRETCH, TILE), lambda l: (0, 0, l)),
        out_shape=shape((3, 2 * STRETCH, channels), BF16),
        scratch_shapes=[
            pltpu.VMEM((2, TAPS - 1, STRETCH, TILE), F32),
            pltpu.VMEM((STRETCH + 8, TILE), F32),
        ],
        compiler_params=params,
        cost_estimate=pl.CostEstimate(flops=40_000_000, bytes_accessed=4_500_000, transcendentals=0),
        name="own_rows",
    )(doc_lengths, streams, cotangent, weights)

    groups = channels // GROUP
    medium_filter, doc_lengths, kvg = lax.optimization_barrier((medium_filter, doc_lengths, kvg))
    tables = pl.pallas_call(
        functools.partial(tables_kernel, members),
        grid=(tiles,),
        in_specs=[smem, anywhere],
        out_specs=[
            pl.BlockSpec((PER_TILE, 128, 256), lambda l: (l, 0, 0)),
            pl.BlockSpec((PER_TILE, 128, 256), lambda l: (l, 0, 0)),
            pl.BlockSpec((2, 3, 128, 256), lambda l: (0, 0, 0, 0)),
            pl.BlockSpec((2, 3, 128, 256), lambda l: (0, 0, 0, 0)),
            pl.BlockSpec((2, 2, 128, 128), lambda l: (0, 0, 0, 0)),
            pl.BlockSpec((2, TAPS - 1, STRETCH, TILE), lambda l: (0, 0, 0, 0)),
            pl.BlockSpec((2, 2, TAPS - 1, EDGE, TILE), lambda l: (0, 0, 0, 0, 0)),
        ],
        out_shape=[
            shape((groups, 128, 256), BF16),
            shape((groups, 128, 256), BF16),
            shape((2, 3, 128, 256), BF16),
            shape((2, 3, 128, 256), BF16),
            shape((2, 2, 128, 128), F32),
            shape((2, TAPS - 1, STRETCH, TILE), F32),
            shape((2, 2, TAPS - 1, EDGE, TILE), F32),
        ],
        scratch_shapes=[
            pltpu.VMEM((256, 256), F32),
            pltpu.VMEM((256, 256), F32),
            pltpu.VMEM((384, TILE), F32),
            pltpu.VMEM(medium_filter.shape, F32),
            pltpu.SemaphoreType.DMA,
        ],
        compiler_params=params,
        cost_estimate=pl.CostEstimate(flops=20_000_000, bytes_accessed=7_000_000, transcendentals=0),
        name="tables",
    )(doc_lengths, medium_filter)

    forward, backward, keep_f, keep_b, keep_r, shifted, edge = tables
    mixed, grads, kv, taps = pl.pallas_call(
        functools.partial(pair_kernel, members),
        grid=(tiles, 2),
        in_specs=[whole] * 9,
        out_specs=[whole] * 4,
        out_shape=[
            shape((2, 512, channels), BF16),
            shape((2, 512, channels), BF16),
            shape((2, 2, STRETCH + EDGE, channels), BF16),
            shape((PER_TILE, channels), F32),
        ],
        scratch_shapes=[
            pltpu.VMEM((TAIL, TILE), BF16),
            pltpu.VMEM((HEAD, TILE), BF16),
            pltpu.VMEM((NEAR + EDGE, TILE), F32),
            pltpu.VMEM((144, TILE), F32),
        ],
        compiler_params=params,
        cost_estimate=pl.CostEstimate(flops=500_000_000, bytes_accessed=10_000_000, transcendentals=0),
        name="pair_rows",
    )(streams, kvg, cotangent, pay_up, got_up, got_down, weights, keep_r, edge)

    def convolve(first, count, mixed, grads):
        return pl.pallas_call(
            functools.partial(conv_kernel, members, first),
            grid=(count, 2),
            in_specs=[whole] * 15,
            out_specs=[
                whole,
                pl.BlockSpec((24, TILE), lambda l, m: (0, l)),
            ],
            out_shape=[
                shape((2, 3, STRETCH + EDGE, count * TILE), BF16),
                shape((24, count * TILE), F32),
            ],
            scratch_shapes=[
                pltpu.VMEM((STRETCH + EDGE, TILE), F32),
                pltpu.VMEM((3, STRETCH + EDGE, TILE), F32),
            ],
            compiler_params=params,
            cost_estimate=pl.CostEstimate(flops=count * 100_000_000, bytes_accessed=count * 2_500_000, transcendentals=0),
            name=f"conv_rows_{first}",
        )(
            streams, mixed, grads, kv, cotangent, pay_up, got_up, got_down,
            weights, skip_bias.reshape(1, channels), forward, backward, keep_f, keep_b, shifted,
        )

    parts, stacks = [], []
    for route, (first, count) in zip(routes_x() + routes_z()[1:2], ((0, 1), (1, 1), (2, 2))):
        other = along(taps, "ctx", route)
        stack, part = convolve(first, count, mixed, grads)
        stacks.append(stack)
        taps, mixed, grads, part = lax.optimization_barrier((taps + other, mixed, grads, part))
        parts.append(part)

    def adjoint(first, pieces, previous):
        return pl.pallas_call(
            functools.partial(adjoint_kernel, len(pieces)),
            grid=(2, 2),
            in_specs=[whole] * len(pieces) + [
                pl.BlockSpec((3, TAPS, TILE), lambda l, m: (0, 0, first + l)), whole, anywhere,
            ],
            out_specs=pl.BlockSpec((3, STRETCH, TILE), lambda l, m: (0, m, first + l)),
            out_shape=shape((3, 2 * STRETCH, channels), BF16),
            input_output_aliases={len(pieces) + 2: 0} if first > 0 else {},
            scratch_shapes=[pltpu.VMEM((3, STRETCH + EDGE, TILE), F32)],
            compiler_params=params,
            cost_estimate=pl.CostEstimate(flops=20_000_000, bytes_accessed=4_000_000, transcendentals=0),
            name=f"adjoint_rows_{first}",
        )(*pieces, weights, shifted, previous)

    sums = jnp.concatenate(parts, axis=1)
    grad_streams = kvg
    routes = routes_z()[:1] + routes_z()[2:] + routes_z()[1:2] + routes_x()
    flip = 1
    for step, route in enumerate(routes):
        if step < 2:
            both = jnp.concatenate([sums, taps], axis=0)
            other = along(both, "ctx", route)
            both = both + other
            sums, taps = both[:24], both[24:]
        else:
            other = along(sums, "ctx", route)
            next_taps = along(taps, "tp", [(i, i ^ flip) for i in range(lax.axis_size("tp"))])
            if step < len(routes) - 1:
                upper = (tp // flip) % 2 == 1
                taps = jnp.concatenate(
                    [jnp.where(upper, next_taps, taps), jnp.where(upper, taps, next_taps)], axis=0
                )
                sums = sums + other
                flip *= 2
        if step < 2:
            grad_streams = adjoint(2 * step, stacks[2 * step : 2 * step + 2], grad_streams)
        sums, taps, grad_streams = lax.optimization_barrier((sums, taps, grad_streams))
    grad_medium, short, bias = pl.pallas_call(
        functools.partial(final_kernel, scale, flip),
        in_specs=[whole] * 4,
        out_shape=[
            shape(medium_filter.shape, F32), shape((3, TAPS, channels), F32), shape((1, channels), F32),
        ],
        compiler_params=params,
        name="final",
    )(taps, next_taps, sums, other)
    return (
        jnp.transpose(grad_streams, (1, 0, 2)), jnp.transpose(short, (1, 0, 2)), grad_medium,
        bias.reshape(channels),
    )


def solution(mesh):
    in_specs = (P("ctx", None, "tp"), P(None, None, "tp"), P(), P("tp"), P("ctx", "tp"), P())
    out_specs = (P("ctx", None, "tp"), P(None, None, "tp"), P(), P("tp"))
    return jax.shard_map(shards, mesh=mesh, in_specs=in_specs, out_specs=out_specs, check_vma=False)
```
